32 devices in a mesh: prow: 4 (over x, core), pcol: 8 (over z, y).
Axes of the slice: x: 2, y: 2, z: 4, core: 2. Of those that a mesh axis runs over, the one named last changes fastest.
Arguments:
- matrix: bfloat16 [8, 4, 512, 4, 8, 512], P(None, 'prow', None, None, 'pcol'), may hold values from -6 to 6
- upper_inv: bfloat16 [2, 512, 512], replicated, may hold values from -4 to 4
- lower_inv: bfloat16 [2, 512, 512], replicated, may hold values from -4 to 4
- solution: bfloat16 [4, 8, 512], P(None, 'pcol'), may hold values from -0.046875 to 0.046875
- right_side: float32 [8, 4, 512], P(None, 'prow'), may hold values from -6 to 6
- diagonal_block_inverses: bfloat16 [1, 4, 512, 512], P(None, 'prow'), may hold values from -0.013671875 to 0.013671875
Outputs:
- updated: bfloat16 [8, 4, 512, 4, 8, 512], P(None, 'prow', None, None, 'pcol')
- residual: float32 [8, 4, 512], P(None, 'prow')
- precond: float32 [4, 512], replicated
The draws below stay inside these ranges and needn't reach their ends.
All inputs are finite; a program needn't handle non-finite values.
Results may differ from the reference program's by a relative error of at most 0.0085.
Values may be sent and summed in bfloat16 or wider, within the bound.
No kernel may reach another device: no remote copies, remote signals or barrier semaphores. Data moves between devices by JAX's collectives and lax.ppermute only.
A program may use at most 128 MiB of HBM per device.

```python
import jax
import jax.numpy as jnp
from jax import lax

N = 16384
PANEL_WIDTH = 512
PANELS = 2
PROW_BLOCK_ROWS = 1
RB = 8
CB = 4
SOLVE_BLOCK_ROWS = 4
N_PROW = 4
N_PCOL = 8


def unit_entries(key, salt):
    folded = jax.random.fold_in(key, salt)
    entries = jax.random.normal(folded, (PANELS, PANEL_WIDTH, PANEL_WIDTH), jnp.float32)
    return jnp.clip(entries, -4.0, 4.0)


def draw_upper_inv(key, part):
    entries = unit_entries(key, 11)
    column_ids = jnp.arange(PANEL_WIDTH, dtype=jnp.float32) + 1.0
    column_factor = 1.0 / jnp.sqrt(column_ids * PANEL_WIDTH)
    return (entries * column_factor[None, None, :]).astype(jnp.bfloat16)


def draw_lower_inv(key, part):
    entries = unit_entries(key, 23)
    row_ids = jnp.arange(PANEL_WIDTH, dtype=jnp.float32) + 1.0
    row_factor = 1.0 / jnp.sqrt(row_ids)
    return (entries * row_factor[None, :, None]).astype(jnp.bfloat16)


def steps_of(rng, shape, cuts, least, largest):
    def one(position, parts):
        steps = jax.random.uniform(jax.random.fold_in(jax.random.fold_in(rng, 6), position), (parts,), jnp.float32, least / len(cuts), largest / len(cuts))
        return jnp.repeat(jnp.exp(steps), shape[position] // parts).reshape((-1,) + (1,) * (len(shape) - position - 1))

    loudness = one(*cuts[0])
    for cut in cuts[1:]:
        loudness = loudness * one(*cut)
    return loudness


def noise(rng, extent, spread, bound, shards=(), kind=jnp.bfloat16):
    values = spread * jax.random.normal(rng, extent, jnp.float32)
    if shards:
        values = values * steps_of(rng, extent, shards, -0.22, 0.18)
    return jnp.clip(values, -bound, bound).astype(kind)


def setup_inputs(seed: int = 0) -> dict:
    seeds = jax.random.split(jax.random.key(seed), 7)
    return {
        "matrix": noise(seeds[0], (RB, N_PROW, PANEL_WIDTH, CB, N_PCOL, PANEL_WIDTH), 1.0, 6.0, ((1, 4), (4, 8))),
        "upper_inv": draw_upper_inv(jax.random.fold_in(seeds[6], 71), 0),
        "lower_inv": draw_lower_inv(jax.random.fold_in(seeds[6], 71), 0),
        "solution": noise(seeds[3], (CB, N_PCOL, PANEL_WIDTH), N ** -0.5, 0.046875, ((1, 8),)),
        "right_side": noise(seeds[4], (RB, N_PROW, PANEL_WIDTH), 1.0, 6.0, ((1, 4),), jnp.float32),
        "diagonal_block_inverses": noise(seeds[5], (PROW_BLOCK_ROWS, N_PROW, PANEL_WIDTH, PANEL_WIDTH), (PANEL_WIDTH * PANEL_WIDTH * SOLVE_BLOCK_ROWS // 6) ** -0.5, 0.013671875, ((1, 4),)),
    }


def reference(matrix, upper_inv, lower_inv, solution, right_side, diagonal_block_inverses):
    base_matrix = matrix.reshape(N, N)
    current = base_matrix
    for section in range(PANELS):
        upper_tri = jnp.triu(upper_inv[section])
        lower_tri = jnp.tril(lower_inv[section])
        column = current[:, section * PANEL_WIDTH:(section + 1) * PANEL_WIDTH]
        row_band = current[section * PANEL_WIDTH:(section + 1) * PANEL_WIDTH, :]
        left_panel = jnp.dot(column, upper_tri, preferred_element_type=jnp.float32).astype(jnp.bfloat16)
        top_panel = jnp.dot(lower_tri, row_band, preferred_element_type=jnp.float32).astype(jnp.bfloat16)
        current = (current.astype(jnp.float32) - jnp.dot(left_panel, top_panel, preferred_element_type=jnp.float32)).astype(jnp.bfloat16)
    updated = current.reshape(matrix.shape)
    residual = right_side.reshape(N) - jnp.dot(base_matrix, solution.reshape(N), preferred_element_type=jnp.float32)
    res_blocks = residual.reshape(N // PANEL_WIDTH, PANEL_WIDTH)
    inverses = diagonal_block_inverses.reshape(SOLVE_BLOCK_ROWS, PANEL_WIDTH, PANEL_WIDTH)
    leading = base_matrix[:SOLVE_BLOCK_ROWS * PANEL_WIDTH, :SOLVE_BLOCK_ROWS * PANEL_WIDTH]

    def carry_forward(blk_id, state):
        rounded, solved = state
        row_piece = lax.dynamic_slice_in_dim(leading, blk_id * PANEL_WIDTH, PANEL_WIDTH, 0)
        pending = jnp.dot(row_piece, rounded.reshape(SOLVE_BLOCK_ROWS * PANEL_WIDTH), preferred_element_type=jnp.float32)
        res_block = lax.dynamic_slice_in_dim(res_blocks, blk_id, 1, 0)[0]
        inv_block = lax.dynamic_slice_in_dim(inverses, blk_id, 1, 0)[0].astype(jnp.float32)
        new_value = jnp.dot(inv_block, res_block - pending, precision=lax.Precision.HIGHEST)
        solved = lax.dynamic_update_slice_in_dim(solved, new_value[None], blk_id, 0)
        rounded = lax.dynamic_update_slice_in_dim(rounded, new_value.astype(jnp.bfloat16)[None], blk_id, 0)
        return rounded, solved

    start = (jnp.zeros((SOLVE_BLOCK_ROWS, PANEL_WIDTH), jnp.bfloat16), jnp.zeros((SOLVE_BLOCK_ROWS, PANEL_WIDTH), jnp.float32))
    precond = lax.fori_loop(0, SOLVE_BLOCK_ROWS, carry_forward, start)[1]
    return updated, residual.reshape(right_side.shape), precond
```

```python
import jax
import jax.numpy as jnp
from jax import lax
from jax.experimental import pallas as pl
from jax.experimental.pallas import tpu as pltpu
from jax.sharding import PartitionSpec as P

LANES = 128
VMEM_BYTES = 48 * 1024 * 1024
F32 = jnp.float32
BF16 = jnp.bfloat16


def matmul(a, b):
    return jnp.dot(a, b, preferred_element_type=F32)


def extract_kernel(groups, stride, a_ref, sol_ref, col_ref, part_ref, wide):
    rows = col_ref.shape[0]
    wide[...] = a_ref[...].astype(F32)
    total = jnp.zeros((rows, LANES), F32)
    for g in range(groups):
        piece = wide[pl.ds(g, rows, stride=groups), :]
        if g % stride == 0:
            col_ref[:, pl.ds(g // stride * LANES, LANES)] = piece.astype(BF16)
        total = total + piece * sol_ref[g : g + 1, :].astype(F32)
    ones = jnp.ones((8, LANES), F32)
    sums = lax.dot_general(
        ones, total, (((1,), (1,)), ((), ())), precision=lax.Precision.HIGHEST, preferred_element_type=F32
    )
    part_ref[...] = sums[0:1, :]


def extract(flat, sol, first, rows, groups, stride, width):
    size = rows * groups
    assert (first * groups) % size == 0
    at = first * groups // size
    return pl.pallas_call(
        lambda *refs: extract_kernel(groups, stride, *refs),
        grid=(1,),
        in_specs=[
            pl.BlockSpec((size, LANES), lambda i: (at, 0)),
            pl.BlockSpec((groups, LANES), lambda i: (0, 0)),
        ],
        out_specs=[
            pl.BlockSpec((rows, width), lambda i: (0, 0)),
            pl.BlockSpec((1, rows), lambda i: (0, 0)),
        ],
        out_shape=[
            jax.ShapeDtypeStruct((rows, width), BF16),
            jax.ShapeDtypeStruct((1, rows), F32),
        ],
        scratch_shapes=[pltpu.VMEM((size, LANES), F32)],
        compiler_params=pltpu.CompilerParams(vmem_limit_bytes=VMEM_BYTES),
        cost_estimate=pl.CostEstimate(flops=4 * size * LANES, bytes_accessed=size * LANES * 2, transcendentals=0),
        name="extract",
    )(flat, sol)


def factor_kernel(groups, where_ref, mine_ref, other_ref, blk_mine_ref, blk_other_ref, up_ref, low_ref, v_ref, bands, blocks):
    core = where_ref[0]
    lane = where_ref[1]
    width = up_ref.shape[1]
    bands[core] = mine_ref[...].astype(F32)
    bands[1 - core] = other_ref[...].astype(F32)
    blocks[core] = blk_mine_ref[...]
    blocks[1 - core] = blk_other_ref[...]
    row = lax.broadcasted_iota(jnp.int32, (width, width), 0)
    col = lax.broadcasted_iota(jnp.int32, (width, width), 1)
    zero = jnp.zeros((width, width), BF16)
    upper = [jnp.where(row <= col, up_ref[s], zero) for s in range(2)]
    lower = [jnp.where(row >= col, low_ref[s], zero) for s in range(2)]
    top_01 = matmul(lower[0], blocks[0]).astype(BF16)
    left_10 = matmul(blocks[1], upper[0]).astype(BF16)

    def step(n, carry):
        def band(s):
            return jnp.concatenate(
                [bands[s, pl.ds(2 * n + h, width, stride=groups), :] for h in range(2)], axis=1
            )

        top_0 = matmul(lower[0], band(0).astype(BF16)).astype(BF16)
        rest = (band(1) - matmul(left_10, top_0)).astype(BF16)
        top_1 = matmul(lower[1], rest).astype(BF16)
        v_1 = matmul(upper[1], top_1).astype(BF16)
        mixed = (top_0.astype(F32) - matmul(top_01, v_1)).astype(BF16)
        v_0 = matmul(upper[0], mixed).astype(BF16)
        at = pl.ds(pl.multiple_of(n * 2 * LANES, 2 * LANES), 2 * LANES)
        v_ref[lane, :, at] = v_0
        v_ref[1 - lane, :, at] = v_1
        return carry

    lax.fori_loop(0, groups // 2, step, 0)


def factors(where, mine, other, blk_mine, blk_other, upper, lower, groups):
    width = upper.shape[1]
    cols = groups * LANES
    vmem = pl.BlockSpec(memory_space=pltpu.VMEM)
    return pl.pallas_call(
        lambda *refs: factor_kernel(groups, *refs),
        in_specs=[pl.BlockSpec(memory_space=pltpu.SMEM)] + [vmem] * 6,
        out_specs=vmem,
        out_shape=jax.ShapeDtypeStruct((2, width, cols), BF16),
        scratch_shapes=[
            pltpu.VMEM((2, width * groups, LANES), F32),
            pltpu.VMEM((2, width, width), BF16),
        ],
        compiler_params=pltpu.CompilerParams(vmem_limit_bytes=VMEM_BYTES),
        cost_estimate=pl.CostEstimate(flops=12 * width * width * cols, bytes_accessed=12 * width * cols, transcendentals=0),
        name="factors",
    )(where, mine, other, blk_mine, blk_other, upper, lower)


def update_kernel(groups, a_ref, mine_ref, other_ref, v_ref, *rest):
    out_ref, wide = rest[-2:]
    rows = mine_ref.shape[0]
    for n in range(groups // 2):
        at = slice(n * 2 * LANES, (n + 1) * 2 * LANES)
        value = matmul(mine_ref[...], v_ref[0, :, at]) + matmul(other_ref[...], v_ref[1, :, at])
        for h in range(2):
            wide[pl.ds(2 * n + h, rows, stride=groups), :] = value[:, h * LANES : (h + 1) * LANES]
    out_ref[...] = (a_ref[...].astype(F32) - wide[...]).astype(BF16)


def update(flat, mine, other, v, out, first, groups):
    rows, width = mine.shape
    sub = min(rows, 256)
    size = sub * groups
    base = first // sub
    cols = groups * LANES
    in_specs = [
        pl.BlockSpec((size, LANES), lambda i: (base + i, 0)),
        pl.BlockSpec((sub, width), lambda i: (i, 0)),
        pl.BlockSpec((sub, width), lambda i: (i, 0)),
        pl.BlockSpec((2, width, cols), lambda i: (0, 0, 0)),
    ]
    args = [flat, mine, other, v]
    aliases = {}
    if out is not None:
        in_specs.append(pl.BlockSpec(memory_space=pl.ANY))
        args.append(out)
        aliases = {4: 0}
    return pl.pallas_call(
        lambda *refs: update_kernel(groups, *refs),
        grid=(rows // sub,),
        in_specs=in_specs,
        out_specs=pl.BlockSpec((size, LANES), lambda i: (base + i, 0)),
        out_shape=jax.ShapeDtypeStruct(flat.shape, BF16),
        scratch_shapes=[pltpu.VMEM((size, LANES), F32)],
        input_output_aliases=aliases,
        compiler_params=pltpu.CompilerParams(vmem_limit_bytes=VMEM_BYTES),
        cost_estimate=pl.CostEstimate(
            flops=4 * rows * width * cols, bytes_accessed=4 * rows * cols + 4 * rows * width + 4 * width * cols, transcendentals=0
        ),
        name="update",
    )(*args)


def solve_kernel(place_ref, state_ref, res_ref, inv_ref, *rest):
    cols, out_ref = rest[:-1], rest[-1]
    place = place_ref[0]
    width = inv_ref.shape[0]
    nt = (((1,), (1,)), ((), ()))
    pending = jnp.zeros((8, width), F32)
    for j, col in enumerate(cols):
        known = jnp.where(j < place, state_ref[j : j + 1, :], 0.0)
        pending = pending + lax.dot_general(
            jnp.broadcast_to(known, (8, width)).astype(BF16), col[...], nt, preferred_element_type=F32
        )
    left = res_ref[...] - pending[0:1, :]
    high = left.astype(BF16)
    rest_1 = left - high.astype(F32)
    mid = rest_1.astype(BF16)
    low = (rest_1 - mid.astype(F32)).astype(BF16)
    total = jnp.zeros((8, width), F32)
    for piece in (low, mid, high):
        wide = jnp.broadcast_to(piece.astype(F32), (8, width)).astype(BF16)
        total = total + lax.dot_general(wide, inv_ref[...], nt, preferred_element_type=F32)
    row = lax.broadcasted_iota(jnp.int32, state_ref.shape, 0)
    out_ref[...] = jnp.where(row == place, jnp.broadcast_to(total[0:1, :], state_ref.shape), state_ref[...])


def solve_step(place, state, res, inv, cols):
    vmem = pl.BlockSpec(memory_space=pltpu.VMEM)
    return pl.pallas_call(
        solve_kernel,
        in_specs=[pl.BlockSpec(memory_space=pltpu.SMEM)] + [vmem] * (3 + len(cols)),
        out_specs=vmem,
        out_shape=jax.ShapeDtypeStruct(state.shape, F32),
        compiler_params=pltpu.CompilerParams(vmem_limit_bytes=VMEM_BYTES),
        cost_estimate=pl.CostEstimate(
            flops=2 * inv.size * (len(cols) + 3), bytes_accessed=2 * inv.size * (len(cols) + 1), transcendentals=0
        ),
        name="solve",
    )(place, state, res, inv, *cols)


def after(value, *others):
    return lax.optimization_barrier((value, *others))[0]


def shards(matrix, upper_inv, lower_inv, solution, right_side, diagonal_block_inverses):
    slots, _, width, col_slots, _, _ = matrix.shape
    n_prow = lax.axis_size("prow")
    n_pcol = lax.axis_size("pcol")
    ny = n_prow // 2
    nz = n_pcol // ny
    prow = lax.axis_index("prow")
    pcol = lax.axis_index("pcol")
    z, y = pcol // ny, pcol % ny
    core, lane = prow % 2, y % 2
    lane_tiles = width // LANES
    groups = lane_tiles * col_slots
    rows = slots * width
    flat = matrix.reshape(rows, col_slots, lane_tiles, LANES).transpose(0, 2, 1, 3).reshape(rows * groups, LANES)
    sol = solution.reshape(col_slots, lane_tiles, LANES).transpose(1, 0, 2).reshape(groups, LANES)

    def spread(value, axis, size):
        for s in range(2, size, 2):
            got = lax.ppermute(value, axis, [(s - 2, s), (s - 1, s + 1)])
            value = jnp.where(lax.axis_index(axis) // 2 == s // 2, got, value)
        return value

    def swap(value, axis, size, bit=1):
        return lax.ppermute(value, axis, [(i, i ^ bit) for i in range(size)])

    band = flat[: width * groups]
    band_mine = spread(band, "prow", n_prow)
    band_other = swap(band_mine, "prow", n_prow)

    def along_z(pairs):
        return [(a * ny + k, b * ny + k) for a, b in pairs for k in range(2)]

    def send_down(local):
        value = local
        step = nz // 2
        held = [0]
        while step:
            if held == [0]:
                moves = [[(0, step)]]
            else:
                moves = [[(m, m - step) for m in held], [(m, m + step) for m in held]]
            got = [(lax.ppermute(value, "pcol", along_z(m)), m) for m in moves]
            for arrived, m in got:
                mask = z == m[0][1]
                for _, b in m[1:]:
                    mask = mask | (z == b)
                value = jnp.where(mask, arrived, value)
            held = [b for m in moves for _, b in m]
            step //= 2
        for s in range(2, ny, 2):
            pairs = [(a * ny + s - 2 + k, a * ny + s + k) for a in range(nz) for k in range(2)]
            got_y = lax.ppermute(value, "pcol", pairs)
            value = jnp.where(y // 2 == s // 2, got_y, value)
        other = swap(value, "pcol", n_pcol)
        return value, other

    column, parts = [], []
    for c in range(slots):
        col, part = extract(flat, sol, c * width, width, groups, col_slots, width)
        column.append(col)
        parts.append(part)
    mine, other = [], []
    for c in range(slots):
        local = column[c]
        if c >= 2:
            local = after(local, mine[c - 2])
        m, o = send_down(local)
        mine.append(m)
        other.append(o)

    pick = jnp.where(core != lane, mine[0], other[0])
    blk_mine = spread(pick, "prow", n_prow)
    blk_other = swap(blk_mine, "prow", n_prow)

    total = jnp.concatenate(parts, axis=0)
    bit = 1
    while bit < n_pcol:
        total = total + swap(total, "pcol", n_pcol, bit)
        bit *= 2
    residual = right_side.reshape(slots, width) - total

    count = n_prow * diagonal_block_inverses.shape[0]
    assert diagonal_block_inverses.shape[0] == 1
    home = count - 2
    inv = diagonal_block_inverses.reshape(width, width)
    needed = [jnp.where(lane == 0, mine[0], other[0]), jnp.where(lane == 0, other[0], mine[0])]
    for j in range(2, home):
        needed.append(lax.ppermute(column[0], "pcol", [(j, home)]))
    needed.append(column[0])
    place = prow.astype(jnp.int32).reshape(1)
    state = jnp.zeros((count, width), F32)
    for k in range(count):
        if k:
            state = lax.ppermute(state, "prow", [(i, i + 1) for i in range(n_prow - 1)])
        state = solve_step(place, state, residual[0:1], inv, needed)
    state = jnp.where((prow == n_prow - 1) & (pcol == home), state, 0.0)
    for axis, size in (("prow", n_prow), ("pcol", n_pcol)):
        bit = 1
        while bit < size:
            state = state + swap(state, axis, size, bit)
            bit *= 2

    where = jnp.stack([core, lane]).astype(jnp.int32)
    v = factors(where, band_mine, band_other, blk_mine, blk_other, upper_inv, lower_inv, groups)
    out = None
    for c in range(slots):
        out = update(flat, mine[c], other[c], v, out, c * width, groups)
    updated = out.reshape(rows, lane_tiles, col_slots, LANES).transpose(0, 2, 1, 3).reshape(matrix.shape)
    return (updated, residual.reshape(right_side.shape), state)


def solution(mesh):
    return jax.shard_map(
        shards,
        mesh=mesh,
        in_specs=(
            P(None, "prow", None, None, "pcol", None),
            P(),
            P(),
            P(None, "pcol", None),
            P(None, "prow", None),
            P(None, "prow", None, None),
        ),
        out_specs=(P(None, "prow", None, None, "pcol", None), P(None, "prow", None), P()),
        check_vma=False,
    )
```

```python
import jax
import jax.numpy as jnp
from jax import lax
from jax.experimental import pallas as pl
from jax.experimental.pallas import tpu as pltpu
from jax.sharding import PartitionSpec as P

LANES = 128
VMEM_BYTES = 28 * 1024 * 1024
F32 = jnp.float32
BF16 = jnp.bfloat16


def matmul(a, b):
    return jnp.dot(a, b, preferred_element_type=F32)


class Chain:
    def __init__(self):
        self.token = None

    def __call__(self, kernel, inputs, in_specs, out_shape, out_specs, name, work, after=(), grid=None, scratch=(), aliases=None):
        deps = list(after) + ([] if self.token is None else [self.token])
        n_in, n_out, n_dep = len(inputs), len(out_shape), len(deps)
        anywhere = pl.BlockSpec(memory_space=pl.ANY)

        def body(*refs):
            outs = n_in + n_dep
            kernel(*refs[:n_in], *refs[outs : outs + n_out], *refs[outs + n_out + 1 :])

        params = {} if grid is None else {"grid": grid}
        *results, self.token = pl.pallas_call(
            body,
            in_specs=list(in_specs) + [anywhere] * n_dep,
            out_specs=list(out_specs) + [anywhere],
            out_shape=list(out_shape) + [jax.ShapeDtypeStruct((8, LANES), F32)],
            scratch_shapes=list(scratch),
            input_output_aliases=aliases or {},
            compiler_params=pltpu.CompilerParams(vmem_limit_bytes=VMEM_BYTES),
            cost_estimate=pl.CostEstimate(flops=work[0], bytes_accessed=work[1], transcendentals=0),
            name=name,
            **params,
        )(*inputs, *deps)
        return results[0] if len(results) == 1 else results

    def gate(self, values, after):
        anywhere = pl.BlockSpec(memory_space=pl.ANY)
        return self(
            lambda *refs: None,
            values,
            [anywhere] * len(values),
            [jax.ShapeDtypeStruct(v.shape, v.dtype) for v in values],
            [anywhere] * len(values),
            "gate",
            (0, 0),
            after=after,
            aliases={i: i for i in range(len(values))},
        )

    def add(self, a, b):
        def kernel(a_ref, b_ref, out_ref):
            out_ref[...] = a_ref[...] + b_ref[...]

        vmem = pl.BlockSpec(memory_space=pltpu.VMEM)
        return self(kernel, [a, b], [vmem] * 2, [jax.ShapeDtypeStruct(a.shape, a.dtype)], [vmem], "add", (a.size, 12 * a.size))

    def choose(self, index, values):
        def kernel(index_ref, *refs):
            for i, ref in enumerate(refs[:-1]):

                @pl.when(index_ref[0] == i)
                def _(ref=ref):
                    refs[-1][...] = ref[...]

        vmem = pl.BlockSpec(memory_space=pltpu.VMEM)
        value = values[0]
        return self(
            kernel,
            [index, *values],
            [pl.BlockSpec(memory_space=pltpu.SMEM)] + [vmem] * len(values),
            [jax.ShapeDtypeStruct(value.shape, value.dtype)],
            [vmem],
            "choose",
            (value.size, 4 * value.size),
        )


def transpose8(x):
    at = lax.broadcasted_iota(jnp.int32, x[0].shape, 1)
    for d in (4, 2, 1):
        low = (at & d) == 0
        y = list(x)
        for i in range(8):
            if i & d == 0:
                a, b = x[i], x[i + d]
                y[i] = jnp.where(low, a, pltpu.roll(b, d, 1))
                y[i + d] = jnp.where(low, pltpu.roll(a, 8 - d, 1), b)
        x = y
    return x


def sum8(x):
    at = lax.broadcasted_iota(jnp.int32, x[0].shape, 1)
    for d in (4, 2, 1):
        low = (at & d) == 0
        y = []
        for a, b in zip(x[:d], x[d : 2 * d]):
            gone = jnp.where(low, b, a)
            back = pltpu.roll(gone, d, 1)
            if d != 4:
                back = jnp.where(low, pltpu.roll(gone, 8 - d, 1), back)
            y.append(jnp.where(low, a, b) + back)
        x = y
    return x[0]


def extract_kernel(groups, stride, a_ref, sol_ref, col_ref, part_ref, *rest):
    wide = rest[-1]
    rows = col_ref.shape[0]
    if len(rest) > 1:
        rest[0][...] = a_ref[...]
    wide[...] = a_ref[...].astype(F32)
    for g in range(0, groups, stride):
        piece = wide[pl.ds(g, rows, stride=groups), :]
        col_ref[:, pl.ds(g // stride * LANES, LANES)] = piece.astype(BF16)
    if groups % 16 == 0:
        sol = sol_ref[...].astype(F32)
        totals = []
        for block in range(rows // 8):
            sums = []
            for r in range(8):
                base = (block * 8 + r) * groups
                sums.append(
                    sum(wide[pl.ds(base + 8 * h, 8), :] * sol[8 * h : 8 * h + 8] for h in range(groups // 8))[None]
                )
            totals.append(sum8(sums)[0])
        total = jnp.concatenate(totals, axis=0)
    else:
        total = jnp.zeros((rows, LANES), F32)
        for g in range(groups):
            total = total + wide[pl.ds(g, rows, stride=groups), :] * sol_ref[g : g + 1, :].astype(F32)
    ones = jnp.ones((8, LANES), F32)
    sums = lax.dot_general(
        ones, total, (((1,), (1,)), ((), ())), precision=lax.Precision.HIGHEST, preferred_element_type=F32
    )
    part_ref[...] = sums[0:1, :]


def extract(chain, flat, sol, first, rows, groups, stride, width, with_band):
    sub = min(rows, 128)
    size = sub * groups
    at = first // sub
    out_specs = [
        pl.BlockSpec((sub, width), lambda i: (i, 0)),
        pl.BlockSpec((1, sub), lambda i: (0, i)),
    ]
    out_shape = [
        jax.ShapeDtypeStruct((rows, width), BF16),
        jax.ShapeDtypeStruct((1, rows), F32),
    ]
    if with_band:
        out_specs.append(pl.BlockSpec((size, LANES), lambda i: (i, 0)))
        out_shape.append(jax.ShapeDtypeStruct((rows * groups, LANES), BF16))
    return chain(
        lambda *refs: extract_kernel(groups, stride, *refs),
        [flat, sol],
        [
            pl.BlockSpec((size, LANES), lambda i: (at + i, 0)),
            pl.BlockSpec((groups, LANES), lambda i: (0, 0)),
        ],
        out_shape,
        out_specs,
        "extract",
        (4 * rows * groups * LANES, rows * groups * LANES * 2),
        grid=(rows // sub,),
        scratch=[pltpu.VMEM((size, LANES), F32)],
    )


def factor_kernel(groups, where_ref, mine_ref, other_ref, blk_mine_ref, blk_other_ref, up_ref, low_ref, v_ref, bands, blocks, *rest):
    core = where_ref[0]
    lane = where_ref[1]
    width = up_ref.shape[1]
    blocks[core] = blk_mine_ref[...]
    blocks[1 - core] = blk_other_ref[...]
    if groups % 16 == 0:
        for slot, ref in ((core, mine_ref), (1 - core, other_ref)):

            def one(block, carry):
                raw = ref[pl.ds(pl.multiple_of(block * 16 * groups, 16 * groups), 16 * groups), :]
                raw = raw.astype(F32).reshape(2, 8, groups, LANES)
                rows = pl.ds(pl.multiple_of(block * 16, 16), 16)
                for h in range(groups // 8):
                    turned = transpose8([raw[:, r, 8 * h : 8 * h + 8] for r in range(8)])
                    for g in range(8):
                        at = pl.ds((8 * h + g) * LANES, LANES)
                        bands[slot, rows, at] = turned[g].reshape(16, LANES).astype(BF16)
                return carry

            lax.fori_loop(0, width // 16, one, 0)
    else:
        wide = rest[0]
        for slot, ref in ((core, mine_ref), (1 - core, other_ref)):
            wide[...] = ref[...].astype(F32)
            for g in range(groups):
                at = pl.ds(g * LANES, LANES)
                bands[slot, :, at] = wide[pl.ds(g, width, stride=groups), :].astype(BF16)
    row = lax.broadcasted_iota(jnp.int32, (width, width), 0)
    col = lax.broadcasted_iota(jnp.int32, (width, width), 1)
    zero = jnp.zeros((width, width), BF16)
    upper = [jnp.where(row <= col, up_ref[s], zero) for s in range(2)]
    lower = [jnp.where(row >= col, low_ref[s], zero) for s in range(2)]
    top_01 = matmul(lower[0], blocks[0]).astype(BF16)
    left_10 = matmul(blocks[1], upper[0]).astype(BF16)
    piece = min(groups * LANES, 1024)
    for n in range(groups * LANES // piece):
        at = slice(n * piece, (n + 1) * piece)
        top_0 = matmul(lower[0], bands[0, :, at]).astype(BF16)
        rest_1 = (bands[1, :, at].astype(F32) - matmul(left_10, top_0)).astype(BF16)
        top_1 = matmul(lower[1], rest_1).astype(BF16)
        v_1 = matmul(upper[1], top_1).astype(BF16)
        mixed = (top_0.astype(F32) - matmul(top_01, v_1)).astype(BF16)
        v_0 = matmul(upper[0], mixed).astype(BF16)
        v_ref[lane, :, at] = v_0
        v_ref[1 - lane, :, at] = v_1


def factors(chain, where, mine, other, blk_mine, blk_other, upper, lower, groups):
    width = upper.shape[1]
    cols = groups * LANES
    vmem = pl.BlockSpec(memory_space=pltpu.VMEM)
    scratch = [pltpu.VMEM((2, width, cols), BF16), pltpu.VMEM((2, width, width), BF16)]
    if groups % 16:
        scratch.append(pltpu.VMEM((width * groups, LANES), F32))
    return chain(
        lambda *refs: factor_kernel(groups, *refs),
        [where, mine, other, blk_mine, blk_other, upper, lower],
        [pl.BlockSpec(memory_space=pltpu.SMEM)] + [vmem] * 6,
        [jax.ShapeDtypeStruct((2, width, cols), BF16)],
        [vmem],
        "factors",
        (12 * width * width * cols, 12 * width * cols),
        scratch=scratch,
    )


def update_kernel(groups, a_ref, mine_ref, other_ref, v_ref, *rest):
    rows = mine_ref.shape[0]
    if groups % 16 == 0:
        out_ref = rest[-1]
        part = min(rows, 256)
        for p in range(rows // part):
            at = slice(p * part, (p + 1) * part)
            value = matmul(mine_ref[at, :], v_ref[0]) + matmul(other_ref[at, :], v_ref[1])
            for block in range(part // 8):
                cut = value[block * 8 : block * 8 + 8, :]
                halves = [
                    transpose8([cut[:, (8 * h + g) * LANES : (8 * h + g + 1) * LANES][None] for g in range(8)])
                    for h in range(groups // 8)
                ]
                for r in range(8):
                    here = pl.ds((p * part + block * 8 + r) * groups, groups)
                    change = jnp.concatenate([half[r][0] for half in halves], axis=0)
                    out_ref[here, :] = (a_ref[here, :].astype(F32) - change).astype(BF16)
        return
    out_ref, wide = rest[-2:]
    value = matmul(mine_ref[...], v_ref[0]) + matmul(other_ref[...], v_ref[1])
    for g in range(groups):
        wide[pl.ds(g, rows, stride=groups), :] = value[:, g * LANES : (g + 1) * LANES]
    out_ref[...] = (a_ref[...].astype(F32) - wide[...]).astype(BF16)


def update(chain, flat, mine, other, v, out, first, groups):
    rows, width = mine.shape
    sub = min(rows, 512)
    size = sub * groups
    base = first // sub
    cols = groups * LANES
    in_specs = [
        pl.BlockSpec((size, LANES), lambda i: (base + i, 0)),
        pl.BlockSpec((sub, width), lambda i: (i, 0)),
        pl.BlockSpec((sub, width), lambda i: (i, 0)),
        pl.BlockSpec(memory_space=pltpu.VMEM),
    ]
    args = [flat, mine, other, v]
    aliases = {}
    if out is not None:
        in_specs.append(pl.BlockSpec(memory_space=pl.ANY))
        args.append(out)
        aliases = {4: 0}
    return chain(
        lambda *refs: update_kernel(groups, *refs),
        args,
        in_specs,
        [jax.ShapeDtypeStruct(flat.shape, BF16)],
        [pl.BlockSpec((size, LANES), lambda i: (base + i, 0))],
        "update",
        (4 * rows * width * cols, 4 * rows * cols + 4 * rows * width),
        grid=(rows // sub,),
        scratch=[pltpu.VMEM((size, LANES), F32)] if groups % 16 else [],
        aliases=aliases,
    )


def solve_kernel(place_ref, state_ref, res_ref, inv_ref, *rest):
    cols, out_ref = rest[:-1], rest[-1]
    place = place_ref[0]
    width = inv_ref.shape[0]
    nt = (((1,), (1,)), ((), ()))
    pending = jnp.zeros((8, width), F32)
    for j, col in enumerate(cols):
        known = jnp.where(j < place, state_ref[j : j + 1, :], 0.0)
        pending = pending + lax.dot_general(
            jnp.broadcast_to(known, (8, width)).astype(BF16), col[...], nt, preferred_element_type=F32
        )
    left = res_ref[...] - pending[0:1, :]
    high = left.astype(BF16)
    rest_1 = left - high.astype(F32)
    mid = rest_1.astype(BF16)
    low = (rest_1 - mid.astype(F32)).astype(BF16)
    total = jnp.zeros((8, width), F32)
    for piece in (low, mid, high):
        wide = jnp.broadcast_to(piece.astype(F32), (8, width)).astype(BF16)
        total = total + lax.dot_general(wide, inv_ref[...], nt, preferred_element_type=F32)
    row = lax.broadcasted_iota(jnp.int32, state_ref.shape, 0)
    out_ref[...] = jnp.where(row == place, jnp.broadcast_to(total[0:1, :], state_ref.shape), state_ref[...])


def solve_step(chain, place, state, res, inv, cols):
    vmem = pl.BlockSpec(memory_space=pltpu.VMEM)
    return chain(
        solve_kernel,
        [place, state, res, inv, *cols],
        [pl.BlockSpec(memory_space=pltpu.SMEM)] + [vmem] * (3 + len(cols)),
        [jax.ShapeDtypeStruct(state.shape, F32)],
        [vmem],
        "solve",
        (2 * inv.size * (len(cols) + 3), 2 * inv.size * (len(cols) + 1)),
    )


def shards(matrix, upper_inv, lower_inv, solution, right_side, diagonal_block_inverses):
    slots, _, width, col_slots, _, _ = matrix.shape
    n_prow = lax.axis_size("prow")
    n_pcol = lax.axis_size("pcol")
    ny = n_prow // 2
    nz = n_pcol // ny
    prow = lax.axis_index("prow")
    pcol = lax.axis_index("pcol")
    z, y = pcol // ny, pcol % ny
    core, lane = prow % 2, y % 2
    lane_tiles = width // LANES
    groups = lane_tiles * col_slots
    rows = slots * width
    flat = matrix.reshape(rows, col_slots, lane_tiles, LANES).transpose(0, 2, 1, 3).reshape(rows * groups, LANES)
    sol = solution.reshape(col_slots, lane_tiles, LANES).transpose(1, 0, 2).reshape(groups, LANES)

    chain = Chain()

    def spread(value, axis, size):
        for s in range(2, size, 2):
            got = lax.ppermute(value, axis, [(s - 2, s), (s - 1, s + 1)])
            value = jnp.where(lax.axis_index(axis) // 2 == s // 2, got, value)
        return value

    def swap(value, axis, size, bit=1):
        return lax.ppermute(value, axis, [(i, i ^ bit) for i in range(size)])

    def along_z(pairs):
        return [(a * ny + k, b * ny + k) for a, b in pairs for k in range(2)]

    stages = [[[(0, nz // 2)]]]
    held, step = [nz // 2], nz // 4
    while step:
        stages.append([[(m, m - step) for m in held], [(m, m + step) for m in held]])
        held = [b for moves in stages[-1] for _, b in moves]
        step //= 2

    def picked(got, moves, value):
        mask = z == moves[0][1]
        for _, b in moves[1:]:
            mask = mask | (z == b)
        return jnp.where(mask, got, value)

    def first_stage(local):
        return lax.ppermute(local, "pcol", along_z(stages[0][0]))

    def second_stage(arrived):
        return [lax.ppermute(arrived, "pcol", along_z(moves)) for moves in stages[1]]

    source = jnp.zeros((), jnp.int32)
    for i, moves in enumerate(stages[0] + stages[1]):
        for _, b in moves:
            source = jnp.where(z == b, i + 1, source)
    source = source.astype(jnp.int32).reshape(1)

    def settle(local, arrived, outward):
        value = chain.choose(source, [local, arrived, *outward])
        for stage in stages[2:]:
            gots = [lax.ppermute(value, "pcol", along_z(moves)) for moves in stage]
            for got, moves in zip(gots, stage):
                value = picked(got, moves, value)
        for s in range(2, ny, 2):
            pairs = [(a * ny + s - 2 + k, a * ny + s + k) for a in range(nz) for k in range(2)]
            got = lax.ppermute(value, "pcol", pairs)
            value = jnp.where(y // 2 == s // 2, got, value)
        return value

    count = n_prow * diagonal_block_inverses.shape[0]
    assert diagonal_block_inverses.shape[0] == 1
    home = count - 2
    inv = diagonal_block_inverses.reshape(width, width)
    place = prow.astype(jnp.int32).reshape(1)
    where = jnp.stack([core, lane]).astype(jnp.int32)
    flag = jnp.where(core != lane, 0, 1).astype(jnp.int32).reshape(1)
    bits = [1 << b for b in range(n_pcol.bit_length() - 1)]

    column, parts, first, outward, mine, other, box = [], [], {}, {}, {}, {}, {"out": None}
    for c in range(slots):
        col, part, *band = extract(chain, flat, sol, c * width, width, groups, col_slots, width, c == 0)
        column.append(col)
        parts.append(part)
        if c < 2:
            first[c] = first_stage(col)
        if c == 0:
            box["band"] = spread(band[0], "prow", n_prow)

    def total_step(bit):
        def run():
            if bit == 1:
                box["total"] = jnp.concatenate(parts, axis=0)
            box["total"] = chain.add(box["total"], swap(box["total"], "pcol", n_pcol, bit))
            if bit == bits[-1]:
                box["residual"] = right_side.reshape(slots, width) - box["total"]

        return run

    def solve(k):
        def run():
            if k == 0:
                a, b = mine[0], other[0]
                needed = [jnp.where(lane == 0, a, b), jnp.where(lane == 0, b, a)]
                for j in range(2, home):
                    needed.append(lax.ppermute(column[0], "pcol", [(j, home)]))
                box["needed"] = needed + [column[0]]
                state = jnp.zeros((count, width), F32)
            else:
                state = lax.ppermute(box["state"], "prow", [(i, i + 1) for i in range(n_prow - 1)])
            state = solve_step(chain, place, state, box["residual"][0:1], inv, box["needed"])
            if k == count - 1:
                state = jnp.where((prow == n_prow - 1) & (pcol == home), state, 0.0)
            box["state"] = state

        return run

    def share(axis, size, bit):
        def run():
            box["state"] = chain.add(box["state"], swap(box["state"], axis, size, bit))

        return run

    def blocks_out():
        box["blk"] = spread(chain.choose(flag, [mine[0], other[0]]), "prow", n_prow)

    def blocks_swap():
        band, blk = chain.gate([box["band"], box["blk"]], [])
        box["bands"] = [band, swap(band, "prow", n_prow)]
        box["blks"] = [blk, swap(blk, "prow", n_prow)]

    def make_factors():
        box["v"] = factors(chain, where, *box["bands"], *box["blks"], upper_inv, lower_inv, groups)

    def updates(c):
        def run():
            box["out"] = update(chain, flat, mine[c], other[c], box["v"], box["out"], c * width, groups)

        return run

    def take(c):
        mine[c] = settle(column[c], first[c], outward[c])
        other[c] = swap(mine[c], "pcol", n_pcol)

    total = [total_step(b) for b in bits]
    line = [solve(k) for k in range(count)]
    line += [share("prow", n_prow, 1 << b) for b in range(n_prow.bit_length() - 1)]
    line += [share("pcol", n_pcol, b) for b in bits]
    if slots == 8 and len(line) == 9:
        plan = {
            0: total[:1],
            1: total[1:],
            2: [blocks_out, line[0]],
            3: [line[1], blocks_swap, line[2]],
            4: [line[3], make_factors, line[4]],
            5: [updates(0), line[5], updates(1)],
            6: [line[6], updates(2), line[7], updates(3)],
            7: [line[8], updates(4), updates(5)],
        }
        tail = [updates(6)]
    else:
        plan = {0: total, slots - 1: [blocks_out, blocks_swap, make_factors] + line}
        tail = [updates(c) for c in range(slots - 1)]

    for k in range(slots):
        ahead = [column[k + 2]] if k + 2 < slots else []
        got = chain.gate([first[k], *ahead], [])
        first[k] = got[0] if ahead else got
        outward[k] = second_stage(first[k])
        if ahead:
            column[k + 2] = got[1]
            first[k + 2] = first_stage(column[k + 2])
        if k:
            take(k - 1)
        for task in plan.get(k, []):
            task()
    for task in tail:
        task()
    take(slots - 1)
    updates(slots - 1)()
    residual, out, state = box["residual"], box["out"], box["state"]
    updated = out.reshape(rows, lane_tiles, col_slots, LANES).transpose(0, 2, 1, 3).reshape(matrix.shape)
    return (updated, residual.reshape(right_side.shape), state)


def solution(mesh):
    return jax.shard_map(
        shards,
        mesh=mesh,
        in_specs=(
            P(None, "prow", None, None, "pcol", None),
            P(),
            P(),
            P(None, "pcol", None),
            P(None, "prow", None),
            P(None, "prow", None, None),
        ),
        out_specs=(P(None, "prow", None, None, "pcol", None), P(None, "prow", None), P()),
        check_vma=False,
    )
```

```python
import jax
import jax.numpy as jnp
from jax import lax
from jax.experimental import pallas as pl
from jax.experimental.pallas import tpu as pltpu
from jax.sharding import PartitionSpec as P

LANES = 128
VMEM_BYTES = 50 * 1024 * 1024
F32 = jnp.float32
BF16 = jnp.bfloat16


def matmul(a, b):
    return jnp.dot(a, b, preferred_element_type=F32)


class Chain:
    def __init__(self):
        self.token = None

    def __call__(self, kernel, inputs, in_specs, out_shape, out_specs, name, work, after=(), grid=None, scratch=(), aliases=None):
        deps = list(after) + ([] if self.token is None else [self.token])
        n_in, n_out, n_dep = len(inputs), len(out_shape), len(deps)
        anywhere = pl.BlockSpec(memory_space=pl.ANY)

        def body(*refs):
            outs = n_in + n_dep
            kernel(*refs[:n_in], *refs[outs : outs + n_out], *refs[outs + n_out + 1 :])

        params = {} if grid is None else {"grid": grid}
        *results, self.token = pl.pallas_call(
            body,
            in_specs=list(in_specs) + [anywhere] * n_dep,
            out_specs=list(out_specs) + [anywhere],
            out_shape=list(out_shape) + [jax.ShapeDtypeStruct((8, LANES), F32)],
            scratch_shapes=list(scratch),
            input_output_aliases=aliases or {},
            compiler_params=pltpu.CompilerParams(vmem_limit_bytes=VMEM_BYTES),
            cost_estimate=pl.CostEstimate(flops=work[0], bytes_accessed=work[1], transcendentals=0),
            name=name,
            **params,
        )(*inputs, *deps)
        return results[0] if len(results) == 1 else results

    def gate(self, values, after):
        anywhere = pl.BlockSpec(memory_space=pl.ANY)
        return self(
            lambda *refs: None,
            values,
            [anywhere] * len(values),
            [jax.ShapeDtypeStruct(v.shape, v.dtype) for v in values],
            [anywhere] * len(values),
            "gate",
            (0, 0),
            after=after,
            aliases={i: i for i in range(len(values))},
        )

    def add(self, a, b):
        def kernel(a_ref, b_ref, out_ref):
            out_ref[...] = a_ref[...] + b_ref[...]

        vmem = pl.BlockSpec(memory_space=pltpu.VMEM)
        return self(kernel, [a, b], [vmem] * 2, [jax.ShapeDtypeStruct(a.shape, a.dtype)], [vmem], "add", (a.size, 12 * a.size))

    def choose(self, index, values):
        def kernel(index_ref, *refs):
            *sources, out, sem = refs
            for i, ref in enumerate(sources):

                @pl.when(index_ref[0] == i)
                def _(ref=ref):
                    copy = pltpu.make_async_copy(ref, out, sem)
                    copy.start()
                    copy.wait()

        anywhere = pl.BlockSpec(memory_space=pl.ANY)
        value = values[0]
        return self(
            kernel,
            [index, *values],
            [pl.BlockSpec(memory_space=pltpu.SMEM)] + [anywhere] * len(values),
            [jax.ShapeDtypeStruct(value.shape, value.dtype)],
            [anywhere],
            "choose",
            (0, 4 * value.size),
            scratch=[pltpu.SemaphoreType.DMA],
        )


def transpose8(x):
    at = lax.broadcasted_iota(jnp.int32, x[0].shape, 1)
    for d in (4, 2, 1):
        low = (at & d) == 0
        y = list(x)
        for i in range(8):
            if i & d == 0:
                a, b = x[i], x[i + d]
                y[i] = jnp.where(low, a, pltpu.roll(b, d, 1))
                y[i + d] = jnp.where(low, pltpu.roll(a, 8 - d, 1), b)
        x = y
    return x


def sum8(x):
    at = lax.broadcasted_iota(jnp.int32, x[0].shape, 1)
    for d in (4, 2, 1):
        low = (at & d) == 0
        y = []
        for a, b in zip(x[:d], x[d : 2 * d]):
            gone = jnp.where(low, b, a)
            back = pltpu.roll(gone, d, 1)
            if d != 4:
                back = jnp.where(low, pltpu.roll(gone, 8 - d, 1), back)
            y.append(jnp.where(low, a, b) + back)
        x = y
    return x[0]


def extract_kernel(groups, stride, a_ref, sol_ref, col_ref, part_ref, *rest):
    wide, totals = rest[-2:]
    rows = col_ref.shape[0]
    if len(rest) > 2:
        rest[0][...] = a_ref[...]
    if groups % 16 == 0:
        sol = sol_ref[...].astype(F32)

        def one(block, carry):
            here = pl.ds(pl.multiple_of(block * 8 * groups, 8 * groups), 8 * groups)
            raw = a_ref[here, :].astype(F32)
            wide[here, :] = raw
            raw = raw.reshape(8, groups, LANES) * sol[None]
            sums = [sum(raw[r : r + 1, 8 * h : 8 * h + 8] for h in range(groups // 8)) for r in range(8)]
            totals[pl.ds(pl.multiple_of(block * 8, 8), 8), :] = sum8(sums)[0]
            return carry

        lax.fori_loop(0, rows // 8, one, 0, unroll=4)
    else:
        wide[...] = a_ref[...].astype(F32)
        total = jnp.zeros((rows, LANES), F32)
        for g in range(groups):
            total = total + wide[pl.ds(g, rows, stride=groups), :] * sol_ref[g : g + 1, :].astype(F32)
        totals[...] = total
    for g in range(0, groups, stride):
        piece = wide[pl.ds(g, rows, stride=groups), :]
        col_ref[:, pl.ds(g // stride * LANES, LANES)] = piece.astype(BF16)
    ones = jnp.ones((8, LANES), F32)
    sums = lax.dot_general(
        ones, totals[...], (((1,), (1,)), ((), ())), precision=lax.Precision.HIGHEST, preferred_element_type=F32
    )
    part_ref[...] = sums[0:1, :]


def extract(chain, flat, sol, first, rows, groups, stride, width, with_band):
    sub = min(rows, 128)
    size = sub * groups
    at = first // sub
    out_specs = [
        pl.BlockSpec((sub, width), lambda i: (i, 0)),
        pl.BlockSpec((1, sub), lambda i: (0, i)),
    ]
    out_shape = [
        jax.ShapeDtypeStruct((rows, width), BF16),
        jax.ShapeDtypeStruct((1, rows), F32),
    ]
    if with_band:
        out_specs.append(pl.BlockSpec((size, LANES), lambda i: (i, 0)))
        out_shape.append(jax.ShapeDtypeStruct((rows * groups, LANES), BF16))
    return chain(
        lambda *refs: extract_kernel(groups, stride, *refs),
        [flat, sol],
        [
            pl.BlockSpec((size, LANES), lambda i: (at + i, 0)),
            pl.BlockSpec((groups, LANES), lambda i: (0, 0)),
        ],
        out_shape,
        out_specs,
        "extract",
        (4 * rows * groups * LANES, rows * groups * LANES * 2),
        grid=(rows // sub,),
        scratch=[pltpu.VMEM((size, LANES), F32), pltpu.VMEM((sub, LANES), F32)],
    )


def factor_kernel(groups, n_x, where_ref, *refs):
    core, lane, x = where_ref[0], where_ref[1], where_ref[2]
    given, (up_ref, low_ref, v_ref, raws, bands, blocks, sems, *rest) = refs[: 4 * n_x], refs[4 * n_x :]
    width = up_ref.shape[1]
    for i in range(n_x):

        @pl.when(x == i)
        def _(i=i):
            pairs = [(raws, given[2 * i], given[2 * i + 1]), (blocks, given[2 * n_x + 2 * i], given[2 * n_x + 2 * i + 1])]
            copies = []
            for kind, (target, mine, other) in enumerate(pairs):
                copies.append(pltpu.make_async_copy(mine, target.at[core], sems.at[kind, 0]))
                copies.append(pltpu.make_async_copy(other, target.at[1 - core], sems.at[kind, 1]))
            for copy in copies:
                copy.start()
            for copy in copies:
                copy.wait()

    for slot in range(2):
        if groups % 16 == 0:

            def one(block, carry, slot=slot):
                here = pl.ds(pl.multiple_of(block * 16 * groups, 16 * groups), 16 * groups)
                raw = raws[slot, here, :].astype(F32).reshape(2, 8, groups, LANES)
                rows = pl.ds(pl.multiple_of(block * 16, 16), 16)
                for h in range(groups // 8):
                    turned = transpose8([raw[:, r, 8 * h : 8 * h + 8] for r in range(8)])
                    for g in range(8):
                        at = pl.ds((8 * h + g) * LANES, LANES)
                        bands[slot, rows, at] = turned[g].reshape(16, LANES).astype(BF16)
                return carry

            lax.fori_loop(0, width // 16, one, 0, unroll=2)
        else:
            wide = rest[0]
            wide[...] = raws[slot].astype(F32)
            for g in range(groups):
                at = pl.ds(g * LANES, LANES)
                bands[slot, :, at] = wide[pl.ds(g, width, stride=groups), :].astype(BF16)
    row = lax.broadcasted_iota(jnp.int32, (width, width), 0)
    col = lax.broadcasted_iota(jnp.int32, (width, width), 1)
    zero = jnp.zeros((width, width), BF16)
    upper = [jnp.where(row <= col, up_ref[s], zero) for s in range(2)]
    lower = [jnp.where(row >= col, low_ref[s], zero) for s in range(2)]
    top_01 = matmul(lower[0], blocks[0]).astype(BF16)
    left_10 = matmul(blocks[1], upper[0]).astype(BF16)
    piece = min(groups * LANES, 1024)
    for n in range(groups * LANES // piece):
        at = slice(n * piece, (n + 1) * piece)
        top_0 = matmul(lower[0], bands[0, :, at]).astype(BF16)
        rest_1 = (bands[1, :, at].astype(F32) - matmul(left_10, top_0)).astype(BF16)
        top_1 = matmul(lower[1], rest_1).astype(BF16)
        v_1 = matmul(upper[1], top_1).astype(BF16)
        mixed = (top_0.astype(F32) - matmul(top_01, v_1)).astype(BF16)
        v_0 = matmul(upper[0], mixed).astype(BF16)
        v_ref[pl.ds(pl.multiple_of(lane * width, width), width), at] = v_0
        v_ref[pl.ds(pl.multiple_of((1 - lane) * width, width), width), at] = v_1


def factors(chain, where, bands, blocks, upper, lower, groups):
    width = upper.shape[1]
    cols = groups * LANES
    n_x = len(bands) // 2
    vmem = pl.BlockSpec(memory_space=pltpu.VMEM)
    anywhere = pl.BlockSpec(memory_space=pl.ANY)
    scratch = [
        pltpu.VMEM((2, width * groups, LANES), BF16),
        pltpu.VMEM((2, width, cols), BF16),
        pltpu.VMEM((2, width, width), BF16),
        pltpu.SemaphoreType.DMA((2, 2)),
    ]
    if groups % 16:
        scratch.append(pltpu.VMEM((width * groups, LANES), F32))
    return chain(
        lambda *refs: factor_kernel(groups, n_x, *refs),
        [where, *bands, *blocks, upper, lower],
        [pl.BlockSpec(memory_space=pltpu.SMEM)] + [anywhere] * (4 * n_x) + [vmem] * 2,
        [jax.ShapeDtypeStruct((2 * width, cols), BF16)],
        [vmem],
        "factors",
        (12 * width * width * cols, 12 * width * cols),
        scratch=scratch,
    )


def update_kernel(groups, a_ref, mine_ref, other_ref, v_ref, *rest):
    rows = mine_ref.shape[0]
    both = jnp.concatenate([mine_ref[...], other_ref[...]], axis=1)
    if groups % 16 == 0:
        out_ref, value = rest[-2:]
        part = min(rows, 128)
        for p in range(rows // part):
            value[p] = matmul(both[p * part : (p + 1) * part], v_ref[...])

            def one(block, carry, p=p):
                at = pl.ds(pl.multiple_of(block * 8, 8), 8)
                halves = [
                    transpose8([value[p, at, (8 * h + g) * LANES : (8 * h + g + 1) * LANES][None] for g in range(8)])
                    for h in range(groups // 8)
                ]
                for r in range(8):
                    here = pl.ds(pl.multiple_of((p * part + block * 8 + r) * groups, groups), groups)
                    change = jnp.concatenate([half[r][0] for half in halves], axis=0)
                    out_ref[here, :] = (a_ref[here, :].astype(F32) - change).astype(BF16)
                return carry

            lax.fori_loop(0, part // 8, one, 0, unroll=part // 8)
        return
    out_ref, wide = rest[-2:]
    value = matmul(both, v_ref[...])
    for g in range(groups):
        wide[pl.ds(g, rows, stride=groups), :] = value[:, g * LANES : (g + 1) * LANES]
    out_ref[...] = (a_ref[...].astype(F32) - wide[...]).astype(BF16)


def update(chain, flat, mine, other, v, out, first, groups):
    rows, width = mine.shape
    sub = min(rows, 256)
    size = sub * groups
    base = first // sub
    cols = groups * LANES
    in_specs = [
        pl.BlockSpec((size, LANES), lambda i: (base + i, 0)),
        pl.BlockSpec((sub, width), lambda i: (i, 0)),
        pl.BlockSpec((sub, width), lambda i: (i, 0)),
        pl.BlockSpec(memory_space=pltpu.VMEM),
    ]
    args = [flat, mine, other, v]
    aliases = {}
    if out is not None:
        in_specs.append(pl.BlockSpec(memory_space=pl.ANY))
        args.append(out)
        aliases = {4: 0}
    return chain(
        lambda *refs: update_kernel(groups, *refs),
        args,
        in_specs,
        [jax.ShapeDtypeStruct(flat.shape, BF16)],
        [pl.BlockSpec((size, LANES), lambda i: (base + i, 0))],
        "update",
        (4 * rows * width * cols, 4 * rows * cols + 4 * rows * width),
        grid=(rows // sub,),
        scratch=[pltpu.VMEM((size, LANES), F32) if groups % 16 else pltpu.VMEM((sub // 128, 128, cols), F32)],
        aliases=aliases,
    )


def solve_kernel(place_ref, state_ref, res_ref, inv_ref, *rest):
    cols, out_ref = rest[:-1], rest[-1]
    place = place_ref[0]
    width = inv_ref.shape[0]
    nt = (((1,), (1,)), ((), ()))
    pending = jnp.zeros((8, width), F32)
    for j, col in enumerate(cols):
        known = jnp.where(j < place, state_ref[j : j + 1, :], 0.0)
        pending = pending + lax.dot_general(
            jnp.broadcast_to(known, (8, width)).astype(BF16), col[...], nt, preferred_element_type=F32
        )
    left = res_ref[...] - pending[0:1, :]
    high = left.astype(BF16)
    rest_1 = left - high.astype(F32)
    mid = rest_1.astype(BF16)
    low = (rest_1 - mid.astype(F32)).astype(BF16)
    total = jnp.zeros((8, width), F32)
    for piece in (low, mid, high):
        wide = jnp.broadcast_to(piece.astype(F32), (8, width)).astype(BF16)
        total = total + lax.dot_general(wide, inv_ref[...], nt, preferred_element_type=F32)
    row = lax.broadcasted_iota(jnp.int32, state_ref.shape, 0)
    out_ref[...] = jnp.where(row == place, jnp.broadcast_to(total[0:1, :], state_ref.shape), state_ref[...])


def solve_step(chain, place, state, res, inv, cols):
    vmem = pl.BlockSpec(memory_space=pltpu.VMEM)
    return chain(
        solve_kernel,
        [place, state, res, inv, *cols],
        [pl.BlockSpec(memory_space=pltpu.SMEM)] + [vmem] * (3 + len(cols)),
        [jax.ShapeDtypeStruct(state.shape, F32)],
        [vmem],
        "solve",
        (2 * inv.size * (len(cols) + 3), 2 * inv.size * (len(cols) + 1)),
    )


def shards(matrix, upper_inv, lower_inv, solution, right_side, diagonal_block_inverses):
    slots, _, width, col_slots, _, _ = matrix.shape
    n_prow = lax.axis_size("prow")
    n_pcol = lax.axis_size("pcol")
    ny = n_prow // 2
    nz = n_pcol // ny
    prow = lax.axis_index("prow")
    pcol = lax.axis_index("pcol")
    z, y = pcol // ny, pcol % ny
    core, lane = prow % 2, y % 2
    lane_tiles = width // LANES
    groups = lane_tiles * col_slots
    rows = slots * width
    flat = matrix.reshape(rows, col_slots, lane_tiles, LANES).transpose(0, 2, 1, 3).reshape(rows * groups, LANES)
    sol = solution.reshape(col_slots, lane_tiles, LANES).transpose(1, 0, 2).reshape(groups, LANES)

    chain = Chain()

    def spread(value, axis, size):
        values = [value]
        for s in range(2, size, 2):
            pairs = [(s - 2, s), (s - 1, s + 1), (s, s - 2), (s + 1, s - 1)]
            values.append(lax.ppermute(values[-1], axis, pairs))
        return values

    def swap(value, axis, size, bit=1):
        return lax.ppermute(value, axis, [(i, i ^ bit) for i in range(size)])

    def along_z(pairs, keep=True, extra=()):
        pairs = [*pairs, *extra]
        if keep:
            busy = {i for pair in pairs for i in pair}
            pairs = pairs + [(i, i) for i in range(nz) if i not in busy]
        return [(a * ny + k, b * ny + k) for a, b in pairs for k in range(ny if keep else 2)]

    stages = [[[(0, nz // 2)]]]
    held, step = [nz // 2], nz // 4
    while step:
        stages.append([[(m, m - step) for m in held], [(m, m + step) for m in held]])
        held = [b for moves in stages[-1] for _, b in moves]
        step //= 2

    def picked(got, moves, value):
        mask = z == moves[0][1]
        for _, b in moves[1:]:
            mask = mask | (z == b)
        return jnp.where(mask, got, value)

    def first_stage(local):
        return lax.ppermute(local, "pcol", along_z(stages[0][0]))

    def second_stage(arrived):
        left, right = stages[1]
        back = [(b, a) for a, b in right]
        return [
            lax.ppermute(arrived, "pcol", along_z(left)),
            lax.ppermute(arrived, "pcol", along_z(right, extra=back)),
        ]

    source = jnp.zeros((), jnp.int32)
    for i, moves in enumerate(stages[0] + stages[1]):
        for _, b in moves:
            source = jnp.where(z == b, i + 1, source)
    source = source.astype(jnp.int32).reshape(1)

    def settle(local, arrived, outward):
        value = chain.choose(source, [local, arrived, *outward])
        for stage in stages[2:]:
            gots = [lax.ppermute(value, "pcol", along_z(moves)) for moves in stage]
            for got, moves in zip(gots, stage):
                value = picked(got, moves, value)
        for s in range(2, ny, 2):
            pairs = [(a * ny + s - 2 + k, a * ny + s + k) for a in range(nz) for k in range(2)]
            got = lax.ppermute(value, "pcol", pairs)
            value = jnp.where(y // 2 == s // 2, got, value)
        return value

    count = n_prow * diagonal_block_inverses.shape[0]
    assert diagonal_block_inverses.shape[0] == 1
    home = count - 2
    inv = diagonal_block_inverses.reshape(width, width)
    place = prow.astype(jnp.int32).reshape(1)
    where = jnp.stack([core, lane, prow // 2]).astype(jnp.int32)
    flag = jnp.where(core != lane, 0, 1).astype(jnp.int32).reshape(1)
    bits = [1 << b for b in range(n_pcol.bit_length() - 1)]

    cuts = [(c * width, width) for c in range(slots - 1)]
    cuts += [((slots - 1) * width + h * width // 2, width // 2) for h in range(2)]
    chunks = len(cuts)
    column, parts, first, outward, mine, other, box = {}, {}, {}, {}, {}, {}, {"out": None}
    for c in [0, 2, 3, 1, *range(4, slots)]:
        col, part, *band = extract(chain, flat, sol, c * width, width, groups, col_slots, width, c == 0)
        parts[c] = part
        if c < slots - 1:
            column[c] = col
        else:
            column[c], column[c + 1] = col[: width // 2], col[width // 2 :]
        if c < 2:
            first[c] = first_stage(col)
        if c == 0:
            box["bands"] = spread(band[0], "prow", n_prow)

    def total_step(bit):
        def run():
            if bit == 1:
                box["total"] = jnp.concatenate([parts[c] for c in range(slots)], axis=0)
            box["total"] = chain.add(box["total"], swap(box["total"], "pcol", n_pcol, bit))
            if bit == bits[-1]:
                box["residual"] = right_side.reshape(slots, width) - box["total"]

        return run

    def solve(k):
        def run():
            if k == 0:
                a, b = mine[0], other[0]
                needed = [jnp.where(lane == 0, a, b), jnp.where(lane == 0, b, a)]
                for j in range(2, home):
                    needed.append(lax.ppermute(column[0], "pcol", [(j, home)]))
                box["needed"] = needed + [column[0]]
                state = jnp.zeros((count, width), F32)
            else:
                state = lax.ppermute(box["state"], "prow", [(i, i + 1) for i in range(n_prow - 1)])
            state = solve_step(chain, place, state, box["residual"][0:1], inv, box["needed"])
            if k == count - 1:
                state = jnp.where((prow == n_prow - 1) & (pcol == home), state, 0.0)
            box["state"] = state

        return run

    def share(axis, size, bit):
        def run():
            box["state"] = chain.add(box["state"], swap(box["state"], axis, size, bit))

        return run

    def blocks_out():
        box["blks"] = spread(chain.choose(flag, [mine[0], other[0]]), "prow", n_prow)
        box["bands"] = [v for b in box["bands"] for v in (b, swap(b, "prow", n_prow))]

    def blocks_swap():
        box["blks"] = [v for b in box["blks"] for v in (b, swap(b, "prow", n_prow))]

    def make_factors():
        box["v"] = factors(chain, where, box["bands"], box["blks"], upper_inv, lower_inv, groups)

    def updates(c):
        def run():
            box["out"] = update(chain, flat, mine[c], other[c], box["v"], box["out"], cuts[c][0], groups)

        return run

    def take(c):
        mine[c] = settle(column[c], first[c], outward[c])
        other[c] = swap(mine[c], "pcol", n_pcol)

    total = [total_step(b) for b in bits]
    line = [solve(k) for k in range(count)]
    line += [share("prow", n_prow, 1 << b) for b in range(n_prow.bit_length() - 1)]
    line += [share("pcol", n_pcol, b) for b in bits]
    if slots == 8 and len(line) == 9:
        plan = {
            0: total[:2],
            1: total[2:],
            2: [blocks_out, line[0]],
            3: [blocks_swap, line[1], make_factors],
            4: [updates(0), line[2], updates(1), updates(2)],
            5: [line[3], updates(3), line[4]],
            6: [updates(4), line[5]],
            7: [updates(5), line[6]],
            8: [updates(6), line[7]],
        }
        tail = []
    else:
        plan = {0: total, slots - 1: [blocks_out, blocks_swap, make_factors] + line}
        tail = [updates(c) for c in range(chunks - 2)]
        line = []

    for k in range(chunks):
        ahead = [column[k + 2]] if k + 2 < chunks else []
        got = chain.gate([first[k], *ahead], [])
        first[k] = got[0] if ahead else got
        outward[k] = second_stage(first[k])
        if ahead:
            column[k + 2] = got[1]
            first[k + 2] = first_stage(column[k + 2])
        if k:
            take(k - 1)
        for task in plan.get(k, []):
            task()
    for task in tail:
        task()
    updates(chunks - 2)()
    take(chunks - 1)
    if line:
        line[-1]()
    updates(chunks - 1)()
    residual, out, state = box["residual"], box["out"], box["state"]
    updated = out.reshape(rows, lane_tiles, col_slots, LANES).transpose(0, 2, 1, 3).reshape(matrix.shape)
    return (updated, residual.reshape(right_side.shape), state)


def solution(mesh):
    return jax.shard_map(
        shards,
        mesh=mesh,
        in_specs=(
            P(None, "prow", None, None, "pcol", None),
            P(),
            P(),
            P(None, "pcol", None),
            P(None, "prow", None),
            P(None, "prow", None, None),
        ),
        out_specs=(P(None, "prow", None, None, "pcol", None), P(None, "prow", None), P()),
        check_vma=False,
    )
```

```python
import jax
import jax.numpy as jnp
from jax import lax
from jax.experimental import pallas as pl
from jax.experimental.pallas import tpu as pltpu
from jax.sharding import PartitionSpec as P

LANES = 128
VMEM_BYTES = 50 * 1024 * 1024
F32 = jnp.float32
BF16 = jnp.bfloat16


def matmul(a, b):
    return jnp.dot(a, b, preferred_element_type=F32)


class Chain:
    def __init__(self):
        self.token = None

    def __call__(self, kernel, inputs, in_specs, out_shape, out_specs, name, work, after=(), grid=None, scratch=(), aliases=None):
        deps = list(after) + ([] if self.token is None else [self.token])
        n_in, n_out, n_dep = len(inputs), len(out_shape), len(deps)
        anywhere = pl.BlockSpec(memory_space=pl.ANY)

        def body(*refs):
            outs = n_in + n_dep
            kernel(*refs[:n_in], *refs[outs : outs + n_out], *refs[outs + n_out + 1 :])

        params = {} if grid is None else {"grid": grid}
        *results, self.token = pl.pallas_call(
            body,
            in_specs=list(in_specs) + [anywhere] * n_dep,
            out_specs=list(out_specs) + [anywhere],
            out_shape=list(out_shape) + [jax.ShapeDtypeStruct((8, LANES), F32)],
            scratch_shapes=list(scratch),
            input_output_aliases=aliases or {},
            compiler_params=pltpu.CompilerParams(vmem_limit_bytes=VMEM_BYTES),
            cost_estimate=pl.CostEstimate(flops=work[0], bytes_accessed=work[1], transcendentals=0),
            name=name,
            **params,
        )(*inputs, *deps)
        return results[0] if len(results) == 1 else results

    def gate(self, values, after):
        anywhere = pl.BlockSpec(memory_space=pl.ANY)
        return self(
            lambda *refs: None,
            values,
            [anywhere] * len(values),
            [jax.ShapeDtypeStruct(v.shape, v.dtype) for v in values],
            [anywhere] * len(values),
            "gate",
            (0, 0),
            after=after,
            aliases={i: i for i in range(len(values))},
        )

    def add(self, a, b):
        def kernel(a_ref, b_ref, out_ref):
            out_ref[...] = a_ref[...] + b_ref[...]

        vmem = pl.BlockSpec(memory_space=pltpu.VMEM)
        return self(kernel, [a, b], [vmem] * 2, [jax.ShapeDtypeStruct(a.shape, a.dtype)], [vmem], "add", (a.size, 12 * a.size))

    def choose(self, index, values):
        def kernel(index_ref, *refs):
            *sources, out, sem = refs
            for i, ref in enumerate(sources):

                @pl.when(index_ref[0] == i)
                def _(ref=ref):
                    copy = pltpu.make_async_copy(ref, out, sem)
                    copy.start()
                    copy.wait()

        anywhere = pl.BlockSpec(memory_space=pl.ANY)
        value = values[0]
        return self(
            kernel,
            [index, *values],
            [pl.BlockSpec(memory_space=pltpu.SMEM)] + [anywhere] * len(values),
            [jax.ShapeDtypeStruct(value.shape, value.dtype)],
            [anywhere],
            "choose",
            (0, 4 * value.size),
            scratch=[pltpu.SemaphoreType.DMA],
        )


def transpose8(x):
    at = lax.broadcasted_iota(jnp.int32, x[0].shape, 1)
    for d in (4, 2, 1):
        low = (at & d) == 0
        y = list(x)
        for i in range(8):
            if i & d == 0:
                a, b = x[i], x[i + d]
                y[i] = jnp.where(low, a, pltpu.roll(b, d, 1))
                y[i + d] = jnp.where(low, pltpu.roll(a, 8 - d, 1), b)
        x = y
    return x


def sum8(x):
    at = lax.broadcasted_iota(jnp.int32, x[0].shape, 1)
    for d in (4, 2, 1):
        low = (at & d) == 0
        y = []
        for a, b in zip(x[:d], x[d : 2 * d]):
            gone = jnp.where(low, b, a)
            back = pltpu.roll(gone, d, 1)
            if d != 4:
                back = jnp.where(low, pltpu.roll(gone, 8 - d, 1), back)
            y.append(jnp.where(low, a, b) + back)
        x = y
    return x[0]


def extract_kernel(groups, stride, a_ref, sol_ref, col_ref, part_ref, *rest):
    wide = rest[-1]
    rows = col_ref.shape[0]
    if len(rest) > 1:
        rest[0][...] = a_ref[...]
    wide[...] = a_ref[...].astype(F32)
    for g in range(0, groups, stride):
        piece = wide[pl.ds(g, rows, stride=groups), :]
        col_ref[:, pl.ds(g // stride * LANES, LANES)] = piece.astype(BF16)
    if groups % 16 == 0:
        sol = sol_ref[...].astype(F32)
        totals = []
        for block in range(rows // 8):
            sums = []
            for r in range(8):
                base = (block * 8 + r) * groups
                sums.append(
                    sum(wide[pl.ds(base + 8 * h, 8), :] * sol[8 * h : 8 * h + 8] for h in range(groups // 8))[None]
                )
            totals.append(sum8(sums)[0])
        total = jnp.concatenate(totals, axis=0)
    else:
        total = jnp.zeros((rows, LANES), F32)
        for g in range(groups):
            total = total + wide[pl.ds(g, rows, stride=groups), :] * sol_ref[g : g + 1, :].astype(F32)
    ones = jnp.ones((8, LANES), F32)
    sums = lax.dot_general(
        ones, total, (((1,), (1,)), ((), ())), precision=lax.Precision.HIGHEST, preferred_element_type=F32
    )
    part_ref[...] = sums[0:1, :]


def extract(chain, flat, sol, first, rows, groups, stride, width, with_band):
    sub = min(rows, 128)
    size = sub * groups
    at = first // sub
    out_specs = [
        pl.BlockSpec((sub, width), lambda i: (i, 0)),
        pl.BlockSpec((1, sub), lambda i: (0, i)),
    ]
    out_shape = [
        jax.ShapeDtypeStruct((rows, width), BF16),
        jax.ShapeDtypeStruct((1, rows), F32),
    ]
    if with_band:
        out_specs.append(pl.BlockSpec((size, LANES), lambda i: (i, 0)))
        out_shape.append(jax.ShapeDtypeStruct((rows * groups, LANES), BF16))
    return chain(
        lambda *refs: extract_kernel(groups, stride, *refs),
        [flat, sol],
        [
            pl.BlockSpec((size, LANES), lambda i: (at + i, 0)),
            pl.BlockSpec((groups, LANES), lambda i: (0, 0)),
        ],
        out_shape,
        out_specs,
        "extract",
        (4 * rows * groups * LANES, rows * groups * LANES * 2),
        grid=(rows // sub,),
        scratch=[pltpu.VMEM((size, LANES), F32)],
    )


def factor_kernel(groups, n_x, where_ref, *refs):
    core, lane, x = where_ref[0], where_ref[1], where_ref[2]
    given, (up_ref, low_ref, v_ref, raws, bands, blocks, sems, *rest) = refs[: 4 * n_x], refs[4 * n_x :]
    width = up_ref.shape[1]
    for i in range(n_x):

        @pl.when(x == i)
        def _(i=i):
            pairs = [(raws, given[2 * i], given[2 * i + 1]), (blocks, given[2 * n_x + 2 * i], given[2 * n_x + 2 * i + 1])]
            copies = []
            for kind, (target, mine, other) in enumerate(pairs):
                copies.append(pltpu.make_async_copy(mine, target.at[core], sems.at[kind, 0]))
                copies.append(pltpu.make_async_copy(other, target.at[1 - core], sems.at[kind, 1]))
            for copy in copies:
                copy.start()
            for copy in copies:
                copy.wait()

    for slot in range(2):
        if groups % 16 == 0:

            def one(block, carry, slot=slot):
                here = pl.ds(pl.multiple_of(block * 16 * groups, 16 * groups), 16 * groups)
                raw = raws[slot, here, :].astype(F32).reshape(2, 8, groups, LANES)
                rows = pl.ds(pl.multiple_of(block * 16, 16), 16)
                for h in range(groups // 8):
                    turned = transpose8([raw[:, r, 8 * h : 8 * h + 8] for r in range(8)])
                    for g in range(8):
                        at = pl.ds((8 * h + g) * LANES, LANES)
                        bands[slot, rows, at] = turned[g].reshape(16, LANES).astype(BF16)
                return carry

            lax.fori_loop(0, width // 16, one, 0, unroll=2)
        else:
            wide = rest[0]
            wide[...] = raws[slot].astype(F32)
            for g in range(groups):
                at = pl.ds(g * LANES, LANES)
                bands[slot, :, at] = wide[pl.ds(g, width, stride=groups), :].astype(BF16)
    row = lax.broadcasted_iota(jnp.int32, (width, width), 0)
    col = lax.broadcasted_iota(jnp.int32, (width, width), 1)
    zero = jnp.zeros((width, width), BF16)
    upper = [jnp.where(row <= col, up_ref[s], zero) for s in range(2)]
    lower = [jnp.where(row >= col, low_ref[s], zero) for s in range(2)]
    top_01 = matmul(lower[0], blocks[0]).astype(BF16)
    left_10 = matmul(blocks[1], upper[0]).astype(BF16)
    piece = min(groups * LANES, 1024)
    for n in range(groups * LANES // piece):
        at = slice(n * piece, (n + 1) * piece)
        top_0 = matmul(lower[0], bands[0, :, at]).astype(BF16)
        rest_1 = (bands[1, :, at].astype(F32) - matmul(left_10, top_0)).astype(BF16)
        top_1 = matmul(lower[1], rest_1).astype(BF16)
        v_1 = matmul(upper[1], top_1).astype(BF16)
        mixed = (top_0.astype(F32) - matmul(top_01, v_1)).astype(BF16)
        v_0 = matmul(upper[0], mixed).astype(BF16)
        v_ref[pl.ds(pl.multiple_of(lane * width, width), width), at] = v_0
        v_ref[pl.ds(pl.multiple_of((1 - lane) * width, width), width), at] = v_1


def factors(chain, where, bands, blocks, upper, lower, groups):
    width = upper.shape[1]
    cols = groups * LANES
    n_x = len(bands) // 2
    vmem = pl.BlockSpec(memory_space=pltpu.VMEM)
    anywhere = pl.BlockSpec(memory_space=pl.ANY)
    scratch = [
        pltpu.VMEM((2, width * groups, LANES), BF16),
        pltpu.VMEM((2, width, cols), BF16),
        pltpu.VMEM((2, width, width), BF16),
        pltpu.SemaphoreType.DMA((2, 2)),
    ]
    if groups % 16:
        scratch.append(pltpu.VMEM((width * groups, LANES), F32))
    return chain(
        lambda *refs: factor_kernel(groups, n_x, *refs),
        [where, *bands, *blocks, upper, lower],
        [pl.BlockSpec(memory_space=pltpu.SMEM)] + [anywhere] * (4 * n_x) + [vmem] * 2,
        [jax.ShapeDtypeStruct((2 * width, cols), BF16)],
        [vmem],
        "factors",
        (12 * width * width * cols, 12 * width * cols),
        scratch=scratch,
    )


def update_kernel(groups, chunks, steps, a_ref, v_ref, *rest):
    out_ref, both, *wide = rest[-3 if groups % 16 else -2 :]
    rows, width = both.shape[0], both.shape[1] // 2
    i = pl.program_id(0)
    for c in range(chunks):

        @pl.when(i // steps == c)
        def _(c=c):
            both[:, :width] = rest[2 * c][...]
            both[:, width:] = rest[2 * c + 1][...]

    if groups % 16 == 0:
        part = min(rows, 128)
        for p in range(rows // part):
            value = matmul(both[p * part : (p + 1) * part, :], v_ref[...])
            for block in range(part // 8):
                cut = value[block * 8 : block * 8 + 8, :]
                halves = [
                    transpose8([cut[:, (8 * h + g) * LANES : (8 * h + g + 1) * LANES][None] for g in range(8)])
                    for h in range(groups // 8)
                ]
                for r in range(8):
                    here = pl.ds((p * part + block * 8 + r) * groups, groups)
                    change = jnp.concatenate([half[r][0] for half in halves], axis=0)
                    out_ref[here, :] = (a_ref[here, :].astype(F32) - change).astype(BF16)
        return
    value = matmul(both[...], v_ref[...])
    for g in range(groups):
        wide[0][pl.ds(g, rows, stride=groups), :] = value[:, g * LANES : (g + 1) * LANES]
    out_ref[...] = (a_ref[...].astype(F32) - wide[0][...]).astype(BF16)


def update(chain, flat, mine, other, v, out, first, groups):
    rows, width = mine[0].shape
    chunks = len(mine)
    sub = min(rows, 256)
    steps = rows // sub
    size = sub * groups
    base = first // sub
    cols = groups * LANES
    in_specs = [pl.BlockSpec((size, LANES), lambda i: (base + i, 0)), pl.BlockSpec(memory_space=pltpu.VMEM)]
    args = [flat, v]
    for c in range(chunks):
        args += [mine[c], other[c]]
        in_specs += [pl.BlockSpec((sub, width), lambda i, c=c: (jnp.clip(i - c * steps, 0, steps - 1), 0))] * 2
    aliases = {}
    if out is not None:
        aliases = {len(args): 0}
        in_specs.append(pl.BlockSpec(memory_space=pl.ANY))
        args.append(out)
    scratch = [pltpu.VMEM((sub, 2 * width), BF16)]
    if groups % 16:
        scratch.append(pltpu.VMEM((size, LANES), F32))
    return chain(
        lambda *refs: update_kernel(groups, chunks, steps, *refs),
        args,
        in_specs,
        [jax.ShapeDtypeStruct(flat.shape, BF16)],
        [pl.BlockSpec((size, LANES), lambda i: (base + i, 0))],
        "update",
        (4 * chunks * rows * width * cols, chunks * (4 * rows * cols + 4 * rows * width)),
        grid=(chunks * steps,),
        scratch=scratch,
        aliases=aliases,
    )


def solve_kernel(place_ref, state_ref, res_ref, inv_ref, *rest):
    cols, out_ref = rest[:-1], rest[-1]
    place, lane = place_ref[0], place_ref[1]
    width = inv_ref.shape[0]
    nt = (((1,), (1,)), ((), ()))
    pending = jnp.zeros((8, width), F32)
    for j, col in enumerate(cols):
        at = (j + lane) % 2 if j < 2 else j
        known = jnp.where(at < place, state_ref[pl.ds(at, 1), :], 0.0)
        pending = pending + lax.dot_general(
            jnp.broadcast_to(known, (8, width)).astype(BF16), col[...], nt, preferred_element_type=F32
        )
    left = res_ref[...] - pending[0:1, :]
    high = left.astype(BF16)
    rest_1 = left - high.astype(F32)
    mid = rest_1.astype(BF16)
    low = (rest_1 - mid.astype(F32)).astype(BF16)
    total = jnp.zeros((8, width), F32)
    for piece in (low, mid, high):
        wide = jnp.broadcast_to(piece.astype(F32), (8, width)).astype(BF16)
        total = total + lax.dot_general(wide, inv_ref[...], nt, preferred_element_type=F32)
    row = lax.broadcasted_iota(jnp.int32, state_ref.shape, 0)
    out_ref[...] = jnp.where(row == place, jnp.broadcast_to(total[0:1, :], state_ref.shape), state_ref[...])


def solve_step(chain, place, state, res, inv, cols):
    vmem = pl.BlockSpec(memory_space=pltpu.VMEM)
    return chain(
        solve_kernel,
        [place, state, res, inv, *cols],
        [pl.BlockSpec(memory_space=pltpu.SMEM)] + [vmem] * (3 + len(cols)),
        [jax.ShapeDtypeStruct(state.shape, F32)],
        [vmem],
        "solve",
        (2 * inv.size * (len(cols) + 3), 2 * inv.size * (len(cols) + 1)),
    )


def shards(matrix, upper_inv, lower_inv, solution, right_side, diagonal_block_inverses):
    slots, _, width, col_slots, _, _ = matrix.shape
    n_prow = lax.axis_size("prow")
    n_pcol = lax.axis_size("pcol")
    ny = n_prow // 2
    nz = n_pcol // ny
    prow = lax.axis_index("prow")
    pcol = lax.axis_index("pcol")
    z, y = pcol // ny, pcol % ny
    core, lane = prow % 2, y % 2
    lane_tiles = width // LANES
    groups = lane_tiles * col_slots
    rows = slots * width
    flat = matrix.reshape(rows, col_slots, lane_tiles, LANES).transpose(0, 2, 1, 3).reshape(rows * groups, LANES)
    sol = solution.reshape(col_slots, lane_tiles, LANES).transpose(1, 0, 2).reshape(groups, LANES)

    chain = Chain()

    def spread(value, axis, size):
        values = [value]
        for s in range(2, size, 2):
            pairs = [(s - 2, s), (s - 1, s + 1), (s, s - 2), (s + 1, s - 1)]
            values.append(lax.ppermute(values[-1], axis, pairs))
        return values

    def swap(value, axis, size, bit=1):
        return lax.ppermute(value, axis, [(i, i ^ bit) for i in range(size)])

    def along_z(pairs):
        return [(a * ny + k, b * ny + k) for a, b in pairs for k in range(2)]

    stages = [[[(0, nz // 2)]]]
    held, step = [nz // 2], nz // 4
    while step:
        stages.append([[(m, m - step) for m in held], [(m, m + step) for m in held]])
        held = [b for moves in stages[-1] for _, b in moves]
        step //= 2

    def picked(got, moves, value):
        mask = z == moves[0][1]
        for _, b in moves[1:]:
            mask = mask | (z == b)
        return jnp.where(mask, got, value)

    def first_stage(local):
        return lax.ppermute(local, "pcol", along_z(stages[0][0]))

    def second_stage(arrived):
        return [lax.ppermute(arrived, "pcol", along_z(moves)) for moves in stages[1]]

    source = jnp.zeros((), jnp.int32)
    for i, moves in enumerate(stages[0] + stages[1]):
        for _, b in moves:
            source = jnp.where(z == b, i + 1, source)
    source = source.astype(jnp.int32).reshape(1)

    def settle(local, arrived, outward):
        value = chain.choose(source, [local, arrived, *outward])
        for stage in stages[2:]:
            gots = [lax.ppermute(value, "pcol", along_z(moves)) for moves in stage]
            for got, moves in zip(gots, stage):
                value = picked(got, moves, value)
        for s in range(2, ny, 2):
            pairs = [(a * ny + s - 2 + k, a * ny + s + k) for a in range(nz) for k in range(2)]
            got = lax.ppermute(value, "pcol", pairs)
            value = jnp.where(y // 2 == s // 2, got, value)
        return value

    count = n_prow * diagonal_block_inverses.shape[0]
    assert diagonal_block_inverses.shape[0] == 1
    home = count - 2
    inv = diagonal_block_inverses.reshape(width, width)
    place = jnp.stack([prow, lane]).astype(jnp.int32)
    where = jnp.stack([core, lane, prow // 2]).astype(jnp.int32)
    flag = jnp.where(core != lane, 0, 1).astype(jnp.int32).reshape(1)
    bits = [1 << b for b in range(n_pcol.bit_length() - 1)]

    cuts = [(c * width, width) for c in range(slots - 1)]
    cuts += [((slots - 1) * width + h * width // 2, width // 2) for h in range(2)]
    chunks = len(cuts)
    column, parts, first, outward, mine, other, box = {}, {}, {}, {}, {}, {}, {"out": None}
    for c in [0, 2, 3, 1, *range(4, slots)]:
        col, part, *band = extract(chain, flat, sol, c * width, width, groups, col_slots, width, c == 0)
        parts[c] = part
        if c < slots - 1:
            column[c] = col
        else:
            column[c], column[c + 1] = col[: width // 2], col[width // 2 :]
        if c < 2:
            first[c] = first_stage(col)
        if c == 0:
            box["bands"] = spread(band[0], "prow", n_prow)

    def total_step(bit):
        def run():
            if bit == 1:
                box["total"] = jnp.concatenate([parts[c] for c in range(slots)], axis=0)
            box["total"] = chain.add(box["total"], swap(box["total"], "pcol", n_pcol, bit))
            if bit == bits[-1]:
                box["residual"] = right_side.reshape(slots, width) - box["total"]

        return run

    def solve(k):
        def run():
            if k == 0:
                needed = [mine[0], other[0]]
                for j in range(2, home):
                    needed.append(lax.ppermute(column[0], "pcol", [(j, home)]))
                box["needed"] = needed + [column[0]]
                state = jnp.zeros((count, width), F32)
            else:
                state = lax.ppermute(box["state"], "prow", [(i, i + 1) for i in range(n_prow - 1)])
            state = solve_step(chain, place, state, box["residual"][0:1], inv, box["needed"])
            if k == count - 1:
                state = jnp.where((prow == n_prow - 1) & (pcol == home), state, 0.0)
            box["state"] = state

        return run

    def share(axis, size, bit):
        def run():
            box["state"] = chain.add(box["state"], swap(box["state"], axis, size, bit))

        return run

    def blocks_out():
        box["blks"] = spread(chain.choose(flag, [mine[0], other[0]]), "prow", n_prow)
        box["bands"] = [v for b in box["bands"] for v in (b, swap(b, "prow", n_prow))]

    def blocks_swap():
        box["blks"] = [v for b in box["blks"] for v in (b, swap(b, "prow", n_prow))]

    def make_factors():
        box["v"] = factors(chain, where, box["bands"], box["blks"], upper_inv, lower_inv, groups)

    def updates(*which):
        def run():
            args = [mine[c] for c in which], [other[c] for c in which]
            box["out"] = update(chain, flat, *args, box["v"], box["out"], cuts[which[0]][0], groups)

        return run

    def take(c):
        mine[c] = settle(column[c], first[c], outward[c])
        other[c] = swap(mine[c], "pcol", n_pcol)

    total = [total_step(b) for b in bits]
    line = [solve(k) for k in range(count)]
    line += [share("prow", n_prow, 1 << b) for b in range(n_prow.bit_length() - 1)]
    line += [share("pcol", n_pcol, b) for b in bits]
    if slots == 8 and len(line) == 9:
        plan = {
            0: total[:1],
            1: total[1:2],
            2: [blocks_out, total[2]],
            3: [blocks_swap, line[0]],
            4: [make_factors, line[1], updates(0, 1, 2)],
            5: [line[2], updates(3), line[3]],
            6: [line[4], updates(4, 5)],
            7: [line[5], line[6]],
            8: [updates(6), line[7]],
        }
        tail = []
    else:
        plan = {0: total, slots - 1: [blocks_out, blocks_swap, make_factors] + line}
        tail = [updates(c) for c in range(chunks - 2)]
        line = []

    for k in range(chunks):
        ahead = [column[k + 2]] if k + 2 < chunks else []
        got = chain.gate([first[k], *ahead], [])
        first[k] = got[0] if ahead else got
        outward[k] = second_stage(first[k])
        if ahead:
            column[k + 2] = got[1]
            first[k + 2] = first_stage(column[k + 2])
        if k:
            take(k - 1)
        for task in plan.get(k, []):
            task()
    for task in tail:
        task()
    updates(chunks - 2)()
    take(chunks - 1)
    if line:
        line[-1]()
    updates(chunks - 1)()
    residual, out, state = box["residual"], box["out"], box["state"]
    updated = out.reshape(rows, lane_tiles, col_slots, LANES).transpose(0, 2, 1, 3).reshape(matrix.shape)
    return (updated, residual.reshape(right_side.shape), state)


def solution(mesh):
    return jax.shard_map(
        shards,
        mesh=mesh,
        in_specs=(
            P(None, "prow", None, None, "pcol", None),
            P(),
            P(),
            P(None, "pcol", None),
            P(None, "prow", None),
            P(None, "prow", None, None),
        ),
        out_specs=(P(None, "prow", None, None, "pcol", None), P(None, "prow", None), P()),
        check_vma=False,
    )
```

```python
import jax
import jax.numpy as jnp
from jax import lax
from jax.experimental import pallas as pl
from jax.experimental.pallas import tpu as pltpu
from jax.sharding import PartitionSpec as P

LANES = 128
VMEM_BYTES = 50 * 1024 * 1024
F32 = jnp.float32
BF16 = jnp.bfloat16


def matmul(a, b):
    return jnp.dot(a, b, preferred_element_type=F32)


class Chain:
    def __init__(self):
        self.token = None

    def __call__(self, kernel, inputs, in_specs, out_shape, out_specs, name, work, after=(), grid=None, scratch=(), aliases=None):
        deps = list(after) + ([] if self.token is None else [self.token])
        n_in, n_out, n_dep = len(inputs), len(out_shape), len(deps)
        anywhere = pl.BlockSpec(memory_space=pl.ANY)

        def body(*refs):
            outs = n_in + n_dep
            kernel(*refs[:n_in], *refs[outs : outs + n_out], *refs[outs + n_out + 1 :])

        params = {} if grid is None else {"grid": grid}
        *results, self.token = pl.pallas_call(
            body,
            in_specs=list(in_specs) + [anywhere] * n_dep,
            out_specs=list(out_specs) + [anywhere],
            out_shape=list(out_shape) + [jax.ShapeDtypeStruct((8, LANES), F32)],
            scratch_shapes=list(scratch),
            input_output_aliases=aliases or {},
            compiler_params=pltpu.CompilerParams(vmem_limit_bytes=VMEM_BYTES),
            cost_estimate=pl.CostEstimate(flops=work[0], bytes_accessed=work[1], transcendentals=0),
            name=name,
            **params,
        )(*inputs, *deps)
        return results[0] if len(results) == 1 else results

    def gate(self, values, after):
        anywhere = pl.BlockSpec(memory_space=pl.ANY)
        return self(
            lambda *refs: None,
            values,
            [anywhere] * len(values),
            [jax.ShapeDtypeStruct(v.shape, v.dtype) for v in values],
            [anywhere] * len(values),
            "gate",
            (0, 0),
            after=after,
            aliases={i: i for i in range(len(values))},
        )

    def add(self, a, b):
        def kernel(a_ref, b_ref, out_ref):
            out_ref[...] = a_ref[...] + b_ref[...]

        vmem = pl.BlockSpec(memory_space=pltpu.VMEM)
        return self(kernel, [a, b], [vmem] * 2, [jax.ShapeDtypeStruct(a.shape, a.dtype)], [vmem], "add", (a.size, 12 * a.size))

    def choose(self, index, values):
        def kernel(index_ref, *refs):
            *sources, out, sem = refs
            for i, ref in enumerate(sources):

                @pl.when(index_ref[0] == i)
                def _(ref=ref):
                    copy = pltpu.make_async_copy(ref, out, sem)
                    copy.start()
                    copy.wait()

        anywhere = pl.BlockSpec(memory_space=pl.ANY)
        value = values[0]
        return self(
            kernel,
            [index, *values],
            [pl.BlockSpec(memory_space=pltpu.SMEM)] + [anywhere] * len(values),
            [jax.ShapeDtypeStruct(value.shape, value.dtype)],
            [anywhere],
            "choose",
            (0, 4 * value.size),
            scratch=[pltpu.SemaphoreType.DMA],
        )


def transpose8(x):
    at = lax.broadcasted_iota(jnp.int32, x[0].shape, 1)
    for d in (4, 2, 1):
        low = (at & d) == 0
        y = list(x)
        for i in range(8):
            if i & d == 0:
                a, b = x[i], x[i + d]
                y[i] = jnp.where(low, a, pltpu.roll(b, d, 1))
                y[i + d] = jnp.where(low, pltpu.roll(a, 8 - d, 1), b)
        x = y
    return x


def sum8(x):
    at = lax.broadcasted_iota(jnp.int32, x[0].shape, 1)
    for d in (4, 2, 1):
        low = (at & d) == 0
        y = []
        for a, b in zip(x[:d], x[d : 2 * d]):
            gone = jnp.where(low, b, a)
            back = pltpu.roll(gone, d, 1)
            if d != 4:
                back = jnp.where(low, pltpu.roll(gone, 8 - d, 1), back)
            y.append(jnp.where(low, a, b) + back)
        x = y
    return x[0]


def extract_kernel(groups, stride, spans, a_ref, sol_ref, part_ref, *rest):
    cols, wide = rest[: len(spans)], rest[-1]
    rows = part_ref.shape[1]
    if len(rest) > len(spans) + 1:
        rest[len(spans)][...] = a_ref[...]
    wide[...] = a_ref[...].astype(F32)
    i = pl.program_id(0)
    for col_ref, (start, stop) in zip(cols, spans):

        @pl.when((i >= start) & (i < stop))
        def _(col_ref=col_ref):
            for g in range(0, groups, stride):
                piece = wide[pl.ds(g, rows, stride=groups), :]
                col_ref[:, pl.ds(g // stride * LANES, LANES)] = piece.astype(BF16)

    if groups % 16 == 0:
        sol = sol_ref[...].astype(F32)
        totals = []
        for block in range(rows // 8):
            sums = []
            for r in range(8):
                base = (block * 8 + r) * groups
                sums.append(
                    sum(wide[pl.ds(base + 8 * h, 8), :] * sol[8 * h : 8 * h + 8] for h in range(groups // 8))[None]
                )
            totals.append(sum8(sums)[0])
        total = jnp.concatenate(totals, axis=0)
    else:
        total = jnp.zeros((rows, LANES), F32)
        for g in range(groups):
            total = total + wide[pl.ds(g, rows, stride=groups), :] * sol_ref[g : g + 1, :].astype(F32)
    ones = jnp.ones((8, LANES), F32)
    sums = lax.dot_general(
        ones, total, (((1,), (1,)), ((), ())), precision=lax.Precision.HIGHEST, preferred_element_type=F32
    )
    part_ref[...] = sums[0:1, :]


def extract(chain, flat, sol, sizes, first, groups, stride, width, with_band):
    sub = min(min(sizes), 256)
    size = sub * groups
    at = first // sub
    rows = sum(sizes)
    spans, out_specs, out_shape = [], [pl.BlockSpec((1, sub), lambda i: (0, i))], [jax.ShapeDtypeStruct((1, rows), F32)]
    start = 0
    for n in sizes:
        stop = start + n // sub
        spans.append((start, stop))
        out_specs.append(pl.BlockSpec((sub, width), lambda i, a=start, b=stop: (jnp.clip(i - a, 0, b - a - 1), 0)))
        out_shape.append(jax.ShapeDtypeStruct((n, width), BF16))
        start = stop
    if with_band:
        out_specs.append(pl.BlockSpec((size, LANES), lambda i: (i, 0)))
        out_shape.append(jax.ShapeDtypeStruct((rows * groups, LANES), BF16))
    return chain(
        lambda *refs: extract_kernel(groups, stride, spans, *refs),
        [flat, sol],
        [
            pl.BlockSpec((size, LANES), lambda i: (at + i, 0)),
            pl.BlockSpec((groups, LANES), lambda i: (0, 0)),
        ],
        out_shape,
        out_specs,
        "extract",
        (4 * rows * groups * LANES, rows * groups * LANES * 2),
        grid=(rows // sub,),
        scratch=[pltpu.VMEM((size, LANES), F32)],
    )


def factor_kernel(groups, n_x, where_ref, *refs):
    core, lane, x = where_ref[0], where_ref[1], where_ref[2]
    given, (mine_ref, other_ref, up_ref, low_ref, v_ref, raws, bands, blocks, sems, *rest) = refs[: 2 * n_x], refs[2 * n_x :]
    width = up_ref.shape[1]

    def both(copies):
        for copy in copies:
            copy.start()
        for copy in copies:
            copy.wait()

    for i in range(n_x):

        @pl.when(x == i)
        def _(i=i):
            both([pltpu.make_async_copy(given[2 * i + k], raws.at[k], sems.at[k]) for k in range(2)])

    for i, (ref_01, ref_10) in enumerate([(other_ref, mine_ref), (mine_ref, other_ref)]):

        @pl.when(lane == i)
        def _(ref_01=ref_01, ref_10=ref_10):
            both([
                pltpu.make_async_copy(ref_01.at[0], blocks.at[0], sems.at[2]),
                pltpu.make_async_copy(ref_10.at[1], blocks.at[1], sems.at[3]),
            ])

    for slot in range(2):
        if groups % 16 == 0:

            def one(block, carry, slot=slot):
                here = pl.ds(pl.multiple_of(block * 16 * groups, 16 * groups), 16 * groups)
                raw = raws[slot ^ core, here, :].astype(F32).reshape(2, 8, groups, LANES)
                rows = pl.ds(pl.multiple_of(block * 16, 16), 16)
                for h in range(groups // 8):
                    turned = transpose8([raw[:, r, 8 * h : 8 * h + 8] for r in range(8)])
                    for g in range(8):
                        at = pl.ds((8 * h + g) * LANES, LANES)
                        bands[slot, rows, at] = turned[g].reshape(16, LANES).astype(BF16)
                return carry

            lax.fori_loop(0, width // 16, one, 0, unroll=2)
        else:
            wide = rest[0]
            wide[...] = raws[slot ^ core].astype(F32)
            for g in range(groups):
                at = pl.ds(g * LANES, LANES)
                bands[slot, :, at] = wide[pl.ds(g, width, stride=groups), :].astype(BF16)
    row = lax.broadcasted_iota(jnp.int32, (width, width), 0)
    col = lax.broadcasted_iota(jnp.int32, (width, width), 1)
    zero = jnp.zeros((width, width), BF16)
    upper = [jnp.where(row <= col, up_ref[s], zero) for s in range(2)]
    lower = [jnp.where(row >= col, low_ref[s], zero) for s in range(2)]
    top_01 = matmul(lower[0], blocks[0]).astype(BF16)
    left_10 = matmul(blocks[1], upper[0]).astype(BF16)
    piece = min(groups * LANES, 1024)
    for n in range(groups * LANES // piece):
        at = slice(n * piece, (n + 1) * piece)
        top_0 = matmul(lower[0], bands[0, :, at]).astype(BF16)
        rest_1 = (bands[1, :, at].astype(F32) - matmul(left_10, top_0)).astype(BF16)
        top_1 = matmul(lower[1], rest_1).astype(BF16)
        v_1 = matmul(upper[1], top_1).astype(BF16)
        mixed = (top_0.astype(F32) - matmul(top_01, v_1)).astype(BF16)
        v_0 = matmul(upper[0], mixed).astype(BF16)
        v_ref[pl.ds(pl.multiple_of(lane * width, width), width), at] = v_0
        v_ref[pl.ds(pl.multiple_of((1 - lane) * width, width), width), at] = v_1


def factors(chain, where, bands, blocks, upper, lower, groups):
    width = upper.shape[1]
    cols = groups * LANES
    n_x = len(bands) // 2
    vmem = pl.BlockSpec(memory_space=pltpu.VMEM)
    anywhere = pl.BlockSpec(memory_space=pl.ANY)
    scratch = [
        pltpu.VMEM((2, width * groups, LANES), BF16),
        pltpu.VMEM((2, width, cols), BF16),
        pltpu.VMEM((2, width, width), BF16),
        pltpu.SemaphoreType.DMA((4,)),
    ]
    if groups % 16:
        scratch.append(pltpu.VMEM((width * groups, LANES), F32))
    return chain(
        lambda *refs: factor_kernel(groups, n_x, *refs),
        [where, *bands, *blocks, upper, lower],
        [pl.BlockSpec(memory_space=pltpu.SMEM)] + [anywhere] * (2 * n_x + 2) + [vmem] * 2,
        [jax.ShapeDtypeStruct((2 * width, cols), BF16)],
        [vmem],
        "factors",
        (12 * width * width * cols, 12 * width * cols),
        scratch=scratch,
    )


def update_kernel(groups, chunks, steps, a_ref, v_ref, *rest):
    out_ref, both, *wide = rest[-3 if groups % 16 else -2 :]
    rows, width = both.shape[0], both.shape[1] // 2
    i = pl.program_id(0)
    for c in range(chunks):

        @pl.when(i // steps == c)
        def _(c=c):
            both[:, :width] = rest[2 * c][...]
            both[:, width:] = rest[2 * c + 1][...]

    if groups % 16 == 0:
        part = min(rows, 128)
        for p in range(rows // part):
            value = matmul(both[p * part : (p + 1) * part, :], v_ref[...])
            for block in range(part // 8):
                cut = value[block * 8 : block * 8 + 8, :]
                halves = [
                    transpose8([cut[:, (8 * h + g) * LANES : (8 * h + g + 1) * LANES][None] for g in range(8)])
                    for h in range(groups // 8)
                ]
                for r in range(8):
                    here = pl.ds((p * part + block * 8 + r) * groups, groups)
                    change = jnp.concatenate([half[r][0] for half in halves], axis=0)
                    out_ref[here, :] = (a_ref[here, :].astype(F32) - change).astype(BF16)
        return
    value = matmul(both[...], v_ref[...])
    for g in range(groups):
        wide[0][pl.ds(g, rows, stride=groups), :] = value[:, g * LANES : (g + 1) * LANES]
    out_ref[...] = (a_ref[...].astype(F32) - wide[0][...]).astype(BF16)


def update(chain, flat, mine, other, v, out, first, groups):
    rows, width = mine[0].shape
    chunks = len(mine)
    sub = min(rows, 256)
    steps = rows // sub
    size = sub * groups
    base = first // sub
    cols = groups * LANES
    in_specs = [pl.BlockSpec((size, LANES), lambda i: (base + i, 0)), pl.BlockSpec(memory_space=pltpu.VMEM)]
    args = [flat, v]
    for c in range(chunks):
        args += [mine[c], other[c]]
        in_specs += [pl.BlockSpec((sub, width), lambda i, c=c: (jnp.clip(i - c * steps, 0, steps - 1), 0))] * 2
    aliases = {}
    if out is not None:
        aliases = {len(args): 0}
        in_specs.append(pl.BlockSpec(memory_space=pl.ANY))
        args.append(out)
    scratch = [pltpu.VMEM((sub, 2 * width), BF16)]
    if groups % 16:
        scratch.append(pltpu.VMEM((size, LANES), F32))
    return chain(
        lambda *refs: update_kernel(groups, chunks, steps, *refs),
        args,
        in_specs,
        [jax.ShapeDtypeStruct(flat.shape, BF16)],
        [pl.BlockSpec((size, LANES), lambda i: (base + i, 0))],
        "update",
        (4 * chunks * rows * width * cols, chunks * (4 * rows * cols + 4 * rows * width)),
        grid=(chunks * steps,),
        scratch=scratch,
        aliases=aliases,
    )


def solve_kernel(lane_ref, res_ref, inv_ref, *rest):
    cols, out_ref = rest[:-1], rest[-1]
    lane = lane_ref[0]
    count, width = out_ref.shape
    nt = (((1,), (1,)), ((), ()))
    out_ref[...] = jnp.zeros((count, width), F32)
    for k in range(count):
        pending = jnp.zeros((8, width), F32)
        for j, col in enumerate(cols):
            if j >= max(k, 2) or k == 0:
                continue
            if j < 2:
                at = (j + lane) % 2
                known = jnp.where(at < k, out_ref[pl.ds(at, 1), :], 0.0)
            else:
                known = out_ref[j : j + 1, :]
            pending = pending + lax.dot_general(
                jnp.broadcast_to(known, (8, width)).astype(BF16), col[k], nt, preferred_element_type=F32
            )
        left = res_ref[k : k + 1, :] - pending[0:1, :]
        high = left.astype(BF16)
        rest_1 = left - high.astype(F32)
        mid = rest_1.astype(BF16)
        low = (rest_1 - mid.astype(F32)).astype(BF16)
        total = jnp.zeros((8, width), F32)
        for piece in (low, mid, high):
            wide = jnp.broadcast_to(piece.astype(F32), (8, width)).astype(BF16)
            total = total + lax.dot_general(wide, inv_ref[k], nt, preferred_element_type=F32)
        out_ref[k : k + 1, :] = total[0:1, :]


def solve_all(chain, lane, res, inv, cols):
    vmem = pl.BlockSpec(memory_space=pltpu.VMEM)
    return chain(
        solve_kernel,
        [lane, res, inv, *cols],
        [pl.BlockSpec(memory_space=pltpu.SMEM)] + [vmem] * (2 + len(cols)),
        [jax.ShapeDtypeStruct(res.shape, F32)],
        [vmem],
        "solve",
        (2 * inv.size * (len(cols) + 3), 2 * inv.size * (len(cols) + 1)),
    )


def shards(matrix, upper_inv, lower_inv, solution, right_side, diagonal_block_inverses):
    slots, _, width, col_slots, _, _ = matrix.shape
    n_prow = lax.axis_size("prow")
    n_pcol = lax.axis_size("pcol")
    ny = n_prow // 2
    nz = n_pcol // ny
    prow = lax.axis_index("prow")
    pcol = lax.axis_index("pcol")
    z, y = pcol // ny, pcol % ny
    core, lane = prow % 2, y % 2
    lane_tiles = width // LANES
    groups = lane_tiles * col_slots
    rows = slots * width
    flat = matrix.reshape(rows, col_slots, lane_tiles, LANES).transpose(0, 2, 1, 3).reshape(rows * groups, LANES)
    sol = solution.reshape(col_slots, lane_tiles, LANES).transpose(1, 0, 2).reshape(groups, LANES)

    chain = Chain()

    def spread(value, axis, size):
        values = [value]
        for s in range(2, size, 2):
            pairs = [(s - 2, s), (s - 1, s + 1), (s, s - 2), (s + 1, s - 1)]
            values.append(lax.ppermute(values[-1], axis, pairs))
        return values

    def swap(value, axis, size, bit=1):
        return lax.ppermute(value, axis, [(i, i ^ bit) for i in range(size)])

    def along_z(pairs):
        return [(a * ny + k, b * ny + k) for a, b in pairs for k in range(2)]

    stages = [[[(0, nz // 2)]]]
    held, step = [nz // 2], nz // 4
    while step:
        stages.append([[(m, m - step) for m in held], [(m, m + step) for m in held]])
        held = [b for moves in stages[-1] for _, b in moves]
        step //= 2

    def picked(got, moves, value):
        mask = z == moves[0][1]
        for _, b in moves[1:]:
            mask = mask | (z == b)
        return jnp.where(mask, got, value)

    def first_stage(local):
        return lax.ppermute(local, "pcol", along_z(stages[0][0]))

    def second_stage(arrived):
        return [lax.ppermute(arrived, "pcol", along_z(moves)) for moves in stages[1]]

    source = jnp.zeros((), jnp.int32)
    for i, moves in enumerate(stages[0] + stages[1]):
        for _, b in moves:
            source = jnp.where(z == b, i + 1, source)
    source = source.astype(jnp.int32).reshape(1)

    def settle(local, arrived, outward):
        value = chain.choose(source, [local, arrived, *outward])
        for stage in stages[2:]:
            gots = [lax.ppermute(value, "pcol", along_z(moves)) for moves in stage]
            for got, moves in zip(gots, stage):
                value = picked(got, moves, value)
        for s in range(2, ny, 2):
            pairs = [(a * ny + s - 2 + k, a * ny + s + k) for a in range(nz) for k in range(2)]
            got = lax.ppermute(value, "pcol", pairs)
            value = jnp.where(y // 2 == s // 2, got, value)
        return value

    count = n_prow * diagonal_block_inverses.shape[0]
    assert diagonal_block_inverses.shape[0] == 1
    home = count - 2
    inv = diagonal_block_inverses.reshape(width, width)
    where = jnp.stack([core, lane, prow // 2]).astype(jnp.int32)

    sizes = [width] + [2 * width] * ((slots - 2) // 2)
    sizes += [width // 2] * ((slots * width - sum(sizes)) // (width // 2))
    starts = [sum(sizes[:c]) for c in range(len(sizes))]
    chunks = len(sizes)
    column, first, outward, mine, other, box = {}, {}, {}, {}, {}, {"out": None}
    part_0, column[0], band = extract(chain, flat, sol, sizes[:1], 0, groups, col_slots, width, True)
    first[0] = first_stage(column[0])
    bands = spread(band, "prow", n_prow)
    part_1, *rest = extract(chain, flat, sol, sizes[1:], width, groups, col_slots, width, False)
    column.update({c + 1: col for c, col in enumerate(rest)})
    partial = jnp.concatenate([part_0, part_1], axis=1).reshape(slots, width)
    residual = right_side.reshape(slots, width) - jnp.sum(lax.all_gather(partial, "pcol"), axis=0)

    def take(c):
        mine[c] = settle(column[c], first[c], outward[c])
        other[c] = swap(mine[c], "pcol", n_pcol)

    def swap_bands():
        box["bands"] = [v for b in bands for v in (b, swap(b, "prow", n_prow))]

    def gather_blocks():
        box["blocks"] = [lax.all_gather(mine[0], "prow"), lax.all_gather(other[0], "prow")]

    def gather_rest():
        own, below, _ = chain.gate([column[0], inv, box["blocks"][0]], [])
        cols = [lax.ppermute(own, "pcol", [(j, home)]) for j in range(2, home)] + [own]
        box["cols"] = box["blocks"] + [lax.all_gather(col, "prow") for col in cols]
        box["inv"] = lax.all_gather(below, "prow")
        box["res"] = lax.all_gather(residual[0:1], "prow", tiled=True)

    def make_factors():
        box["v"] = factors(chain, where, box["bands"], box["blocks"], upper_inv, lower_inv, groups)

    def solve():
        state = solve_all(chain, where[1:2], box["res"], box["inv"], box["cols"])
        box["state"] = lax.all_gather(state, "pcol")[home]

    def updates(*which):
        def run():
            for c in which:
                box["out"] = update(chain, flat, [mine[c]], [other[c]], box["v"], box["out"], starts[c], groups)

        return run

    plan = {0: [swap_bands], 1: [gather_blocks]}
    if chunks == 6:
        plan[2] = [gather_rest, make_factors, updates(0)]
        plan[3] = [updates(1)]
        plan[4] = [updates(2), solve]
        plan[5] = [updates(3)]
    else:
        plan[chunks - 1] = plan.pop(chunks - 1, []) + [gather_rest, make_factors, solve, updates(*range(chunks - 2))]

    for k in range(chunks):
        ahead = [column[k + 1]] if k + 1 < chunks else []
        got = chain.gate([first[k], *ahead], [])
        first[k] = got[0] if ahead else got
        if ahead:
            column[k + 1] = got[1]
            first[k + 1] = first_stage(column[k + 1])
        outward[k] = second_stage(first[k])
        if k:
            take(k - 1)
        for task in plan.get(k, []):
            task()
    updates(chunks - 2)()
    take(chunks - 1)
    updates(chunks - 1)()
    out, state = box["out"], box["state"]
    updated = out.reshape(rows, lane_tiles, col_slots, LANES).transpose(0, 2, 1, 3).reshape(matrix.shape)
    return (updated, residual.reshape(right_side.shape), state)


def solution(mesh):
    return jax.shard_map(
        shards,
        mesh=mesh,
        in_specs=(
            P(None, "prow", None, None, "pcol", None),
            P(),
            P(),
            P(None, "pcol", None),
            P(None, "prow", None),
            P(None, "prow", None, None),
        ),
        out_specs=(P(None, "prow", None, None, "pcol", None), P(None, "prow", None), P()),
        check_vma=False,
    )
```

```python
import jax
import jax.numpy as jnp
from jax import lax
from jax.experimental import pallas as pl
from jax.experimental.pallas import tpu as pltpu
from jax.sharding import PartitionSpec as P

LANES = 128
VMEM_BYTES = 50 * 1024 * 1024
F32 = jnp.float32
BF16 = jnp.bfloat16


def matmul(a, b):
    return jnp.dot(a, b, preferred_element_type=F32)


class Chain:
    def __init__(self):
        self.token = None

    def __call__(self, kernel, inputs, in_specs, out_shape, out_specs, name, work, after=(), grid=None, scratch=(), aliases=None):
        deps = list(after) + ([] if self.token is None else [self.token])
        n_in, n_out, n_dep = len(inputs), len(out_shape), len(deps)
        anywhere = pl.BlockSpec(memory_space=pl.ANY)

        def body(*refs):
            outs = n_in + n_dep
            kernel(*refs[:n_in], *refs[outs : outs + n_out], *refs[outs + n_out + 1 :])

        params = {} if grid is None else {"grid": grid}
        *results, self.token = pl.pallas_call(
            body,
            in_specs=list(in_specs) + [anywhere] * n_dep,
            out_specs=list(out_specs) + [anywhere],
            out_shape=list(out_shape) + [jax.ShapeDtypeStruct((8, LANES), F32)],
            scratch_shapes=list(scratch),
            input_output_aliases=aliases or {},
            compiler_params=pltpu.CompilerParams(vmem_limit_bytes=VMEM_BYTES),
            cost_estimate=pl.CostEstimate(flops=work[0], bytes_accessed=work[1], transcendentals=0),
            name=name,
            **params,
        )(*inputs, *deps)
        return results[0] if len(results) == 1 else results

    def gate(self, values, after):
        anywhere = pl.BlockSpec(memory_space=pl.ANY)
        return self(
            lambda *refs: None,
            values,
            [anywhere] * len(values),
            [jax.ShapeDtypeStruct(v.shape, v.dtype) for v in values],
            [anywhere] * len(values),
            "gate",
            (0, 0),
            after=after,
            aliases={i: i for i in range(len(values))},
        )

    def add(self, a, b):
        def kernel(a_ref, b_ref, out_ref):
            out_ref[...] = a_ref[...] + b_ref[...]

        vmem = pl.BlockSpec(memory_space=pltpu.VMEM)
        return self(kernel, [a, b], [vmem] * 2, [jax.ShapeDtypeStruct(a.shape, a.dtype)], [vmem], "add", (a.size, 12 * a.size))

    def choose(self, index, values):
        def kernel(index_ref, *refs):
            *sources, out, sem = refs
            for i, ref in enumerate(sources):

                @pl.when(index_ref[0] == i)
                def _(ref=ref):
                    copy = pltpu.make_async_copy(ref, out, sem)
                    copy.start()
                    copy.wait()

        anywhere = pl.BlockSpec(memory_space=pl.ANY)
        value = values[0]
        return self(
            kernel,
            [index, *values],
            [pl.BlockSpec(memory_space=pltpu.SMEM)] + [anywhere] * len(values),
            [jax.ShapeDtypeStruct(value.shape, value.dtype)],
            [pl.BlockSpec(memory_space=pltpu.VMEM)],
            "choose",
            (0, 4 * value.size),
            scratch=[pltpu.SemaphoreType.DMA],
        )


def transpose8(x):
    at = lax.broadcasted_iota(jnp.int32, x[0].shape, 1)
    for d in (4, 2, 1):
        low = (at & d) == 0
        y = list(x)
        for i in range(8):
            if i & d == 0:
                a, b = x[i], x[i + d]
                y[i] = jnp.where(low, a, pltpu.roll(b, d, 1))
                y[i + d] = jnp.where(low, pltpu.roll(a, 8 - d, 1), b)
        x = y
    return x


def sum8(x):
    at = lax.broadcasted_iota(jnp.int32, x[0].shape, 1)
    for d in (4, 2, 1):
        low = (at & d) == 0
        y = []
        for a, b in zip(x[:d], x[d : 2 * d]):
            gone = jnp.where(low, b, a)
            back = pltpu.roll(gone, d, 1)
            if d != 4:
                back = jnp.where(low, pltpu.roll(gone, 8 - d, 1), back)
            y.append(jnp.where(low, a, b) + back)
        x = y
    return x[0]


def extract_kernel(groups, stride, spans, a_ref, sol_ref, part_ref, *rest):
    cols, wide = rest[: len(spans)], rest[-1]
    rows = part_ref.shape[1]
    if len(rest) > len(spans) + 1:
        rest[len(spans)][...] = a_ref[...]
    wide[...] = a_ref[...].astype(F32)
    i = pl.program_id(0)
    for col_ref, (start, stop) in zip(cols, spans):

        @pl.when((i >= start) & (i < stop))
        def _(col_ref=col_ref):
            for g in range(0, groups, stride):
                piece = wide[pl.ds(g, rows, stride=groups), :]
                col_ref[:, pl.ds(g // stride * LANES, LANES)] = piece.astype(BF16)

    if groups % 16 == 0:
        sol = sol_ref[...].astype(F32)
        totals = []
        for block in range(rows // 8):
            sums = []
            for r in range(8):
                base = (block * 8 + r) * groups
                sums.append(
                    sum(wide[pl.ds(base + 8 * h, 8), :] * sol[8 * h : 8 * h + 8] for h in range(groups // 8))[None]
                )
            totals.append(sum8(sums)[0])
        total = jnp.concatenate(totals, axis=0)
    else:
        total = jnp.zeros((rows, LANES), F32)
        for g in range(groups):
            total = total + wide[pl.ds(g, rows, stride=groups), :] * sol_ref[g : g + 1, :].astype(F32)
    ones = jnp.ones((8, LANES), F32)
    sums = lax.dot_general(
        ones, total, (((1,), (1,)), ((), ())), precision=lax.Precision.HIGHEST, preferred_element_type=F32
    )
    part_ref[...] = sums[0:1, :]


def extract(chain, flat, sol, sizes, first, groups, stride, width, with_band):
    sub = min(min(sizes), 256)
    size = sub * groups
    at = first // sub
    rows = sum(sizes)
    spans, out_specs, out_shape = [], [pl.BlockSpec((1, sub), lambda i: (0, i))], [jax.ShapeDtypeStruct((1, rows), F32)]
    start = 0
    for n in sizes:
        stop = start + n // sub
        spans.append((start, stop))
        out_specs.append(pl.BlockSpec((sub, width), lambda i, a=start, b=stop: (jnp.clip(i - a, 0, b - a - 1), 0)))
        out_shape.append(jax.ShapeDtypeStruct((n, width), BF16))
        start = stop
    if with_band:
        out_specs.append(pl.BlockSpec((size, LANES), lambda i: (i, 0)))
        out_shape.append(jax.ShapeDtypeStruct((rows * groups, LANES), BF16))
    return chain(
        lambda *refs: extract_kernel(groups, stride, spans, *refs),
        [flat, sol],
        [
            pl.BlockSpec((size, LANES), lambda i: (at + i, 0)),
            pl.BlockSpec((groups, LANES), lambda i: (0, 0)),
        ],
        out_shape,
        out_specs,
        "extract",
        (4 * rows * groups * LANES, rows * groups * LANES * 2),
        grid=(rows // sub,),
        scratch=[pltpu.VMEM((size, LANES), F32)],
    )


def factor_kernel(groups, n_x, where_ref, *refs):
    core, lane, x = where_ref[0], where_ref[1], where_ref[2]
    given, (up_ref, low_ref, v_ref, raws, bands, blocks, sems, *rest) = refs[: 4 * n_x], refs[4 * n_x :]
    width = up_ref.shape[1]
    for i in range(n_x):

        @pl.when(x == i)
        def _(i=i):
            pairs = [(raws, given[2 * i], given[2 * i + 1]), (blocks, given[2 * n_x + 2 * i], given[2 * n_x + 2 * i + 1])]
            copies = []
            for kind, (target, mine, other) in enumerate(pairs):
                copies.append(pltpu.make_async_copy(mine, target.at[core], sems.at[kind, 0]))
                copies.append(pltpu.make_async_copy(other, target.at[1 - core], sems.at[kind, 1]))
            for copy in copies:
                copy.start()
            for copy in copies:
                copy.wait()

    for slot in range(2):
        if groups % 16 == 0:

            def one(block, carry, slot=slot):
                here = pl.ds(pl.multiple_of(block * 16 * groups, 16 * groups), 16 * groups)
                raw = raws[slot, here, :].astype(F32).reshape(2, 8, groups, LANES)
                rows = pl.ds(pl.multiple_of(block * 16, 16), 16)
                for h in range(groups // 8):
                    turned = transpose8([raw[:, r, 8 * h : 8 * h + 8] for r in range(8)])
                    for g in range(8):
                        at = pl.ds((8 * h + g) * LANES, LANES)
                        bands[slot, rows, at] = turned[g].reshape(16, LANES).astype(BF16)
                return carry

            lax.fori_loop(0, width // 16, one, 0, unroll=2)
        else:
            wide = rest[0]
            wide[...] = raws[slot].astype(F32)
            for g in range(groups):
                at = pl.ds(g * LANES, LANES)
                bands[slot, :, at] = wide[pl.ds(g, width, stride=groups), :].astype(BF16)
    row = lax.broadcasted_iota(jnp.int32, (width, width), 0)
    col = lax.broadcasted_iota(jnp.int32, (width, width), 1)
    zero = jnp.zeros((width, width), BF16)
    upper = [jnp.where(row <= col, up_ref[s], zero) for s in range(2)]
    lower = [jnp.where(row >= col, low_ref[s], zero) for s in range(2)]
    top_01 = matmul(lower[0], blocks[0]).astype(BF16)
    left_10 = matmul(blocks[1], upper[0]).astype(BF16)
    piece = min(groups * LANES, 1024)
    for n in range(groups * LANES // piece):
        at = slice(n * piece, (n + 1) * piece)
        top_0 = matmul(lower[0], bands[0, :, at]).astype(BF16)
        rest_1 = (bands[1, :, at].astype(F32) - matmul(left_10, top_0)).astype(BF16)
        top_1 = matmul(lower[1], rest_1).astype(BF16)
        v_1 = matmul(upper[1], top_1).astype(BF16)
        mixed = (top_0.astype(F32) - matmul(top_01, v_1)).astype(BF16)
        v_0 = matmul(upper[0], mixed).astype(BF16)
        v_ref[pl.ds(pl.multiple_of(lane * width, width), width), at] = v_0
        v_ref[pl.ds(pl.multiple_of((1 - lane) * width, width), width), at] = v_1


def factors(chain, where, bands, blocks, upper, lower, groups):
    width = upper.shape[1]
    cols = groups * LANES
    n_x = len(bands) // 2
    vmem = pl.BlockSpec(memory_space=pltpu.VMEM)
    anywhere = pl.BlockSpec(memory_space=pl.ANY)
    scratch = [
        pltpu.VMEM((2, width * groups, LANES), BF16),
        pltpu.VMEM((2, width, cols), BF16),
        pltpu.VMEM((2, width, width), BF16),
        pltpu.SemaphoreType.DMA((2, 2)),
    ]
    if groups % 16:
        scratch.append(pltpu.VMEM((width * groups, LANES), F32))
    return chain(
        lambda *refs: factor_kernel(groups, n_x, *refs),
        [where, *bands, *blocks, upper, lower],
        [pl.BlockSpec(memory_space=pltpu.SMEM)] + [anywhere] * (4 * n_x) + [vmem] * 2,
        [jax.ShapeDtypeStruct((2 * width, cols), BF16)],
        [vmem],
        "factors",
        (12 * width * width * cols, 12 * width * cols),
        scratch=scratch,
    )


def update_kernel(groups, spans, a_ref, v_ref, *rest):
    out_ref, both, *wide = rest[-3 if groups % 16 else -2 :]
    rows, width = both.shape[0], both.shape[1] // 2
    i = pl.program_id(0)
    for c, (start, stop) in enumerate(spans):

        @pl.when((i >= start) & (i < stop))
        def _(c=c):
            both[:, :width] = rest[2 * c][...]
            both[:, width:] = rest[2 * c + 1][...]

    if groups % 16 == 0:
        part = min(rows, 128)
        for p in range(rows // part):
            value = matmul(both[p * part : (p + 1) * part, :], v_ref[...])
            for block in range(part // 8):
                cut = value[block * 8 : block * 8 + 8, :]
                halves = [
                    transpose8([cut[:, (8 * h + g) * LANES : (8 * h + g + 1) * LANES][None] for g in range(8)])
                    for h in range(groups // 8)
                ]
                for r in range(8):
                    here = pl.ds((p * part + block * 8 + r) * groups, groups)
                    change = jnp.concatenate([half[r][0] for half in halves], axis=0)
                    out_ref[here, :] = (a_ref[here, :].astype(F32) - change).astype(BF16)
        return
    value = matmul(both[...], v_ref[...])
    for g in range(groups):
        wide[0][pl.ds(g, rows, stride=groups), :] = value[:, g * LANES : (g + 1) * LANES]
    out_ref[...] = (a_ref[...].astype(F32) - wide[0][...]).astype(BF16)


def update(chain, flat, mine, other, v, out, first, groups):
    rows, width = sum(m.shape[0] for m in mine), mine[0].shape[1]
    sub = min(256, *(m.shape[0] for m in mine))
    size = sub * groups
    base = first // sub
    cols = groups * LANES
    in_specs = [pl.BlockSpec((size, LANES), lambda i: (base + i, 0)), pl.BlockSpec(memory_space=pltpu.VMEM)]
    args, spans, start = [flat, v], [], 0
    for m, o in zip(mine, other):
        stop = start + m.shape[0] // sub
        args += [m, o]
        in_specs += [pl.BlockSpec((sub, width), lambda i, a=start, b=stop: (jnp.clip(i - a, 0, b - a - 1), 0))] * 2
        spans.append((start, stop))
        start = stop
    aliases = {}
    if out is not None:
        aliases = {len(args): 0}
        in_specs.append(pl.BlockSpec(memory_space=pl.ANY))
        args.append(out)
    scratch = [pltpu.VMEM((sub, 2 * width), BF16)]
    if groups % 16:
        scratch.append(pltpu.VMEM((size, LANES), F32))
    return chain(
        lambda *refs: update_kernel(groups, spans, *refs),
        args,
        in_specs,
        [jax.ShapeDtypeStruct(flat.shape, BF16)],
        [pl.BlockSpec((size, LANES), lambda i: (base + i, 0))],
        "update",
        (4 * rows * width * cols, 4 * rows * cols + 4 * rows * width),
        grid=(rows // sub,),
        scratch=scratch,
        aliases=aliases,
    )


def solve_kernel(place_ref, state_ref, res_ref, inv_ref, *rest):
    cols, out_ref = rest[:-1], rest[-1]
    place, lane = place_ref[0], place_ref[1]
    width = inv_ref.shape[0]
    nt = (((1,), (1,)), ((), ()))
    pending = jnp.zeros((8, width), F32)
    for j, col in enumerate(cols):
        at = (j + lane) % 2 if j < 2 else j
        known = jnp.where(at < place, state_ref[pl.ds(at, 1), :], 0.0)
        pending = pending + lax.dot_general(
            jnp.broadcast_to(known, (8, width)).astype(BF16), col[...], nt, preferred_element_type=F32
        )
    left = res_ref[...] - pending[0:1, :]
    high = left.astype(BF16)
    rest_1 = left - high.astype(F32)
    mid = rest_1.astype(BF16)
    low = (rest_1 - mid.astype(F32)).astype(BF16)
    total = jnp.zeros((8, width), F32)
    for piece in (low, mid, high):
        wide = jnp.broadcast_to(piece.astype(F32), (8, width)).astype(BF16)
        total = total + lax.dot_general(wide, inv_ref[...], nt, preferred_element_type=F32)
    row = lax.broadcasted_iota(jnp.int32, state_ref.shape, 0)
    out_ref[...] = jnp.where(row == place, jnp.broadcast_to(total[0:1, :], state_ref.shape), state_ref[...])


def solve_step(chain, place, state, res, inv, cols):
    vmem = pl.BlockSpec(memory_space=pltpu.VMEM)
    return chain(
        solve_kernel,
        [place, state, res, inv, *cols],
        [pl.BlockSpec(memory_space=pltpu.SMEM)] + [vmem] * (3 + len(cols)),
        [jax.ShapeDtypeStruct(state.shape, F32)],
        [vmem],
        "solve",
        (2 * inv.size * (len(cols) + 3), 2 * inv.size * (len(cols) + 1)),
    )


def shards(matrix, upper_inv, lower_inv, solution, right_side, diagonal_block_inverses):
    slots, _, width, col_slots, _, _ = matrix.shape
    n_prow = lax.axis_size("prow")
    n_pcol = lax.axis_size("pcol")
    ny = n_prow // 2
    nz = n_pcol // ny
    prow = lax.axis_index("prow")
    pcol = lax.axis_index("pcol")
    z, y = pcol // ny, pcol % ny
    core, lane = prow % 2, y % 2
    lane_tiles = width // LANES
    groups = lane_tiles * col_slots
    rows = slots * width
    flat = matrix.reshape(rows, col_slots, lane_tiles, LANES).transpose(0, 2, 1, 3).reshape(rows * groups, LANES)
    sol = solution.reshape(col_slots, lane_tiles, LANES).transpose(1, 0, 2).reshape(groups, LANES)

    chain = Chain()

    def spread(value, axis, size):
        values = [value]
        for s in range(2, size, 2):
            pairs = [(s - 2, s), (s - 1, s + 1), (s, s - 2), (s + 1, s - 1)]
            values.append(lax.ppermute(values[-1], axis, pairs))
        return values

    def swap(value, axis, size, bit=1):
        return lax.ppermute(value, axis, [(i, i ^ bit) for i in range(size)])

    def along_z(pairs):
        return [(a * ny + k, b * ny + k) for a, b in pairs for k in range(2)]

    stages = [[[(0, nz // 2)]]]
    held, step = [nz // 2], nz // 4
    while step:
        stages.append([[(m, m - step) for m in held], [(m, m + step) for m in held]])
        held = [b for moves in stages[-1] for _, b in moves]
        step //= 2

    def picked(got, moves, value):
        mask = z == moves[0][1]
        for _, b in moves[1:]:
            mask = mask | (z == b)
        return jnp.where(mask, got, value)

    def first_stage(local):
        return lax.ppermute(local, "pcol", along_z(stages[0][0]))

    def second_stage(arrived):
        return [lax.ppermute(arrived, "pcol", along_z(moves)) for moves in stages[1]]

    source = jnp.zeros((), jnp.int32)
    for i, moves in enumerate(stages[0] + stages[1]):
        for _, b in moves:
            source = jnp.where(z == b, i + 1, source)
    source = source.astype(jnp.int32).reshape(1)

    def settle(local, arrived, outward):
        value = chain.choose(source, [local, arrived, *outward])
        for stage in stages[2:]:
            gots = [lax.ppermute(value, "pcol", along_z(moves)) for moves in stage]
            for got, moves in zip(gots, stage):
                value = picked(got, moves, value)
        for s in range(2, ny, 2):
            pairs = [(a * ny + s - 2 + k, a * ny + s + k) for a in range(nz) for k in range(2)]
            got = lax.ppermute(value, "pcol", pairs)
            value = jnp.where(y // 2 == s // 2, got, value)
        return value

    count = n_prow * diagonal_block_inverses.shape[0]
    assert diagonal_block_inverses.shape[0] == 1
    home = count - 2
    inv = diagonal_block_inverses.reshape(width, width)
    place = jnp.stack([prow, lane]).astype(jnp.int32)
    where = jnp.stack([core, lane, prow // 2]).astype(jnp.int32)
    flag = jnp.where(core != lane, 0, 1).astype(jnp.int32).reshape(1)
    bits = [1 << b for b in range(n_pcol.bit_length() - 1)]

    sizes = [width] + [2 * width] * ((slots - 2) // 2)
    sizes += [width] * (slots - sum(sizes) // width)
    starts = [sum(sizes[:c]) for c in range(len(sizes) + 1)]
    chunks = len(sizes)
    column, first, outward, mine, other, box = {}, {}, {}, {}, {}, {"out": None}

    def extracts(a, b, with_band=False):
        part, *cols = extract(chain, flat, sol, sizes[a:b], starts[a], groups, col_slots, width, with_band)
        column.update(zip(range(a, b), cols))
        return part, cols[-1]

    parts = []
    part, band = extracts(0, 1, True)
    parts.append(part)
    first[0] = first_stage(column[0])
    box["bands"] = spread(band, "prow", n_prow)
    parts.append(extracts(1, 2)[0])

    def total_step(bit):
        def run():
            if bit == 1:
                box["total"] = jnp.concatenate(parts, axis=1).reshape(slots, width)
            box["total"] = chain.add(box["total"], swap(box["total"], "pcol", n_pcol, bit))
            if bit == bits[-1]:
                box["residual"] = right_side.reshape(slots, width) - box["total"]

        return run

    def solve(k):
        def run():
            if k == 0:
                needed = [mine[0], other[0]]
                for j in range(2, home):
                    needed.append(lax.ppermute(column[0], "pcol", [(j, home)]))
                box["needed"] = needed + [column[0]]
                state = jnp.zeros((count, width), F32)
            else:
                state = lax.ppermute(box["state"], "prow", [(i, i + 1) for i in range(n_prow - 1)])
            state = solve_step(chain, place, state, box["residual"][0:1], inv, box["needed"])
            if k == count - 1:
                state = jnp.where((prow == n_prow - 1) & (pcol == home), state, 0.0)
            box["state"] = state

        return run

    def share(axis, size, bit):
        def run():
            box["state"] = chain.add(box["state"], swap(box["state"], axis, size, bit))

        return run

    def blocks_out():
        box["blks"] = spread(chain.choose(flag, [mine[0], other[0]]), "prow", n_prow)
        box["bands"] = [v for b in box["bands"] for v in (b, swap(b, "prow", n_prow))]

    def blocks_swap():
        box["blks"] = [v for b in box["blks"] for v in (b, swap(b, "prow", n_prow))]

    def make_factors():
        box["v"] = factors(chain, where, box["bands"], box["blks"], upper_inv, lower_inv, groups)

    def updates(*which):
        def run():
            args = [mine[c] for c in which], [other[c] for c in which]
            box["out"] = update(chain, flat, *args, box["v"], box["out"], starts[which[0]], groups)

        return run

    def take(c):
        mine[c] = settle(column[c], first[c], outward[c])
        other[c] = swap(mine[c], "pcol", n_pcol)

    total = [total_step(b) for b in bits]
    line = [solve(k) for k in range(count)]
    line += [share("prow", n_prow, 1 << b) for b in range(n_prow.bit_length() - 1)]
    line += [share("pcol", n_pcol, b) for b in bits]
    def rest_extracted():
        if chunks > 2:
            parts.append(extracts(2, chunks)[0])

    if chunks == 5 and len(line) == 9:
        plan = {
            0: [rest_extracted, *total],
            1: [blocks_out, *line[:3], blocks_swap, *line[3:5]],
            2: [make_factors, line[5], updates(0, 1), line[6]],
            3: [updates(2), line[7]],
            4: [updates(3), line[8]],
        }
    else:
        plan = {0: [rest_extracted, *total], chunks - 1: [blocks_out, blocks_swap, make_factors, *line, updates(*range(chunks - 1))]}

    for k in range(chunks):
        ahead = [column[k + 1]] if k + 1 < chunks else []
        got = chain.gate([first[k], *ahead], [])
        first[k] = got[0] if ahead else got
        if ahead:
            column[k + 1] = got[1]
            first[k + 1] = first_stage(column[k + 1])
        outward[k] = second_stage(first[k])
        if k:
            take(k - 1)
        for task in plan.get(k, []):
            task()
    take(chunks - 1)
    updates(chunks - 1)()
    residual, out, state = box["residual"], box["out"], box["state"]
    updated = out.reshape(rows, lane_tiles, col_slots, LANES).transpose(0, 2, 1, 3).reshape(matrix.shape)
    return (updated, residual.reshape(right_side.shape), state)


def solution(mesh):
    return jax.shard_map(
        shards,
        mesh=mesh,
        in_specs=(
            P(None, "prow", None, None, "pcol", None),
            P(),
            P(),
            P(None, "pcol", None),
            P(None, "prow", None),
            P(None, "prow", None, None),
        ),
        out_specs=(P(None, "prow", None, None, "pcol", None), P(None, "prow", None), P()),
        check_vma=False,
    )
```

```python
import jax
import jax.numpy as jnp
from jax import lax
from jax.experimental import pallas as pl
from jax.experimental.pallas import tpu as pltpu
from jax.sharding import PartitionSpec as P

LANES = 128
VMEM_BYTES = 50 * 1024 * 1024
F32 = jnp.float32
BF16 = jnp.bfloat16


def matmul(a, b):
    return jnp.dot(a, b, preferred_element_type=F32)


class Chain:
    def __init__(self):
        self.token = None

    def __call__(self, kernel, inputs, in_specs, out_shape, out_specs, name, work, after=(), grid=None, scratch=(), aliases=None):
        deps = list(after) + ([] if self.token is None else [self.token])
        n_in, n_out, n_dep = len(inputs), len(out_shape), len(deps)
        anywhere = pl.BlockSpec(memory_space=pl.ANY)

        def body(*refs):
            outs = n_in + n_dep
            kernel(*refs[:n_in], *refs[outs : outs + n_out], *refs[outs + n_out + 1 :])

        params = {} if grid is None else {"grid": grid}
        *results, self.token = pl.pallas_call(
            body,
            in_specs=list(in_specs) + [anywhere] * n_dep,
            out_specs=list(out_specs) + [anywhere],
            out_shape=list(out_shape) + [jax.ShapeDtypeStruct((8, LANES), F32)],
            scratch_shapes=list(scratch),
            input_output_aliases=aliases or {},
            compiler_params=pltpu.CompilerParams(vmem_limit_bytes=VMEM_BYTES),
            cost_estimate=pl.CostEstimate(flops=0, bytes_accessed=0, transcendentals=0),
            name=name,
            **params,
        )(*inputs, *deps)
        return results[0] if len(results) == 1 else results

    def gate(self, values, after):
        anywhere = pl.BlockSpec(memory_space=pl.ANY)
        return self(
            lambda *refs: None,
            values,
            [anywhere] * len(values),
            [jax.ShapeDtypeStruct(v.shape, v.dtype) for v in values],
            [anywhere] * len(values),
            "gate",
            (0, 0),
            after=after,
            aliases={i: i for i in range(len(values))},
        )

    def add(self, a, b):
        def kernel(a_ref, b_ref, out_ref):
            out_ref[...] = a_ref[...] + b_ref[...]

        vmem = pl.BlockSpec(memory_space=pltpu.VMEM)
        return self(kernel, [a, b], [vmem] * 2, [jax.ShapeDtypeStruct(a.shape, a.dtype)], [vmem], "add", (a.size, 12 * a.size))

    def choose(self, index, values):
        def kernel(index_ref, *refs):
            *sources, out, sem = refs
            for i, ref in enumerate(sources):

                @pl.when(index_ref[0] == i)
                def _(ref=ref):
                    copy = pltpu.make_async_copy(ref, out, sem)
                    copy.start()
                    copy.wait()

        anywhere = pl.BlockSpec(memory_space=pl.ANY)
        value = values[0]
        return self(
            kernel,
            [index, *values],
            [pl.BlockSpec(memory_space=pltpu.SMEM)] + [anywhere] * len(values),
            [jax.ShapeDtypeStruct(value.shape, value.dtype)],
            [pl.BlockSpec(memory_space=pltpu.VMEM)],
            "choose",
            (0, 4 * value.size),
            scratch=[pltpu.SemaphoreType.DMA],
        )


def transpose8(x):
    at = lax.broadcasted_iota(jnp.int32, x[0].shape, 1)
    for d in (4, 2, 1):
        low = (at & d) == 0
        y = list(x)
        for i in range(8):
            if i & d == 0:
                a, b = x[i], x[i + d]
                y[i] = jnp.where(low, a, pltpu.roll(b, d, 1))
                y[i + d] = jnp.where(low, pltpu.roll(a, 8 - d, 1), b)
        x = y
    return x


def sum8(x):
    at = lax.broadcasted_iota(jnp.int32, x[0].shape, 1)
    for d in (4, 2, 1):
        low = (at & d) == 0
        y = []
        for a, b in zip(x[:d], x[d : 2 * d]):
            gone = jnp.where(low, b, a)
            back = pltpu.roll(gone, d, 1)
            if d != 4:
                back = jnp.where(low, pltpu.roll(gone, 8 - d, 1), back)
            y.append(jnp.where(low, a, b) + back)
        x = y
    return x[0]


def extract_kernel(groups, stride, spans, a_ref, sol_ref, part_ref, *rest):
    cols, wide = rest[: len(spans)], rest[-1]
    rows = part_ref.shape[1]
    if len(rest) > len(spans) + 1:
        rest[len(spans)][...] = a_ref[...]
    wide[...] = a_ref[...].astype(F32)
    i = pl.program_id(0)
    for col_ref, (start, stop) in zip(cols, spans):

        @pl.when((i >= start) & (i < stop))
        def _(col_ref=col_ref):
            for g in range(0, groups, stride):
                piece = wide[pl.ds(g, rows, stride=groups), :]
                col_ref[:, pl.ds(g // stride * LANES, LANES)] = piece.astype(BF16)

    if groups % 16 == 0:
        sol = sol_ref[...].astype(F32)
        totals = []
        for block in range(rows // 8):
            sums = []
            for r in range(8):
                base = (block * 8 + r) * groups
                sums.append(
                    sum(wide[pl.ds(base + 8 * h, 8), :] * sol[8 * h : 8 * h + 8] for h in range(groups // 8))[None]
                )
            totals.append(sum8(sums)[0])
        total = jnp.concatenate(totals, axis=0)
    else:
        total = jnp.zeros((rows, LANES), F32)
        for g in range(groups):
            total = total + wide[pl.ds(g, rows, stride=groups), :] * sol_ref[g : g + 1, :].astype(F32)
    ones = jnp.ones((8, LANES), F32)
    sums = lax.dot_general(
        ones, total, (((1,), (1,)), ((), ())), precision=lax.Precision.HIGHEST, preferred_element_type=F32
    )
    part_ref[...] = sums[0:1, :]


def extract(chain, flat, sol, sizes, first, groups, stride, width, with_band):
    sub = min(min(sizes), 256)
    size = sub * groups
    at = first // sub
    rows = sum(sizes)
    spans, out_specs, out_shape = [], [pl.BlockSpec((1, sub), lambda i: (0, i))], [jax.ShapeDtypeStruct((1, rows), F32)]
    start = 0
    for n in sizes:
        stop = start + n // sub
        spans.append((start, stop))
        out_specs.append(pl.BlockSpec((sub, width), lambda i, a=start, b=stop: (jnp.clip(i - a, 0, b - a - 1), 0)))
        out_shape.append(jax.ShapeDtypeStruct((n, width), BF16))
        start = stop
    if with_band:
        out_specs.append(pl.BlockSpec((size, LANES), lambda i: (i, 0)))
        out_shape.append(jax.ShapeDtypeStruct((rows * groups, LANES), BF16))
    return chain(
        lambda *refs: extract_kernel(groups, stride, spans, *refs),
        [flat, sol],
        [
            pl.BlockSpec((size, LANES), lambda i: (at + i, 0)),
            pl.BlockSpec((groups, LANES), lambda i: (0, 0)),
        ],
        out_shape,
        out_specs,
        "extract",
        (4 * rows * groups * LANES, rows * groups * LANES * 2),
        grid=(rows // sub,),
        scratch=[pltpu.VMEM((size, LANES), F32)],
    )


def factor_kernel(groups, n_x, where_ref, *refs):
    core, lane, x = where_ref[0], where_ref[1], where_ref[2]
    given, (blk_mine_ref, blk_other_ref, up_ref, low_ref, v_ref, raws, bands, blocks, sems, *rest) = refs[: 2 * n_x], refs[2 * n_x :]
    width = up_ref.shape[1]
    for i in range(n_x):

        @pl.when(x == i)
        def _(i=i):
            pairs = [(raws, given[2 * i], given[2 * i + 1]), (blocks, blk_mine_ref, blk_other_ref)]
            copies = []
            for kind, (target, mine, other) in enumerate(pairs):
                copies.append(pltpu.make_async_copy(mine, target.at[core], sems.at[kind, 0]))
                copies.append(pltpu.make_async_copy(other, target.at[1 - core], sems.at[kind, 1]))
            for copy in copies:
                copy.start()
            for copy in copies:
                copy.wait()

    for slot in range(2):
        if groups % 16 == 0:

            def one(block, carry, slot=slot):
                here = pl.ds(pl.multiple_of(block * 16 * groups, 16 * groups), 16 * groups)
                raw = raws[slot, here, :].astype(F32).reshape(2, 8, groups, LANES)
                rows = pl.ds(pl.multiple_of(block * 16, 16), 16)
                for h in range(groups // 8):
                    turned = transpose8([raw[:, r, 8 * h : 8 * h + 8] for r in range(8)])
                    for g in range(8):
                        at = pl.ds((8 * h + g) * LANES, LANES)
                        bands[slot, rows, at] = turned[g].reshape(16, LANES).astype(BF16)
                return carry

            lax.fori_loop(0, width // 16, one, 0, unroll=2)
        else:
            wide = rest[0]
            wide[...] = raws[slot].astype(F32)
            for g in range(groups):
                at = pl.ds(g * LANES, LANES)
                bands[slot, :, at] = wide[pl.ds(g, width, stride=groups), :].astype(BF16)
    row = lax.broadcasted_iota(jnp.int32, (width, width), 0)
    col = lax.broadcasted_iota(jnp.int32, (width, width), 1)
    zero = jnp.zeros((width, width), BF16)
    upper = [jnp.where(row <= col, up_ref[s], zero) for s in range(2)]
    lower = [jnp.where(row >= col, low_ref[s], zero) for s in range(2)]
    top_01 = matmul(lower[0], blocks[0]).astype(BF16)
    left_10 = matmul(blocks[1], upper[0]).astype(BF16)
    piece = min(groups * LANES, 1024)
    for n in range(groups * LANES // piece):
        at = slice(n * piece, (n + 1) * piece)
        top_0 = matmul(lower[0], bands[0, :, at]).astype(BF16)
        rest_1 = (bands[1, :, at].astype(F32) - matmul(left_10, top_0)).astype(BF16)
        top_1 = matmul(lower[1], rest_1).astype(BF16)
        v_1 = matmul(upper[1], top_1).astype(BF16)
        mixed = (top_0.astype(F32) - matmul(top_01, v_1)).astype(BF16)
        v_0 = matmul(upper[0], mixed).astype(BF16)
        v_ref[pl.ds(pl.multiple_of(lane * width, width), width), at] = v_0
        v_ref[pl.ds(pl.multiple_of((1 - lane) * width, width), width), at] = v_1


def factors(chain, where, bands, blocks, upper, lower, groups):
    width = upper.shape[1]
    cols = groups * LANES
    n_x = len(bands) // 2
    vmem = pl.BlockSpec(memory_space=pltpu.VMEM)
    anywhere = pl.BlockSpec(memory_space=pl.ANY)
    scratch = [
        pltpu.VMEM((2, width * groups, LANES), BF16),
        pltpu.VMEM((2, width, cols), BF16),
        pltpu.VMEM((2, width, width), BF16),
        pltpu.SemaphoreType.DMA((2, 2)),
    ]
    if groups % 16:
        scratch.append(pltpu.VMEM((width * groups, LANES), F32))
    return chain(
        lambda *refs: factor_kernel(groups, n_x, *refs),
        [where, *bands, *blocks, upper, lower],
        [pl.BlockSpec(memory_space=pltpu.SMEM)] + [anywhere] * (2 * n_x + 2) + [vmem] * 2,
        [jax.ShapeDtypeStruct((2 * width, cols), BF16)],
        [vmem],
        "factors",
        (12 * width * width * cols, 12 * width * cols),
        scratch=scratch,
    )


def update_kernel(groups, spans, a_ref, v_ref, *rest):
    out_ref, both, *wide = rest[-3 if groups % 16 else -2 :]
    rows, width = both.shape[0], both.shape[1] // 2
    i = pl.program_id(0)
    for c, (start, stop) in enumerate(spans):

        @pl.when((i >= start) & (i < stop))
        def _(c=c):
            both[:, :width] = rest[2 * c][...]
            both[:, width:] = rest[2 * c + 1][...]

    if groups % 16 == 0:
        part = min(rows, 128)
        for p in range(rows // part):
            value = matmul(both[p * part : (p + 1) * part, :], v_ref[...])
            for block in range(part // 8):
                cut = value[block * 8 : block * 8 + 8, :]
                halves = [
                    transpose8([cut[:, (8 * h + g) * LANES : (8 * h + g + 1) * LANES][None] for g in range(8)])
                    for h in range(groups // 8)
                ]
                for r in range(8):
                    here = pl.ds((p * part + block * 8 + r) * groups, groups)
                    change = jnp.concatenate([half[r][0] for half in halves], axis=0)
                    out_ref[here, :] = (a_ref[here, :].astype(F32) - change).astype(BF16)
        return
    value = matmul(both[...], v_ref[...])
    for g in range(groups):
        wide[0][pl.ds(g, rows, stride=groups), :] = value[:, g * LANES : (g + 1) * LANES]
    out_ref[...] = (a_ref[...].astype(F32) - wide[0][...]).astype(BF16)


def update(chain, flat, mine, other, v, out, first, groups):
    rows, width = sum(m.shape[0] for m in mine), mine[0].shape[1]
    sub = min(256, *(m.shape[0] for m in mine))
    size = sub * groups
    base = first // sub
    cols = groups * LANES
    in_specs = [pl.BlockSpec((size, LANES), lambda i: (base + i, 0)), pl.BlockSpec(memory_space=pltpu.VMEM)]
    args, spans, start = [flat, v], [], 0
    for m, o in zip(mine, other):
        stop = start + m.shape[0] // sub
        args += [m, o]
        in_specs += [pl.BlockSpec((sub, width), lambda i, a=start, b=stop: (jnp.clip(i - a, 0, b - a - 1), 0))] * 2
        spans.append((start, stop))
        start = stop
    aliases = {}
    if out is not None:
        aliases = {len(args): 0}
        in_specs.append(pl.BlockSpec(memory_space=pl.ANY))
        args.append(out)
    scratch = [pltpu.VMEM((sub, 2 * width), BF16)]
    if groups % 16:
        scratch.append(pltpu.VMEM((size, LANES), F32))
    return chain(
        lambda *refs: update_kernel(groups, spans, *refs),
        args,
        in_specs,
        [jax.ShapeDtypeStruct(flat.shape, BF16)],
        [pl.BlockSpec((size, LANES), lambda i: (base + i, 0))],
        "update",
        (4 * rows * width * cols, 4 * rows * cols + 4 * rows * width),
        grid=(rows // sub,),
        scratch=scratch,
        aliases=aliases,
    )


def solve_kernel(place_ref, state_ref, res_ref, inv_ref, *rest):
    cols, out_ref = rest[:-1], rest[-1]
    place, lane = place_ref[0], place_ref[1]
    width = inv_ref.shape[0]
    nt = (((1,), (1,)), ((), ()))
    pending = jnp.zeros((8, width), F32)
    for j, col in enumerate(cols):
        at = (j + lane) % 2 if j < 2 else j
        known = jnp.where(at < place, state_ref[pl.ds(at, 1), :], 0.0)
        pending = pending + lax.dot_general(
            jnp.broadcast_to(known, (8, width)).astype(BF16), col[...], nt, preferred_element_type=F32
        )
    left = res_ref[...] - pending[0:1, :]
    high = left.astype(BF16)
    rest_1 = left - high.astype(F32)
    mid = rest_1.astype(BF16)
    low = (rest_1 - mid.astype(F32)).astype(BF16)
    total = jnp.zeros((8, width), F32)
    for piece in (low, mid, high):
        wide = jnp.broadcast_to(piece.astype(F32), (8, width)).astype(BF16)
        total = total + lax.dot_general(wide, inv_ref[...], nt, preferred_element_type=F32)
    row = lax.broadcasted_iota(jnp.int32, state_ref.shape, 0)
    out_ref[...] = jnp.where(row == place, jnp.broadcast_to(total[0:1, :], state_ref.shape), state_ref[...])


def solve_step(chain, place, state, res, inv, cols):
    vmem = pl.BlockSpec(memory_space=pltpu.VMEM)
    return chain(
        solve_kernel,
        [place, state, res, inv, *cols],
        [pl.BlockSpec(memory_space=pltpu.SMEM)] + [vmem] * (3 + len(cols)),
        [jax.ShapeDtypeStruct(state.shape, F32)],
        [vmem],
        "solve",
        (2 * inv.size * (len(cols) + 3), 2 * inv.size * (len(cols) + 1)),
    )


def shards(matrix, upper_inv, lower_inv, solution, right_side, diagonal_block_inverses):
    slots, _, width, col_slots, _, _ = matrix.shape
    n_prow = lax.axis_size("prow")
    n_pcol = lax.axis_size("pcol")
    ny = n_prow // 2
    nz = n_pcol // ny
    prow = lax.axis_index("prow")
    pcol = lax.axis_index("pcol")
    z, y = pcol // ny, pcol % ny
    core, lane = prow % 2, y % 2
    lane_tiles = width // LANES
    groups = lane_tiles * col_slots
    rows = slots * width
    flat = matrix.reshape(rows, col_slots, lane_tiles, LANES).transpose(0, 2, 1, 3).reshape(rows * groups, LANES)
    sol = solution.reshape(col_slots, lane_tiles, LANES).transpose(1, 0, 2).reshape(groups, LANES)

    chain = Chain()

    def spread(value, axis, size):
        values = [value]
        for s in range(2, size, 2):
            pairs = [(s - 2, s), (s - 1, s + 1), (s, s - 2), (s + 1, s - 1)]
            values.append(lax.ppermute(values[-1], axis, pairs))
        return values

    def swap(value, axis, size, bit=1):
        return lax.ppermute(value, axis, [(i, i ^ bit) for i in range(size)])

    def along_z(pairs):
        return [(a * ny + k, b * ny + k) for a, b in pairs for k in range(2)]

    stages = [[[(0, nz // 2)]]]
    held, step = [nz // 2], nz // 4
    while step:
        stages.append([[(m, m - step) for m in held], [(m, m + step) for m in held]])
        held = [b for moves in stages[-1] for _, b in moves]
        step //= 2

    def picked(got, moves, value):
        mask = z == moves[0][1]
        for _, b in moves[1:]:
            mask = mask | (z == b)
        return jnp.where(mask, got, value)

    def first_stage(local):
        return lax.ppermute(local, "pcol", along_z(stages[0][0]))

    def second_stage(arrived):
        return [lax.ppermute(arrived, "pcol", along_z(moves)) for moves in stages[1]]

    source = jnp.zeros((), jnp.int32)
    for i, moves in enumerate(stages[0] + stages[1]):
        for _, b in moves:
            source = jnp.where(z == b, i + 1, source)
    source = source.astype(jnp.int32).reshape(1)

    def settle(local, arrived, outward):
        value = chain.choose(source, [local, arrived, *outward])
        for stage in stages[2:]:
            gots = [lax.ppermute(value, "pcol", along_z(moves)) for moves in stage]
            for got, moves in zip(gots, stage):
                value = picked(got, moves, value)
        for s in range(2, ny, 2):
            pairs = [(a * ny + s - 2 + k, a * ny + s + k) for a in range(nz) for k in range(2)]
            got = lax.ppermute(value, "pcol", pairs)
            value = jnp.where(y // 2 == s // 2, got, value)
        return value

    count = n_prow * diagonal_block_inverses.shape[0]
    assert diagonal_block_inverses.shape[0] == 1
    home = count - 2
    inv = diagonal_block_inverses.reshape(width, width)
    place = jnp.stack([prow, lane]).astype(jnp.int32)
    where = jnp.stack([core, lane, prow // 2]).astype(jnp.int32)
    flag = jnp.where(core != lane, 0, 1).astype(jnp.int32).reshape(1)
    bits = [1 << b for b in range(n_pcol.bit_length() - 1)]

    sizes = [width] + [2 * width] * ((slots - 2) // 2)
    sizes += [width] * (slots - sum(sizes) // width)
    starts = [sum(sizes[:c]) for c in range(len(sizes) + 1)]
    chunks = len(sizes)
    column, first, outward, mine, other, box = {}, {}, {}, {}, {}, {"out": None}

    def extracts(a, b, with_band=False):
        part, *cols = extract(chain, flat, sol, sizes[a:b], starts[a], groups, col_slots, width, with_band)
        column.update(zip(range(a, b), cols))
        return part, cols[-1]

    parts = []
    part, band = extracts(0, 1, True)
    parts.append(part)
    first[0] = first_stage(column[0])
    bands = spread(band, "prow", n_prow)
    swaps = {0: swap(band, "prow", n_prow)}
    parts.append(extracts(1, 2)[0])

    def total_step(bit):
        def run():
            if bit == 1:
                box["total"] = jnp.concatenate(parts, axis=1).reshape(slots, width)
            box["total"] = chain.add(box["total"], swap(box["total"], "pcol", n_pcol, bit))
            if bit == bits[-1]:
                box["residual"] = right_side.reshape(slots, width) - box["total"]

        return run

    def solve(k):
        def run():
            if k == 0:
                needed = [mine[0], other[0]]
                for j in range(2, home):
                    needed.append(lax.ppermute(column[0], "pcol", [(j, home)]))
                box["needed"] = needed + [column[0]]
                state = jnp.zeros((count, width), F32)
            else:
                state = lax.ppermute(box["state"], "prow", [(i, i + 1) for i in range(n_prow - 1)])
            state = solve_step(chain, place, state, box["residual"][0:1], inv, box["needed"])
            if k == count - 1:
                state = jnp.where((prow == n_prow - 1) & (pcol == home), state, 0.0)
            box["state"] = state

        return run

    def share(axis, size, bit):
        def run():
            box["state"] = chain.add(box["state"], swap(box["state"], axis, size, bit))

        return run

    def arrive(values):
        got = chain.gate(list(values), [])
        return got if len(values) > 1 else [got]

    def blocks_out():
        box["pick"] = spread(chain.choose(flag, [mine[0], other[0]]), "prow", n_prow)
        bands[1:] = arrive(bands[1:])
        for i, value in enumerate(bands[1:]):
            swaps[i + 1] = swap(value, "prow", n_prow)

    def bands_in():
        for i, value in zip(range(1, len(bands)), arrive([swaps[i] for i in range(1, len(bands))])):
            swaps[i] = value
        box["bands"] = [v for i, b in enumerate(bands) for v in (b, swaps[i])]

    def blocks_swap():
        blk = chain.choose(where[2:3], box["pick"])
        box["blks"] = [blk, swap(blk, "prow", n_prow)]

    def blocks_in():
        box["blks"][1:] = arrive(box["blks"][1:])

    def make_factors():
        box["v"] = factors(chain, where, box["bands"], box["blks"], upper_inv, lower_inv, groups)

    def updates(*which):
        def run():
            args = [mine[c] for c in which], [other[c] for c in which]
            box["out"] = update(chain, flat, *args, box["v"], box["out"], starts[which[0]], groups)

        return run

    def take(c):
        mine[c] = settle(column[c], first[c], outward[c])
        other[c] = swap(mine[c], "pcol", n_pcol)

    total = [total_step(b) for b in bits]
    line = [solve(k) for k in range(count)]
    line += [share("prow", n_prow, 1 << b) for b in range(n_prow.bit_length() - 1)]
    line += [share("pcol", n_pcol, b) for b in bits]
    def rest_extracted():
        if chunks > 2:
            parts.append(extracts(2, chunks)[0])

    if chunks == 5 and len(line) == 9:
        plan = {
            0: [rest_extracted, lambda: take(0), *total],
            1: [blocks_out, line[0], bands_in, *line[1:3], blocks_swap, line[3], blocks_in],
            2: [make_factors, line[4], updates(0, 1), line[5]],
            3: [line[6], updates(2), line[7]],
            4: [updates(3), line[8]],
        }
    else:
        plan = {0: [rest_extracted, lambda: take(0), *total], chunks - 1: [blocks_out, bands_in, blocks_swap, blocks_in, make_factors, *line, updates(*range(chunks - 1))]}

    for k in range(chunks):
        ahead = [column[k + 1]] if k + 1 < chunks else []
        extra = [swaps[0]] if k == 0 else []
        got = chain.gate([first[k], *ahead, *extra], [])
        got = got if ahead or extra else [got]
        first[k] = got[0]
        if ahead:
            column[k + 1] = got[1]
            first[k + 1] = first_stage(column[k + 1])
        extra = got[1 + len(ahead) :]
        if k == 0:
            swaps[0] = extra[0]
        outward[k] = second_stage(first[k])
        if k > 1:
            take(k - 1)
        for task in plan.get(k, []):
            task()
    take(chunks - 1)
    updates(chunks - 1)()
    residual, out, state = box["residual"], box["out"], box["state"]
    updated = out.reshape(rows, lane_tiles, col_slots, LANES).transpose(0, 2, 1, 3).reshape(matrix.shape)
    return (updated, residual.reshape(right_side.shape), state)


def solution(mesh):
    return jax.shard_map(
        shards,
        mesh=mesh,
        in_specs=(
            P(None, "prow", None, None, "pcol", None),
            P(),
            P(),
            P(None, "pcol", None),
            P(None, "prow", None),
            P(None, "prow", None, None),
        ),
        out_specs=(P(None, "prow", None, None, "pcol", None), P(None, "prow", None), P()),
        check_vma=False,
    )
```

```python
import jax
import jax.numpy as jnp
from jax import lax
from jax.experimental import pallas as pl
from jax.experimental.pallas import tpu as pltpu
from jax.sharding import PartitionSpec as P

LANES = 128
VMEM_BYTES = 50 * 1024 * 1024
F32 = jnp.float32
BF16 = jnp.bfloat16


def matmul(a, b):
    return jnp.dot(a, b, preferred_element_type=F32)


class Chain:
    def __init__(self):
        self.token = None

    def __call__(self, kernel, inputs, in_specs, out_shape, out_specs, name, work, after=(), grid=None, scratch=(), aliases=None):
        deps = list(after) + ([] if self.token is None else [self.token])
        n_in, n_out, n_dep = len(inputs), len(out_shape), len(deps)
        anywhere = pl.BlockSpec(memory_space=pl.ANY)

        def body(*refs):
            outs = n_in + n_dep
            kernel(*refs[:n_in], *refs[outs : outs + n_out], *refs[outs + n_out + 1 :])

        params = {} if grid is None else {"grid": grid}
        *results, self.token = pl.pallas_call(
            body,
            in_specs=list(in_specs) + [anywhere] * n_dep,
            out_specs=list(out_specs) + [anywhere],
            out_shape=list(out_shape) + [jax.ShapeDtypeStruct((8, LANES), F32)],
            scratch_shapes=list(scratch),
            input_output_aliases=aliases or {},
            compiler_params=pltpu.CompilerParams(vmem_limit_bytes=VMEM_BYTES),
            cost_estimate=pl.CostEstimate(flops=0, bytes_accessed=0, transcendentals=0),
            name=name,
            **params,
        )(*inputs, *deps)
        return results[0] if len(results) == 1 else results

    def gate(self, values, after):
        anywhere = pl.BlockSpec(memory_space=pl.ANY)
        return self(
            lambda *refs: None,
            values,
            [anywhere] * len(values),
            [jax.ShapeDtypeStruct(v.shape, v.dtype) for v in values],
            [anywhere] * len(values),
            "gate",
            (0, 0),
            after=after,
            aliases={i: i for i in range(len(values))},
        )

    def add(self, a, b):
        def kernel(a_ref, b_ref, out_ref):
            out_ref[...] = a_ref[...] + b_ref[...]

        vmem = pl.BlockSpec(memory_space=pltpu.VMEM)
        return self(kernel, [a, b], [vmem] * 2, [jax.ShapeDtypeStruct(a.shape, a.dtype)], [vmem], "add", (a.size, 12 * a.size))

    def choose(self, index, values):
        def kernel(index_ref, *refs):
            *sources, out, sem = refs
            for i, ref in enumerate(sources):

                @pl.when(index_ref[0] == i)
                def _(ref=ref):
                    copy = pltpu.make_async_copy(ref, out, sem)
                    copy.start()
                    copy.wait()

        anywhere = pl.BlockSpec(memory_space=pl.ANY)
        value = values[0]
        return self(
            kernel,
            [index, *values],
            [pl.BlockSpec(memory_space=pltpu.SMEM)] + [anywhere] * len(values),
            [jax.ShapeDtypeStruct(value.shape, value.dtype)],
            [pl.BlockSpec(memory_space=pltpu.VMEM)],
            "choose",
            (0, 4 * value.size),
            scratch=[pltpu.SemaphoreType.DMA],
        )


def transpose8(x):
    at = lax.broadcasted_iota(jnp.int32, x[0].shape, 1)
    for d in (4, 2, 1):
        low = (at & d) == 0
        y = list(x)
        for i in range(8):
            if i & d == 0:
                a, b = x[i], x[i + d]
                y[i] = jnp.where(low, a, pltpu.roll(b, d, 1))
                y[i + d] = jnp.where(low, pltpu.roll(a, 8 - d, 1), b)
        x = y
    return x


def sum8(x):
    at = lax.broadcasted_iota(jnp.int32, x[0].shape, 1)
    for d in (4, 2, 1):
        low = (at & d) == 0
        y = []
        for a, b in zip(x[:d], x[d : 2 * d]):
            gone = jnp.where(low, b, a)
            back = pltpu.roll(gone, d, 1)
            if d != 4:
                back = jnp.where(low, pltpu.roll(gone, 8 - d, 1), back)
            y.append(jnp.where(low, a, b) + back)
        x = y
    return x[0]


def extract_kernel(groups, stride, spans, a_ref, sol_ref, part_ref, *rest):
    cols, wide = rest[: len(spans)], rest[-1]
    rows = part_ref.shape[1]
    if len(rest) > len(spans) + 1:
        rest[len(spans)][...] = a_ref[...]
    wide[...] = a_ref[...].astype(F32)
    i = pl.program_id(0)
    for col_ref, (start, stop) in zip(cols, spans):

        @pl.when((i >= start) & (i < stop))
        def _(col_ref=col_ref):
            for g in range(0, groups, stride):
                piece = wide[pl.ds(g, rows, stride=groups), :]
                col_ref[:, pl.ds(g // stride * LANES, LANES)] = piece.astype(BF16)

    if groups % 16 == 0:
        sol = sol_ref[...].astype(F32)
        totals = []
        for block in range(rows // 8):
            sums = []
            for r in range(8):
                base = (block * 8 + r) * groups
                sums.append(
                    sum(wide[pl.ds(base + 8 * h, 8), :] * sol[8 * h : 8 * h + 8] for h in range(groups // 8))[None]
                )
            totals.append(sum8(sums)[0])
        total = jnp.concatenate(totals, axis=0)
    else:
        total = jnp.zeros((rows, LANES), F32)
        for g in range(groups):
            total = total + wide[pl.ds(g, rows, stride=groups), :] * sol_ref[g : g + 1, :].astype(F32)
    ones = jnp.ones((8, LANES), F32)
    sums = lax.dot_general(
        ones, total, (((1,), (1,)), ((), ())), precision=lax.Precision.HIGHEST, preferred_element_type=F32
    )
    part_ref[...] = sums[0:1, :]


def extract(chain, flat, sol, sizes, first, groups, stride, width, with_band):
    sub = min(min(sizes), 256)
    size = sub * groups
    at = first // sub
    rows = sum(sizes)
    spans, out_specs, out_shape = [], [pl.BlockSpec((1, sub), lambda i: (0, i))], [jax.ShapeDtypeStruct((1, rows), F32)]
    start = 0
    for n in sizes:
        stop = start + n // sub
        spans.append((start, stop))
        out_specs.append(pl.BlockSpec((sub, width), lambda i, a=start, b=stop: (jnp.clip(i - a, 0, b - a - 1), 0)))
        out_shape.append(jax.ShapeDtypeStruct((n, width), BF16))
        start = stop
    if with_band:
        out_specs.append(pl.BlockSpec((size, LANES), lambda i: (i, 0)))
        out_shape.append(jax.ShapeDtypeStruct((rows * groups, LANES), BF16))
    return chain(
        lambda *refs: extract_kernel(groups, stride, spans, *refs),
        [flat, sol],
        [
            pl.BlockSpec((size, LANES), lambda i: (at + i, 0)),
            pl.BlockSpec((groups, LANES), lambda i: (0, 0)),
        ],
        out_shape,
        out_specs,
        "extract",
        (4 * rows * groups * LANES, rows * groups * LANES * 2),
        grid=(rows // sub,),
        scratch=[pltpu.VMEM((size, LANES), F32)],
    )


def factor_kernel(groups, n_x, where_ref, *refs):
    core, lane, x = where_ref[0], where_ref[1], where_ref[2]
    given, (blk_mine_ref, blk_other_ref, up_ref, low_ref, v_ref, raws, bands, blocks, sems, *rest) = refs[: 2 * n_x], refs[2 * n_x :]
    width = up_ref.shape[1]
    for i in range(n_x):

        @pl.when(x == i)
        def _(i=i):
            pairs = [(raws, given[2 * i], given[2 * i + 1]), (blocks, blk_mine_ref, blk_other_ref)]
            copies = []
            for kind, (target, mine, other) in enumerate(pairs):
                copies.append(pltpu.make_async_copy(mine, target.at[core], sems.at[kind, 0]))
                copies.append(pltpu.make_async_copy(other, target.at[1 - core], sems.at[kind, 1]))
            for copy in copies:
                copy.start()
            for copy in copies:
                copy.wait()

    for slot in range(2):
        if groups % 16 == 0:

            def one(block, carry, slot=slot):
                here = pl.ds(pl.multiple_of(block * 16 * groups, 16 * groups), 16 * groups)
                raw = raws[slot, here, :].astype(F32).reshape(2, 8, groups, LANES)
                rows = pl.ds(pl.multiple_of(block * 16, 16), 16)
                for h in range(groups // 8):
                    turned = transpose8([raw[:, r, 8 * h : 8 * h + 8] for r in range(8)])
                    for g in range(8):
                        at = pl.ds((8 * h + g) * LANES, LANES)
                        bands[slot, rows, at] = turned[g].reshape(16, LANES).astype(BF16)
                return carry

            lax.fori_loop(0, width // 16, one, 0, unroll=2)
        else:
            wide = rest[0]
            wide[...] = raws[slot].astype(F32)
            for g in range(groups):
                at = pl.ds(g * LANES, LANES)
                bands[slot, :, at] = wide[pl.ds(g, width, stride=groups), :].astype(BF16)
    row = lax.broadcasted_iota(jnp.int32, (width, width), 0)
    col = lax.broadcasted_iota(jnp.int32, (width, width), 1)
    zero = jnp.zeros((width, width), BF16)
    upper = [jnp.where(row <= col, up_ref[s], zero) for s in range(2)]
    lower = [jnp.where(row >= col, low_ref[s], zero) for s in range(2)]
    top_01 = matmul(lower[0], blocks[0]).astype(BF16)
    left_10 = matmul(blocks[1], upper[0]).astype(BF16)
    piece = min(groups * LANES, 1024)
    for n in range(groups * LANES // piece):
        at = slice(n * piece, (n + 1) * piece)
        top_0 = matmul(lower[0], bands[0, :, at]).astype(BF16)
        rest_1 = (bands[1, :, at].astype(F32) - matmul(left_10, top_0)).astype(BF16)
        top_1 = matmul(lower[1], rest_1).astype(BF16)
        v_1 = matmul(upper[1], top_1).astype(BF16)
        mixed = (top_0.astype(F32) - matmul(top_01, v_1)).astype(BF16)
        v_0 = matmul(upper[0], mixed).astype(BF16)
        v_ref[pl.ds(pl.multiple_of(lane * width, width), width), at] = v_0
        v_ref[pl.ds(pl.multiple_of((1 - lane) * width, width), width), at] = v_1


def factors(chain, where, bands, blocks, upper, lower, groups):
    width = upper.shape[1]
    cols = groups * LANES
    n_x = len(bands) // 2
    vmem = pl.BlockSpec(memory_space=pltpu.VMEM)
    anywhere = pl.BlockSpec(memory_space=pl.ANY)
    scratch = [
        pltpu.VMEM((2, width * groups, LANES), BF16),
        pltpu.VMEM((2, width, cols), BF16),
        pltpu.VMEM((2, width, width), BF16),
        pltpu.SemaphoreType.DMA((2, 2)),
    ]
    if groups % 16:
        scratch.append(pltpu.VMEM((width * groups, LANES), F32))
    return chain(
        lambda *refs: factor_kernel(groups, n_x, *refs),
        [where, *bands, *blocks, upper, lower],
        [pl.BlockSpec(memory_space=pltpu.SMEM)] + [anywhere] * (2 * n_x + 2) + [vmem] * 2,
        [jax.ShapeDtypeStruct((2 * width, cols), BF16)],
        [vmem],
        "factors",
        (12 * width * width * cols, 12 * width * cols),
        scratch=scratch,
    )


def update_kernel(groups, spans, a_ref, v_ref, *rest):
    out_ref, both, *wide = rest[-3 if groups % 16 else -2 :]
    rows, width = both.shape[0], both.shape[1] // 2
    i = pl.program_id(0)
    for c, (start, stop) in enumerate(spans):

        @pl.when((i >= start) & (i < stop))
        def _(c=c):
            both[:, :width] = rest[2 * c][...]
            both[:, width:] = rest[2 * c + 1][...]

    if groups % 16 == 0:
        part = min(rows, 128)
        for p in range(rows // part):
            value = matmul(both[p * part : (p + 1) * part, :], v_ref[...])
            for block in range(part // 8):
                cut = value[block * 8 : block * 8 + 8, :]
                halves = [
                    transpose8([cut[:, (8 * h + g) * LANES : (8 * h + g + 1) * LANES][None] for g in range(8)])
                    for h in range(groups // 8)
                ]
                for r in range(8):
                    here = pl.ds((p * part + block * 8 + r) * groups, groups)
                    change = jnp.concatenate([half[r][0] for half in halves], axis=0)
                    out_ref[here, :] = (a_ref[here, :].astype(F32) - change).astype(BF16)
        return
    value = matmul(both[...], v_ref[...])
    for g in range(groups):
        wide[0][pl.ds(g, rows, stride=groups), :] = value[:, g * LANES : (g + 1) * LANES]
    out_ref[...] = (a_ref[...].astype(F32) - wide[0][...]).astype(BF16)


def update(chain, flat, mine, other, v, out, first, groups):
    rows, width = sum(m.shape[0] for m in mine), mine[0].shape[1]
    sub = min(256, *(m.shape[0] for m in mine))
    size = sub * groups
    base = first // sub
    cols = groups * LANES
    in_specs = [pl.BlockSpec((size, LANES), lambda i: (base + i, 0)), pl.BlockSpec(memory_space=pltpu.VMEM)]
    args, spans, start = [flat, v], [], 0
    for m, o in zip(mine, other):
        stop = start + m.shape[0] // sub
        args += [m, o]
        in_specs += [pl.BlockSpec((sub, width), lambda i, a=start, b=stop: (jnp.clip(i - a, 0, b - a - 1), 0))] * 2
        spans.append((start, stop))
        start = stop
    aliases = {}
    if out is not None:
        aliases = {len(args): 0}
        in_specs.append(pl.BlockSpec(memory_space=pl.ANY))
        args.append(out)
    scratch = [pltpu.VMEM((sub, 2 * width), BF16)]
    if groups % 16:
        scratch.append(pltpu.VMEM((size, LANES), F32))
    return chain(
        lambda *refs: update_kernel(groups, spans, *refs),
        args,
        in_specs,
        [jax.ShapeDtypeStruct(flat.shape, BF16)],
        [pl.BlockSpec((size, LANES), lambda i: (base + i, 0))],
        "update",
        (4 * rows * width * cols, 4 * rows * cols + 4 * rows * width),
        grid=(rows // sub,),
        scratch=scratch,
        aliases=aliases,
    )


def solve_kernel(place_ref, state_ref, res_ref, inv_ref, *rest):
    cols, out_ref = rest[:-1], rest[-1]
    place, lane = place_ref[0], place_ref[1]
    width = inv_ref.shape[0]
    nt = (((1,), (1,)), ((), ()))
    pending = jnp.zeros((8, width), F32)
    for j, col in enumerate(cols):
        at = (j + lane) % 2 if j < 2 else j
        known = jnp.where(at < place, state_ref[pl.ds(at, 1), :], 0.0)
        pending = pending + lax.dot_general(
            jnp.broadcast_to(known, (8, width)).astype(BF16), col[...], nt, preferred_element_type=F32
        )
    left = res_ref[...] - pending[0:1, :]
    high = left.astype(BF16)
    rest_1 = left - high.astype(F32)
    mid = rest_1.astype(BF16)
    low = (rest_1 - mid.astype(F32)).astype(BF16)
    total = jnp.zeros((8, width), F32)
    for piece in (low, mid, high):
        wide = jnp.broadcast_to(piece.astype(F32), (8, width)).astype(BF16)
        total = total + lax.dot_general(wide, inv_ref[...], nt, preferred_element_type=F32)
    row = lax.broadcasted_iota(jnp.int32, state_ref.shape, 0)
    out_ref[...] = jnp.where(row == place, jnp.broadcast_to(total[0:1, :], state_ref.shape), state_ref[...])


def solve_step(chain, place, state, res, inv, cols):
    vmem = pl.BlockSpec(memory_space=pltpu.VMEM)
    return chain(
        solve_kernel,
        [place, state, res, inv, *cols],
        [pl.BlockSpec(memory_space=pltpu.SMEM)] + [vmem] * (3 + len(cols)),
        [jax.ShapeDtypeStruct(state.shape, F32)],
        [vmem],
        "solve",
        (2 * inv.size * (len(cols) + 3), 2 * inv.size * (len(cols) + 1)),
    )


def shards(matrix, upper_inv, lower_inv, solution, right_side, diagonal_block_inverses):
    slots, _, width, col_slots, _, _ = matrix.shape
    n_prow = lax.axis_size("prow")
    n_pcol = lax.axis_size("pcol")
    ny = n_prow // 2
    nz = n_pcol // ny
    prow = lax.axis_index("prow")
    pcol = lax.axis_index("pcol")
    z, y = pcol // ny, pcol % ny
    core, lane = prow % 2, y % 2
    lane_tiles = width // LANES
    groups = lane_tiles * col_slots
    rows = slots * width
    flat = matrix.reshape(rows, col_slots, lane_tiles, LANES).transpose(0, 2, 1, 3).reshape(rows * groups, LANES)
    sol = solution.reshape(col_slots, lane_tiles, LANES).transpose(1, 0, 2).reshape(groups, LANES)

    chain = Chain()

    def spread(value, axis, size):
        values = [value]
        for s in range(2, size, 2):
            pairs = [(s - 2, s), (s - 1, s + 1), (s, s - 2), (s + 1, s - 1)]
            values.append(lax.ppermute(values[-1], axis, pairs))
        return values

    def swap(value, axis, size, bit=1):
        return lax.ppermute(value, axis, [(i, i ^ bit) for i in range(size)])

    def along_z(pairs):
        return [(a * ny + k, b * ny + k) for a, b in pairs for k in range(2)]

    stages = [[[(0, nz // 2)]]]
    held, step = [nz // 2], nz // 4
    while step:
        stages.append([[(m, m - step) for m in held], [(m, m + step) for m in held]])
        held = [b for moves in stages[-1] for _, b in moves]
        step //= 2

    def picked(got, moves, value):
        mask = z == moves[0][1]
        for _, b in moves[1:]:
            mask = mask | (z == b)
        return jnp.where(mask, got, value)

    def first_stage(local):
        return lax.ppermute(local, "pcol", along_z(stages[0][0]))

    def second_stage(arrived):
        return [lax.ppermute(arrived, "pcol", along_z(moves)) for moves in stages[1]]

    source = jnp.zeros((), jnp.int32)
    for i, moves in enumerate(stages[0] + stages[1]):
        for _, b in moves:
            source = jnp.where(z == b, i + 1, source)
    source = source.astype(jnp.int32).reshape(1)

    def settle(local, arrived, outward):
        value = chain.choose(source, [local, arrived, *outward])
        for stage in stages[2:]:
            gots = [lax.ppermute(value, "pcol", along_z(moves)) for moves in stage]
            for got, moves in zip(gots, stage):
                value = picked(got, moves, value)
        for s in range(2, ny, 2):
            pairs = [(a * ny + s - 2 + k, a * ny + s + k) for a in range(nz) for k in range(2)]
            got = lax.ppermute(value, "pcol", pairs)
            value = jnp.where(y // 2 == s // 2, got, value)
        return value

    count = n_prow * diagonal_block_inverses.shape[0]
    assert diagonal_block_inverses.shape[0] == 1
    home = count - 2
    inv = diagonal_block_inverses.reshape(width, width)
    place = jnp.stack([prow, lane]).astype(jnp.int32)
    where = jnp.stack([core, lane, prow // 2]).astype(jnp.int32)
    flag = jnp.where(core != lane, 0, 1).astype(jnp.int32).reshape(1)
    bits = [1 << b for b in range(n_pcol.bit_length() - 1)]
    order = bits[1:] + bits[:1]

    sizes = [width] + [2 * width] * ((slots - 2) // 2)
    sizes += [width] * (slots - sum(sizes) // width)
    starts = [sum(sizes[:c]) for c in range(len(sizes) + 1)]
    chunks = len(sizes)
    column, first, outward, mine, other, box = {}, {}, {}, {}, {}, {"out": None}

    def extracts(a, b, with_band=False):
        part, *cols = extract(chain, flat, sol, sizes[a:b], starts[a], groups, col_slots, width, with_band)
        column.update(zip(range(a, b), cols))
        return part, cols[-1]

    parts = []
    part, band = extracts(0, 1, True)
    parts.append(part)
    first[0] = first_stage(column[0])
    bands = spread(band, "prow", n_prow)
    swaps = {0: swap(band, "prow", n_prow)}
    parts.append(extracts(1, 2)[0])

    def total_step(bit):
        def run():
            if bit == order[0]:
                box["total"] = jnp.concatenate(parts, axis=1).reshape(slots, width)
            box["total"] = chain.add(box["total"], swap(box["total"], "pcol", n_pcol, bit))
            if bit == order[-1]:
                box["residual"] = right_side.reshape(slots, width) - box["total"]

        return run

    def solve(k):
        def run():
            if k == 0:
                needed = [mine[0], other[0]]
                for j in range(2, home):
                    needed.append(lax.ppermute(column[0], "pcol", [(j, home)]))
                box["needed"] = needed + [column[0]]
                state = jnp.zeros((count, width), F32)
            else:
                state = lax.ppermute(box["state"], "prow", [(i, i + 1) for i in range(n_prow - 1)])
            state = solve_step(chain, place, state, box["residual"][0:1], inv, box["needed"])
            if k == count - 1:
                state = jnp.where((prow == n_prow - 1) & (pcol == home), state, 0.0)
            box["state"] = state

        return run

    def share(axis, size, bit):
        def run():
            box["state"] = chain.add(box["state"], swap(box["state"], axis, size, bit))

        return run

    def arrive(values):
        got = chain.gate(list(values), [])
        return got if len(values) > 1 else [got]

    def blocks_out():
        box["pick"] = spread(chain.choose(flag, [mine[0], other[0]]), "prow", n_prow)
        bands[1:] = arrive(bands[1:])
        for i, value in enumerate(bands[1:]):
            swaps[i + 1] = swap(value, "prow", n_prow)

    def bands_in():
        for i, value in zip(range(1, len(bands)), arrive([swaps[i] for i in range(1, len(bands))])):
            swaps[i] = value
        box["bands"] = [v for i, b in enumerate(bands) for v in (b, swaps[i])]

    def blocks_swap():
        blk = chain.choose(where[2:3], box["pick"])
        box["blks"] = [blk, swap(blk, "prow", n_prow)]

    def blocks_in():
        box["blks"][1:] = arrive(box["blks"][1:])

    def make_factors():
        box["v"] = factors(chain, where, box["bands"], box["blks"], upper_inv, lower_inv, groups)

    def updates(*which):
        def run():
            args = [mine[c] for c in which], [other[c] for c in which]
            box["out"] = update(chain, flat, *args, box["v"], box["out"], starts[which[0]], groups)

        return run

    def take(c):
        mine[c] = settle(column[c], first[c], outward[c])
        other[c] = swap(mine[c], "pcol", n_pcol)

    total = [total_step(b) for b in order]
    line = [solve(k) for k in range(count)]
    line += [share("prow", n_prow, 1 << b) for b in range(n_prow.bit_length() - 1)]
    line += [share("pcol", n_pcol, b) for b in bits]
    def extracted(a, b):
        if a < b:
            parts.append(extracts(a, b)[0])

    def advance(k):
        ahead = [column[k + 1]] if k + 1 < chunks else []
        extra = [swaps[0]] if k == 0 else []
        got = chain.gate([first[k], *ahead, *extra], [])
        got = got if ahead or extra else [got]
        first[k] = got[0]
        if ahead:
            column[k + 1] = got[1]
            first[k + 1] = first_stage(column[k + 1])
        if extra:
            swaps[0] = got[-1]
        outward[k] = second_stage(first[k])

    def each(tasks):
        for task in tasks:
            task()

    advance(0)
    extracted(2, min(3, chunks))
    take(0)
    extracted(3, chunks)
    if chunks == 5 and len(line) == 9:
        each(total[:2])
        advance(1)
        each([blocks_out, total[2], bands_in, line[0], blocks_swap, blocks_in, make_factors])
        advance(2)
        take(1)
        updates(0)()
        other[1] = arrive([other[1]])[0]
        advance(3)
        take(2)
        each([updates(1), *line[1:6]])
        advance(4)
        take(3)
        each([line[6], updates(2)])
        take(4)
        each([line[7], updates(3), line[8], updates(4)])
    else:
        each([*total, blocks_out, bands_in, blocks_swap, blocks_in, make_factors, *line])
        for k in range(1, chunks):
            advance(k)
            take(k)
        updates(*range(chunks))()
    residual, out, state = box["residual"], box["out"], box["state"]
    updated = out.reshape(rows, lane_tiles, col_slots, LANES).transpose(0, 2, 1, 3).reshape(matrix.shape)
    return (updated, residual.reshape(right_side.shape), state)


def solution(mesh):
    return jax.shard_map(
        shards,
        mesh=mesh,
        in_specs=(
            P(None, "prow", None, None, "pcol", None),
            P(),
            P(),
            P(None, "pcol", None),
            P(None, "prow", None),
            P(None, "prow", None, None),
        ),
        out_specs=(P(None, "prow", None, None, "pcol", None), P(None, "prow", None), P()),
        check_vma=False,
    )
```

```python
import jax
import jax.numpy as jnp
from jax import lax
from jax.experimental import pallas as pl
from jax.experimental.pallas import tpu as pltpu
from jax.sharding import PartitionSpec as P

LANES = 128
VMEM_BYTES = 50 * 1024 * 1024
F32 = jnp.float32
BF16 = jnp.bfloat16


def matmul(a, b):
    return jnp.dot(a, b, preferred_element_type=F32)


class Chain:
    def __init__(self):
        self.token = None

    def __call__(self, kernel, inputs, in_specs, out_shape, out_specs, name, work, after=(), grid=None, scratch=(), aliases=None):
        deps = list(after) + ([] if self.token is None else [self.token])
        n_in, n_out, n_dep = len(inputs), len(out_shape), len(deps)
        anywhere = pl.BlockSpec(memory_space=pl.ANY)

        def body(*refs):
            outs = n_in + n_dep
            kernel(*refs[:n_in], *refs[outs : outs + n_out], *refs[outs + n_out + 1 :])

        params = {} if grid is None else {"grid": grid}
        *results, self.token = pl.pallas_call(
            body,
            in_specs=list(in_specs) + [anywhere] * n_dep,
            out_specs=list(out_specs) + [anywhere],
            out_shape=list(out_shape) + [jax.ShapeDtypeStruct((8, LANES), F32)],
            scratch_shapes=list(scratch),
            input_output_aliases=aliases or {},
            compiler_params=pltpu.CompilerParams(vmem_limit_bytes=VMEM_BYTES),
            cost_estimate=pl.CostEstimate(flops=0, bytes_accessed=0, transcendentals=0),
            name=name,
            **params,
        )(*inputs, *deps)
        return results[0] if len(results) == 1 else results

    def gate(self, values, after):
        anywhere = pl.BlockSpec(memory_space=pl.ANY)
        return self(
            lambda *refs: None,
            values,
            [anywhere] * len(values),
            [jax.ShapeDtypeStruct(v.shape, v.dtype) for v in values],
            [anywhere] * len(values),
            "gate",
            (0, 0),
            after=after,
            aliases={i: i for i in range(len(values))},
        )

    def add(self, a, b):
        def kernel(a_ref, b_ref, out_ref):
            out_ref[...] = a_ref[...] + b_ref[...]

        vmem = pl.BlockSpec(memory_space=pltpu.VMEM)
        return self(kernel, [a, b], [vmem] * 2, [jax.ShapeDtypeStruct(a.shape, a.dtype)], [vmem], "add", (a.size, 12 * a.size))

    def choose(self, index, values):
        def kernel(index_ref, *refs):
            *sources, out, sem = refs
            for i, ref in enumerate(sources):

                @pl.when(index_ref[0] == i)
                def _(ref=ref):
                    copy = pltpu.make_async_copy(ref, out, sem)
                    copy.start()
                    copy.wait()

        anywhere = pl.BlockSpec(memory_space=pl.ANY)
        value = values[0]
        return self(
            kernel,
            [index, *values],
            [pl.BlockSpec(memory_space=pltpu.SMEM)] + [anywhere] * len(values),
            [jax.ShapeDtypeStruct(value.shape, value.dtype)],
            [pl.BlockSpec(memory_space=pltpu.VMEM)],
            "choose",
            (0, 4 * value.size),
            scratch=[pltpu.SemaphoreType.DMA],
        )


def transpose8(x):
    at = lax.broadcasted_iota(jnp.int32, x[0].shape, 1)
    for d in (4, 2, 1):
        low = (at & d) == 0
        y = list(x)
        for i in range(8):
            if i & d == 0:
                a, b = x[i], x[i + d]
                y[i] = jnp.where(low, a, pltpu.roll(b, d, 1))
                y[i + d] = jnp.where(low, pltpu.roll(a, 8 - d, 1), b)
        x = y
    return x


def sum8(x):
    at = lax.broadcasted_iota(jnp.int32, x[0].shape, 1)
    for d in (4, 2, 1):
        low = (at & d) == 0
        y = []
        for a, b in zip(x[:d], x[d : 2 * d]):
            gone = jnp.where(low, b, a)
            back = pltpu.roll(gone, d, 1)
            if d != 4:
                back = jnp.where(low, pltpu.roll(gone, 8 - d, 1), back)
            y.append(jnp.where(low, a, b) + back)
        x = y
    return x[0]


def extract_kernel(groups, stride, spans, a_ref, sol_ref, part_ref, *rest):
    cols, wide = rest[: len(spans)], rest[-1]
    rows = part_ref.shape[1]
    if len(rest) > len(spans) + 1:
        rest[len(spans)][...] = a_ref[...]
    wide[...] = a_ref[...].astype(F32)
    i = pl.program_id(0)
    for col_ref, (start, stop) in zip(cols, spans):

        @pl.when((i >= start) & (i < stop))
        def _(col_ref=col_ref):
            for g in range(0, groups, stride):
                piece = wide[pl.ds(g, rows, stride=groups), :]
                col_ref[:, pl.ds(g // stride * LANES, LANES)] = piece.astype(BF16)

    if groups % 16 == 0:
        sol = sol_ref[...].astype(F32)
        totals = []
        for block in range(rows // 8):
            sums = []
            for r in range(8):
                base = (block * 8 + r) * groups
                sums.append(
                    sum(wide[pl.ds(base + 8 * h, 8), :] * sol[8 * h : 8 * h + 8] for h in range(groups // 8))[None]
                )
            totals.append(sum8(sums)[0])
        total = jnp.concatenate(totals, axis=0)
    else:
        total = jnp.zeros((rows, LANES), F32)
        for g in range(groups):
            total = total + wide[pl.ds(g, rows, stride=groups), :] * sol_ref[g : g + 1, :].astype(F32)
    ones = jnp.ones((8, LANES), F32)
    sums = lax.dot_general(
        ones, total, (((1,), (1,)), ((), ())), precision=lax.Precision.HIGHEST, preferred_element_type=F32
    )
    part_ref[...] = sums[0:1, :]


def extract(chain, flat, sol, sizes, first, groups, stride, width, with_band):
    sub = min(min(sizes), 256)
    size = sub * groups
    at = first // sub
    rows = sum(sizes)
    spans, out_specs, out_shape = [], [pl.BlockSpec((1, sub), lambda i: (0, i))], [jax.ShapeDtypeStruct((1, rows), F32)]
    start = 0
    for n in sizes:
        stop = start + n // sub
        spans.append((start, stop))
        out_specs.append(pl.BlockSpec((sub, width), lambda i, a=start, b=stop: (jnp.clip(i - a, 0, b - a - 1), 0)))
        out_shape.append(jax.ShapeDtypeStruct((n, width), BF16))
        start = stop
    if with_band:
        out_specs.append(pl.BlockSpec((size, LANES), lambda i: (i, 0)))
        out_shape.append(jax.ShapeDtypeStruct((rows * groups, LANES), BF16))
    return chain(
        lambda *refs: extract_kernel(groups, stride, spans, *refs),
        [flat, sol],
        [
            pl.BlockSpec((size, LANES), lambda i: (at + i, 0)),
            pl.BlockSpec((groups, LANES), lambda i: (0, 0)),
        ],
        out_shape,
        out_specs,
        "extract",
        (4 * rows * groups * LANES, rows * groups * LANES * 2),
        grid=(rows // sub,),
        scratch=[pltpu.VMEM((size, LANES), F32)],
    )


def factor_kernel(groups, n_x, where_ref, *refs):
    core, lane, x = where_ref[0], where_ref[1], where_ref[2]
    given, (blk_mine_ref, blk_other_ref, up_ref, low_ref, v_ref, raws, bands, blocks, sems, *rest) = refs[: 2 * n_x], refs[2 * n_x :]
    width = up_ref.shape[1]
    for i in range(n_x):

        @pl.when(x == i)
        def _(i=i):
            pairs = [(raws, given[2 * i], given[2 * i + 1]), (blocks, blk_mine_ref, blk_other_ref)]
            copies = []
            for kind, (target, mine, other) in enumerate(pairs):
                copies.append(pltpu.make_async_copy(mine, target.at[core], sems.at[kind, 0]))
                copies.append(pltpu.make_async_copy(other, target.at[1 - core], sems.at[kind, 1]))
            for copy in copies:
                copy.start()
            for copy in copies:
                copy.wait()

    for slot in range(2):
        if groups % 16 == 0:

            def one(block, carry, slot=slot):
                here = pl.ds(pl.multiple_of(block * 16 * groups, 16 * groups), 16 * groups)
                raw = raws[slot, here, :].astype(F32).reshape(2, 8, groups, LANES)
                rows = pl.ds(pl.multiple_of(block * 16, 16), 16)
                for h in range(groups // 8):
                    turned = transpose8([raw[:, r, 8 * h : 8 * h + 8] for r in range(8)])
                    for g in range(8):
                        at = pl.ds((8 * h + g) * LANES, LANES)
                        bands[slot, rows, at] = turned[g].reshape(16, LANES).astype(BF16)
                return carry

            lax.fori_loop(0, width // 16, one, 0, unroll=2)
        else:
            wide = rest[0]
            wide[...] = raws[slot].astype(F32)
            for g in range(groups):
                at = pl.ds(g * LANES, LANES)
                bands[slot, :, at] = wide[pl.ds(g, width, stride=groups), :].astype(BF16)
    row = lax.broadcasted_iota(jnp.int32, (width, width), 0)
    col = lax.broadcasted_iota(jnp.int32, (width, width), 1)
    zero = jnp.zeros((width, width), BF16)
    upper = [jnp.where(row <= col, up_ref[s], zero) for s in range(2)]
    lower = [jnp.where(row >= col, low_ref[s], zero) for s in range(2)]
    top_01 = matmul(lower[0], blocks[0]).astype(BF16)
    left_10 = matmul(blocks[1], upper[0]).astype(BF16)
    piece = min(groups * LANES, 1024)
    for n in range(groups * LANES // piece):
        at = slice(n * piece, (n + 1) * piece)
        top_0 = matmul(lower[0], bands[0, :, at]).astype(BF16)
        rest_1 = (bands[1, :, at].astype(F32) - matmul(left_10, top_0)).astype(BF16)
        top_1 = matmul(lower[1], rest_1).astype(BF16)
        v_1 = matmul(upper[1], top_1).astype(BF16)
        mixed = (top_0.astype(F32) - matmul(top_01, v_1)).astype(BF16)
        v_0 = matmul(upper[0], mixed).astype(BF16)
        v_ref[pl.ds(pl.multiple_of(lane * width, width), width), at] = v_0
        v_ref[pl.ds(pl.multiple_of((1 - lane) * width, width), width), at] = v_1


def factors(chain, where, bands, blocks, upper, lower, groups):
    width = upper.shape[1]
    cols = groups * LANES
    n_x = len(bands) // 2
    vmem = pl.BlockSpec(memory_space=pltpu.VMEM)
    anywhere = pl.BlockSpec(memory_space=pl.ANY)
    scratch = [
        pltpu.VMEM((2, width * groups, LANES), BF16),
        pltpu.VMEM((2, width, cols), BF16),
        pltpu.VMEM((2, width, width), BF16),
        pltpu.SemaphoreType.DMA((2, 2)),
    ]
    if groups % 16:
        scratch.append(pltpu.VMEM((width * groups, LANES), F32))
    return chain(
        lambda *refs: factor_kernel(groups, n_x, *refs),
        [where, *bands, *blocks, upper, lower],
        [pl.BlockSpec(memory_space=pltpu.SMEM)] + [anywhere] * (2 * n_x + 2) + [vmem] * 2,
        [jax.ShapeDtypeStruct((2 * width, cols), BF16)],
        [vmem],
        "factors",
        (12 * width * width * cols, 12 * width * cols),
        scratch=scratch,
    )


def update_kernel(groups, spans, a_ref, v_ref, *rest):
    out_ref, both, *wide = rest[-3 if groups % 16 else -2 :]
    rows, width = both.shape[0], both.shape[1] // 2
    i = pl.program_id(0)
    for c, (start, stop) in enumerate(spans):

        @pl.when((i >= start) & (i < stop))
        def _(c=c):
            both[:, :width] = rest[2 * c][...]
            both[:, width:] = rest[2 * c + 1][...]

    if groups % 16 == 0:
        part = min(rows, 128)
        for p in range(rows // part):
            value = matmul(both[p * part : (p + 1) * part, :], v_ref[...])
            for block in range(part // 8):
                cut = value[block * 8 : block * 8 + 8, :]
                halves = [
                    transpose8([cut[:, (8 * h + g) * LANES : (8 * h + g + 1) * LANES][None] for g in range(8)])
                    for h in range(groups // 8)
                ]
                for r in range(8):
                    here = pl.ds((p * part + block * 8 + r) * groups, groups)
                    change = jnp.concatenate([half[r][0] for half in halves], axis=0)
                    out_ref[here, :] = (a_ref[here, :].astype(F32) - change).astype(BF16)
        return
    value = matmul(both[...], v_ref[...])
    for g in range(groups):
        wide[0][pl.ds(g, rows, stride=groups), :] = value[:, g * LANES : (g + 1) * LANES]
    out_ref[...] = (a_ref[...].astype(F32) - wide[0][...]).astype(BF16)


def update(chain, flat, mine, other, v, out, first, groups):
    rows, width = sum(m.shape[0] for m in mine), mine[0].shape[1]
    sub = min(256, *(m.shape[0] for m in mine))
    size = sub * groups
    base = first // sub
    cols = groups * LANES
    in_specs = [pl.BlockSpec((size, LANES), lambda i: (base + i, 0)), pl.BlockSpec(memory_space=pltpu.VMEM)]
    args, spans, start = [flat, v], [], 0
    for m, o in zip(mine, other):
        stop = start + m.shape[0] // sub
        args += [m, o]
        in_specs += [pl.BlockSpec((sub, width), lambda i, a=start, b=stop: (jnp.clip(i - a, 0, b - a - 1), 0))] * 2
        spans.append((start, stop))
        start = stop
    aliases = {}
    if out is not None:
        aliases = {len(args): 0}
        in_specs.append(pl.BlockSpec(memory_space=pl.ANY))
        args.append(out)
    scratch = [pltpu.VMEM((sub, 2 * width), BF16)]
    if groups % 16:
        scratch.append(pltpu.VMEM((size, LANES), F32))
    return chain(
        lambda *refs: update_kernel(groups, spans, *refs),
        args,
        in_specs,
        [jax.ShapeDtypeStruct(flat.shape, BF16)],
        [pl.BlockSpec((size, LANES), lambda i: (base + i, 0))],
        "update",
        (4 * rows * width * cols, 4 * rows * cols + 4 * rows * width),
        grid=(rows // sub,),
        scratch=scratch,
        aliases=aliases,
    )


def solve_kernel(place_ref, state_ref, res_ref, inv_ref, *rest):
    cols, out_ref = rest[:-1], rest[-1]
    place, lane = place_ref[0], place_ref[1]
    width = inv_ref.shape[0]
    nt = (((1,), (1,)), ((), ()))
    pending = jnp.zeros((8, width), F32)
    for j, col in enumerate(cols):
        at = (j + lane) % 2 if j < 2 else j
        known = jnp.where(at < place, state_ref[pl.ds(at, 1), :], 0.0)
        pending = pending + lax.dot_general(
            jnp.broadcast_to(known, (8, width)).astype(BF16), col[...], nt, preferred_element_type=F32
        )
    left = res_ref[...] - pending[0:1, :]
    high = left.astype(BF16)
    rest_1 = left - high.astype(F32)
    mid = rest_1.astype(BF16)
    low = (rest_1 - mid.astype(F32)).astype(BF16)
    total = jnp.zeros((8, width), F32)
    for piece in (low, mid, high):
        wide = jnp.broadcast_to(piece.astype(F32), (8, width)).astype(BF16)
        total = total + lax.dot_general(wide, inv_ref[...], nt, preferred_element_type=F32)
    row = lax.broadcasted_iota(jnp.int32, state_ref.shape, 0)
    out_ref[...] = jnp.where(row == place, jnp.broadcast_to(total[0:1, :], state_ref.shape), state_ref[...])


def solve_step(chain, place, state, res, inv, cols):
    vmem = pl.BlockSpec(memory_space=pltpu.VMEM)
    return chain(
        solve_kernel,
        [place, state, res, inv, *cols],
        [pl.BlockSpec(memory_space=pltpu.SMEM)] + [vmem] * (3 + len(cols)),
        [jax.ShapeDtypeStruct(state.shape, F32)],
        [vmem],
        "solve",
        (2 * inv.size * (len(cols) + 3), 2 * inv.size * (len(cols) + 1)),
    )


def shards(matrix, upper_inv, lower_inv, solution, right_side, diagonal_block_inverses):
    slots, _, width, col_slots, _, _ = matrix.shape
    n_prow = lax.axis_size("prow")
    n_pcol = lax.axis_size("pcol")
    ny = n_prow // 2
    nz = n_pcol // ny
    prow = lax.axis_index("prow")
    pcol = lax.axis_index("pcol")
    z, y = pcol // ny, pcol % ny
    core, lane = prow % 2, y % 2
    lane_tiles = width // LANES
    groups = lane_tiles * col_slots
    rows = slots * width
    flat = matrix.reshape(rows, col_slots, lane_tiles, LANES).transpose(0, 2, 1, 3).reshape(rows * groups, LANES)
    sol = solution.reshape(col_slots, lane_tiles, LANES).transpose(1, 0, 2).reshape(groups, LANES)

    chain = Chain()

    def spread(value, axis, size):
        values = [value]
        for s in range(2, size, 2):
            pairs = [(s - 2, s), (s - 1, s + 1), (s, s - 2), (s + 1, s - 1)]
            values.append(lax.ppermute(values[-1], axis, pairs))
        return values

    def swap(value, axis, size, bit=1):
        return lax.ppermute(value, axis, [(i, i ^ bit) for i in range(size)])

    def along_z(pairs):
        return [(a * ny + k, b * ny + k) for a, b in pairs for k in range(2)]

    stages = [[[(0, nz // 2)]]]
    held, step = [nz // 2], nz // 4
    while step:
        stages.append([[(m, m - step) for m in held], [(m, m + step) for m in held]])
        held = [b for moves in stages[-1] for _, b in moves]
        step //= 2

    def picked(got, moves, value):
        mask = z == moves[0][1]
        for _, b in moves[1:]:
            mask = mask | (z == b)
        return jnp.where(mask, got, value)

    def first_stage(local):
        return lax.ppermute(local, "pcol", along_z(stages[0][0]))

    def second_stage(arrived):
        return [lax.ppermute(arrived, "pcol", along_z(moves)) for moves in stages[1]]

    source = jnp.zeros((), jnp.int32)
    for i, moves in enumerate(stages[0] + stages[1]):
        for _, b in moves:
            source = jnp.where(z == b, i + 1, source)
    source = source.astype(jnp.int32).reshape(1)

    def settle(local, arrived, outward):
        value = chain.choose(source, [local, arrived, *outward])
        for stage in stages[2:]:
            gots = [lax.ppermute(value, "pcol", along_z(moves)) for moves in stage]
            for got, moves in zip(gots, stage):
                value = picked(got, moves, value)
        for s in range(2, ny, 2):
            pairs = [(a * ny + s - 2 + k, a * ny + s + k) for a in range(nz) for k in range(2)]
            got = lax.ppermute(value, "pcol", pairs)
            value = jnp.where(y // 2 == s // 2, got, value)
        return value

    count = n_prow * diagonal_block_inverses.shape[0]
    assert diagonal_block_inverses.shape[0] == 1
    home = count - 2
    inv = diagonal_block_inverses.reshape(width, width)
    place = jnp.stack([prow, lane]).astype(jnp.int32)
    where = jnp.stack([core, lane, prow // 2]).astype(jnp.int32)
    flag = jnp.where(core != lane, 0, 1).astype(jnp.int32).reshape(1)
    bits = [1 << b for b in range(n_pcol.bit_length() - 1)]
    order = bits[1:] + bits[:1]

    sizes = [width] + [2 * width] * ((slots - 2) // 2)
    sizes += [width] * (slots - sum(sizes) // width)
    starts = [sum(sizes[:c]) for c in range(len(sizes) + 1)]
    chunks = len(sizes)
    column, first, outward, mine, other, box = {}, {}, {}, {}, {}, {"out": None}

    def extracts(a, b, with_band=False):
        part, *cols = extract(chain, flat, sol, sizes[a:b], starts[a], groups, col_slots, width, with_band)
        column.update(zip(range(a, b), cols))
        return part, cols[-1]

    parts = []
    part, band = extracts(0, 1, True)
    parts.append(part)
    first[0] = first_stage(column[0])
    bands = spread(band, "prow", n_prow)
    swaps = {0: swap(band, "prow", n_prow)}
    parts.append(extracts(1, 2)[0])

    def total_step(bit):
        def run():
            if bit == order[0]:
                box["total"] = jnp.concatenate(parts, axis=1).reshape(slots, width)
            box["total"] = chain.add(box["total"], swap(box["total"], "pcol", n_pcol, bit))
            if bit == order[-1]:
                box["residual"] = right_side.reshape(slots, width) - box["total"]

        return run

    def solve(k):
        def run():
            if k == 0:
                needed = [mine[0], other[0]]
                for j in range(2, home):
                    needed.append(lax.ppermute(column[0], "pcol", [(j, home)]))
                box["needed"] = needed + [column[0]]
                state = jnp.zeros((count, width), F32)
            else:
                state = lax.ppermute(box["state"], "prow", [(i, i + 1) for i in range(n_prow - 1)])
            state = solve_step(chain, place, state, box["residual"][0:1], inv, box["needed"])
            if k == count - 1:
                state = jnp.where((prow == n_prow - 1) & (pcol == home), state, 0.0)
            box["state"] = state

        return run

    def share(axis, size, bit):
        def run():
            box["state"] = chain.add(box["state"], swap(box["state"], axis, size, bit))

        return run

    def arrive(values):
        got = chain.gate(list(values), [])
        return got if len(values) > 1 else [got]

    def blocks_out():
        box["pick"] = spread(chain.choose(flag, [mine[0], other[0]]), "prow", n_prow)
        bands[1:] = arrive(bands[1:])
        for i, value in enumerate(bands[1:]):
            swaps[i + 1] = swap(value, "prow", n_prow)

    def bands_in():
        for i, value in zip(range(1, len(bands)), arrive([swaps[i] for i in range(1, len(bands))])):
            swaps[i] = value
        box["bands"] = [v for i, b in enumerate(bands) for v in (b, swaps[i])]

    def blocks_swap():
        blk = chain.choose(where[2:3], box["pick"])
        box["blks"] = [blk, swap(blk, "prow", n_prow)]

    def blocks_in():
        box["blks"][1:] = arrive(box["blks"][1:])

    def make_factors():
        box["v"] = factors(chain, where, box["bands"], box["blks"], upper_inv, lower_inv, groups)

    def updates(*which):
        def run():
            args = [mine[c] for c in which], [other[c] for c in which]
            box["out"] = update(chain, flat, *args, box["v"], box["out"], starts[which[0]], groups)

        return run

    def take(c):
        mine[c] = settle(column[c], first[c], outward[c])
        other[c] = swap(mine[c], "pcol", n_pcol)

    total = [total_step(b) for b in order]
    line = [solve(k) for k in range(count)]
    line += [share("prow", n_prow, 1 << b) for b in range(n_prow.bit_length() - 1)]
    line += [share("pcol", n_pcol, b) for b in bits]
    def extracted(a, b):
        if a < b:
            parts.append(extracts(a, b)[0])

    def advance(k):
        ahead = [column[k + 1]] if k + 1 < chunks else []
        extra = [swaps[0]] if k == 0 else []
        got = chain.gate([first[k], *ahead, *extra], [])
        got = got if ahead or extra else [got]
        first[k] = got[0]
        if ahead:
            column[k + 1] = got[1]
            first[k + 1] = first_stage(column[k + 1])
        if extra:
            swaps[0] = got[-1]
        outward[k] = second_stage(first[k])

    def each(tasks):
        for task in tasks:
            task()

    advance(0)
    extracted(2, min(3, chunks))
    take(0)
    extracted(3, chunks)
    if chunks == 5 and len(line) == 9:
        each(total[:2])
        advance(1)
        each([blocks_out, total[2], bands_in, line[0], blocks_swap, blocks_in, make_factors])
        advance(2)
        take(1)
        each([updates(0), *line[1:4]])
        other[1] = arrive([other[1]])[0]
        advance(3)
        take(2)
        updates(1)()
        advance(4)
        each(line[4:7])
        take(3)
        each([line[7], updates(2), line[8]])
        take(4)
        each([updates(3), updates(4)])
    else:
        each([*total, blocks_out, bands_in, blocks_swap, blocks_in, make_factors, *line])
        for k in range(1, chunks):
            advance(k)
            take(k)
        updates(*range(chunks))()
    residual, out, state = box["residual"], box["out"], box["state"]
    updated = out.reshape(rows, lane_tiles, col_slots, LANES).transpose(0, 2, 1, 3).reshape(matrix.shape)
    return (updated, residual.reshape(right_side.shape), state)


def solution(mesh):
    return jax.shard_map(
        shards,
        mesh=mesh,
        in_specs=(
            P(None, "prow", None, None, "pcol", None),
            P(),
            P(),
            P(None, "pcol", None),
            P(None, "prow", None),
            P(None, "prow", None, None),
        ),
        out_specs=(P(None, "prow", None, None, "pcol", None), P(None, "prow", None), P()),
        check_vma=False,
    )
```

```python
import jax
import jax.numpy as jnp
from jax import lax
from jax.experimental import pallas as pl
from jax.experimental.pallas import tpu as pltpu
from jax.sharding import PartitionSpec as P

LANES = 128
VMEM_BYTES = 50 * 1024 * 1024
F32 = jnp.float32
BF16 = jnp.bfloat16


def matmul(a, b):
    return jnp.dot(a, b, preferred_element_type=F32)


class Chain:
    def __init__(self):
        self.token = None

    def __call__(self, kernel, inputs, in_specs, out_shape, out_specs, name, work, after=(), grid=None, scratch=(), aliases=None):
        deps = list(after) + ([] if self.token is None else [self.token])
        n_in, n_out, n_dep = len(inputs), len(out_shape), len(deps)
        anywhere = pl.BlockSpec(memory_space=pl.ANY)

        def body(*refs):
            outs = n_in + n_dep
            kernel(*refs[:n_in], *refs[outs : outs + n_out], *refs[outs + n_out + 1 :])

        params = {} if grid is None else {"grid": grid}
        *results, self.token = pl.pallas_call(
            body,
            in_specs=list(in_specs) + [anywhere] * n_dep,
            out_specs=list(out_specs) + [anywhere],
            out_shape=list(out_shape) + [jax.ShapeDtypeStruct((8, LANES), F32)],
            scratch_shapes=list(scratch),
            input_output_aliases=aliases or {},
            compiler_params=pltpu.CompilerParams(vmem_limit_bytes=VMEM_BYTES),
            cost_estimate=pl.CostEstimate(flops=0, bytes_accessed=0, transcendentals=0),
            name=name,
            **params,
        )(*inputs, *deps)
        return results[0] if len(results) == 1 else results

    def gate(self, values, after):
        anywhere = pl.BlockSpec(memory_space=pl.ANY)
        return self(
            lambda *refs: None,
            values,
            [anywhere] * len(values),
            [jax.ShapeDtypeStruct(v.shape, v.dtype) for v in values],
            [anywhere] * len(values),
            "gate",
            (0, 0),
            after=after,
            aliases={i: i for i in range(len(values))},
        )

    def add(self, a, b):
        def kernel(a_ref, b_ref, out_ref):
            out_ref[...] = a_ref[...] + b_ref[...]

        vmem = pl.BlockSpec(memory_space=pltpu.VMEM)
        return self(kernel, [a, b], [vmem] * 2, [jax.ShapeDtypeStruct(a.shape, a.dtype)], [vmem], "add", (a.size, 12 * a.size))

    def choose(self, index, values):
        def kernel(index_ref, *refs):
            *sources, out, sem = refs
            for i, ref in enumerate(sources):

                @pl.when(index_ref[0] == i)
                def _(ref=ref):
                    copy = pltpu.make_async_copy(ref, out, sem)
                    copy.start()
                    copy.wait()

        anywhere = pl.BlockSpec(memory_space=pl.ANY)
        value = values[0]
        return self(
            kernel,
            [index, *values],
            [pl.BlockSpec(memory_space=pltpu.SMEM)] + [anywhere] * len(values),
            [jax.ShapeDtypeStruct(value.shape, value.dtype)],
            [pl.BlockSpec(memory_space=pltpu.VMEM)],
            "choose",
            (0, 4 * value.size),
            scratch=[pltpu.SemaphoreType.DMA],
        )


def transpose8(x):
    at = lax.broadcasted_iota(jnp.int32, x[0].shape, 1)
    for d in (4, 2, 1):
        low = (at & d) == 0
        y = list(x)
        for i in range(8):
            if i & d == 0:
                a, b = x[i], x[i + d]
                y[i] = jnp.where(low, a, pltpu.roll(b, d, 1))
                y[i + d] = jnp.where(low, pltpu.roll(a, 8 - d, 1), b)
        x = y
    return x


def sum8(x):
    at = lax.broadcasted_iota(jnp.int32, x[0].shape, 1)
    for d in (4, 2, 1):
        low = (at & d) == 0
        y = []
        for a, b in zip(x[:d], x[d : 2 * d]):
            gone = jnp.where(low, b, a)
            back = pltpu.roll(gone, d, 1)
            if d != 4:
                back = jnp.where(low, pltpu.roll(gone, 8 - d, 1), back)
            y.append(jnp.where(low, a, b) + back)
        x = y
    return x[0]


def extract_kernel(groups, stride, spans, a_ref, sol_ref, part_ref, *rest):
    cols, wide = rest[: len(spans)], rest[-1]
    rows = part_ref.shape[1]
    if len(rest) > len(spans) + 1:
        rest[len(spans)][...] = a_ref[...]
    wide[...] = a_ref[...].astype(F32)
    i = pl.program_id(0)
    for col_ref, (start, stop) in zip(cols, spans):

        @pl.when((i >= start) & (i < stop))
        def _(col_ref=col_ref):
            for g in range(0, groups, stride):
                piece = wide[pl.ds(g, rows, stride=groups), :]
                col_ref[:, pl.ds(g // stride * LANES, LANES)] = piece.astype(BF16)

    if groups % 16 == 0:
        sol = sol_ref[...].astype(F32)
        totals = []
        for block in range(rows // 8):
            sums = []
            for r in range(8):
                base = (block * 8 + r) * groups
                sums.append(
                    sum(wide[pl.ds(base + 8 * h, 8), :] * sol[8 * h : 8 * h + 8] for h in range(groups // 8))[None]
                )
            totals.append(sum8(sums)[0])
        total = jnp.concatenate(totals, axis=0)
    else:
        total = jnp.zeros((rows, LANES), F32)
        for g in range(groups):
            total = total + wide[pl.ds(g, rows, stride=groups), :] * sol_ref[g : g + 1, :].astype(F32)
    ones = jnp.ones((8, LANES), F32)
    sums = lax.dot_general(
        ones, total, (((1,), (1,)), ((), ())), precision=lax.Precision.HIGHEST, preferred_element_type=F32
    )
    part_ref[...] = sums[0:1, :]


def extract(chain, flat, sol, sizes, first, groups, stride, width, with_band):
    sub = min(min(sizes), 256)
    size = sub * groups
    at = first // sub
    rows = sum(sizes)
    spans, out_specs, out_shape = [], [pl.BlockSpec((1, sub), lambda i: (0, i))], [jax.ShapeDtypeStruct((1, rows), F32)]
    start = 0
    for n in sizes:
        stop = start + n // sub
        spans.append((start, stop))
        out_specs.append(pl.BlockSpec((sub, width), lambda i, a=start, b=stop: (jnp.clip(i - a, 0, b - a - 1), 0)))
        out_shape.append(jax.ShapeDtypeStruct((n, width), BF16))
        start = stop
    if with_band:
        out_specs.append(pl.BlockSpec((size, LANES), lambda i: (i, 0)))
        out_shape.append(jax.ShapeDtypeStruct((rows * groups, LANES), BF16))
    return chain(
        lambda *refs: extract_kernel(groups, stride, spans, *refs),
        [flat, sol],
        [
            pl.BlockSpec((size, LANES), lambda i: (at + i, 0)),
            pl.BlockSpec((groups, LANES), lambda i: (0, 0)),
        ],
        out_shape,
        out_specs,
        "extract",
        (4 * rows * groups * LANES, rows * groups * LANES * 2),
        grid=(rows // sub,),
        scratch=[pltpu.VMEM((size, LANES), F32)],
    )


def factor_kernel(groups, n_x, where_ref, *refs):
    core, lane, x = where_ref[0], where_ref[1], where_ref[2]
    given, (blk_mine_ref, blk_other_ref, up_ref, low_ref, v_ref, raws, bands, blocks, sems, *rest) = refs[: 2 * n_x], refs[2 * n_x :]
    width = up_ref.shape[1]
    for i in range(n_x):

        @pl.when(x == i)
        def _(i=i):
            pairs = [(raws, given[2 * i], given[2 * i + 1]), (blocks, blk_mine_ref, blk_other_ref)]
            copies = []
            for kind, (target, mine, other) in enumerate(pairs):
                copies.append(pltpu.make_async_copy(mine, target.at[core], sems.at[kind, 0]))
                copies.append(pltpu.make_async_copy(other, target.at[1 - core], sems.at[kind, 1]))
            for copy in copies:
                copy.start()
            for copy in copies:
                copy.wait()

    for slot in range(2):
        if groups % 16 == 0:

            def one(block, carry, slot=slot):
                here = pl.ds(pl.multiple_of(block * 16 * groups, 16 * groups), 16 * groups)
                raw = raws[slot, here, :].astype(F32).reshape(2, 8, groups, LANES)
                rows = pl.ds(pl.multiple_of(block * 16, 16), 16)
                for h in range(groups // 8):
                    turned = transpose8([raw[:, r, 8 * h : 8 * h + 8] for r in range(8)])
                    for g in range(8):
                        at = pl.ds((8 * h + g) * LANES, LANES)
                        bands[slot, rows, at] = turned[g].reshape(16, LANES).astype(BF16)
                return carry

            lax.fori_loop(0, width // 16, one, 0, unroll=2)
        else:
            wide = rest[0]
            wide[...] = raws[slot].astype(F32)
            for g in range(groups):
                at = pl.ds(g * LANES, LANES)
                bands[slot, :, at] = wide[pl.ds(g, width, stride=groups), :].astype(BF16)
    row = lax.broadcasted_iota(jnp.int32, (width, width), 0)
    col = lax.broadcasted_iota(jnp.int32, (width, width), 1)
    zero = jnp.zeros((width, width), BF16)
    upper = [jnp.where(row <= col, up_ref[s], zero) for s in range(2)]
    lower = [jnp.where(row >= col, low_ref[s], zero) for s in range(2)]
    top_01 = matmul(lower[0], blocks[0]).astype(BF16)
    left_10 = matmul(blocks[1], upper[0]).astype(BF16)
    piece = min(groups * LANES, 1024)
    for n in range(groups * LANES // piece):
        at = slice(n * piece, (n + 1) * piece)
        top_0 = matmul(lower[0], bands[0, :, at]).astype(BF16)
        rest_1 = (bands[1, :, at].astype(F32) - matmul(left_10, top_0)).astype(BF16)
        top_1 = matmul(lower[1], rest_1).astype(BF16)
        v_1 = matmul(upper[1], top_1).astype(BF16)
        mixed = (top_0.astype(F32) - matmul(top_01, v_1)).astype(BF16)
        v_0 = matmul(upper[0], mixed).astype(BF16)
        v_ref[pl.ds(pl.multiple_of(lane * width, width), width), at] = v_0
        v_ref[pl.ds(pl.multiple_of((1 - lane) * width, width), width), at] = v_1


def factors(chain, where, bands, blocks, upper, lower, groups):
    width = upper.shape[1]
    cols = groups * LANES
    n_x = len(bands) // 2
    vmem = pl.BlockSpec(memory_space=pltpu.VMEM)
    anywhere = pl.BlockSpec(memory_space=pl.ANY)
    scratch = [
        pltpu.VMEM((2, width * groups, LANES), BF16),
        pltpu.VMEM((2, width, cols), BF16),
        pltpu.VMEM((2, width, width), BF16),
        pltpu.SemaphoreType.DMA((2, 2)),
    ]
    if groups % 16:
        scratch.append(pltpu.VMEM((width * groups, LANES), F32))
    return chain(
        lambda *refs: factor_kernel(groups, n_x, *refs),
        [where, *bands, *blocks, upper, lower],
        [pl.BlockSpec(memory_space=pltpu.SMEM)] + [anywhere] * (2 * n_x + 2) + [vmem] * 2,
        [jax.ShapeDtypeStruct((2 * width, cols), BF16)],
        [vmem],
        "factors",
        (12 * width * width * cols, 12 * width * cols),
        scratch=scratch,
    )


def update_kernel(groups, spans, a_ref, v_ref, *rest):
    out_ref, both, *wide = rest[-3 if groups % 16 else -2 :]
    rows, width = both.shape[0], both.shape[1] // 2
    i = pl.program_id(0)
    for c, (start, stop) in enumerate(spans):

        @pl.when((i >= start) & (i < stop))
        def _(c=c):
            both[:, :width] = rest[2 * c][...]
            both[:, width:] = rest[2 * c + 1][...]

    if groups % 16 == 0:
        part = min(rows, 128)
        for p in range(rows // part):
            value = matmul(both[p * part : (p + 1) * part, :], v_ref[...])
            for block in range(part // 8):
                cut = value[block * 8 : block * 8 + 8, :]
                halves = [
                    transpose8([cut[:, (8 * h + g) * LANES : (8 * h + g + 1) * LANES][None] for g in range(8)])
                    for h in range(groups // 8)
                ]
                for r in range(8):
                    here = pl.ds((p * part + block * 8 + r) * groups, groups)
                    change = jnp.concatenate([half[r][0] for half in halves], axis=0)
                    out_ref[here, :] = (a_ref[here, :].astype(F32) - change).astype(BF16)
        return
    value = matmul(both[...], v_ref[...])
    for g in range(groups):
        wide[0][pl.ds(g, rows, stride=groups), :] = value[:, g * LANES : (g + 1) * LANES]
    out_ref[...] = (a_ref[...].astype(F32) - wide[0][...]).astype(BF16)


def update(chain, flat, mine, other, v, out, first, groups):
    rows, width = sum(m.shape[0] for m in mine), mine[0].shape[1]
    sub = min(256, *(m.shape[0] for m in mine))
    size = sub * groups
    base = first // sub
    cols = groups * LANES
    in_specs = [pl.BlockSpec((size, LANES), lambda i: (base + i, 0)), pl.BlockSpec(memory_space=pltpu.VMEM)]
    args, spans, start = [flat, v], [], 0
    for m, o in zip(mine, other):
        stop = start + m.shape[0] // sub
        args += [m, o]
        in_specs += [pl.BlockSpec((sub, width), lambda i, a=start, b=stop: (jnp.clip(i - a, 0, b - a - 1), 0))] * 2
        spans.append((start, stop))
        start = stop
    aliases = {}
    if out is not None:
        aliases = {len(args): 0}
        in_specs.append(pl.BlockSpec(memory_space=pl.ANY))
        args.append(out)
    scratch = [pltpu.VMEM((sub, 2 * width), BF16)]
    if groups % 16:
        scratch.append(pltpu.VMEM((size, LANES), F32))
    return chain(
        lambda *refs: update_kernel(groups, spans, *refs),
        args,
        in_specs,
        [jax.ShapeDtypeStruct(flat.shape, BF16)],
        [pl.BlockSpec((size, LANES), lambda i: (base + i, 0))],
        "update",
        (4 * rows * width * cols, 4 * rows * cols + 4 * rows * width),
        grid=(rows // sub,),
        scratch=scratch,
        aliases=aliases,
    )


def solve_kernel(place_ref, state_ref, res_ref, inv_ref, *rest):
    cols, out_ref = rest[:-1], rest[-1]
    place, lane = place_ref[0], place_ref[1]
    width = inv_ref.shape[0]
    nt = (((1,), (1,)), ((), ()))
    pending = jnp.zeros((8, width), F32)
    for j, col in enumerate(cols):
        at = (j + lane) % 2 if j < 2 else j
        known = jnp.where(at < place, state_ref[pl.ds(at, 1), :], 0.0)
        pending = pending + lax.dot_general(
            jnp.broadcast_to(known, (8, width)).astype(BF16), col[...], nt, preferred_element_type=F32
        )
    left = res_ref[...] - pending[0:1, :]
    high = left.astype(BF16)
    rest_1 = left - high.astype(F32)
    mid = rest_1.astype(BF16)
    low = (rest_1 - mid.astype(F32)).astype(BF16)
    total = jnp.zeros((8, width), F32)
    for piece in (low, mid, high):
        wide = jnp.broadcast_to(piece.astype(F32), (8, width)).astype(BF16)
        total = total + lax.dot_general(wide, inv_ref[...], nt, preferred_element_type=F32)
    row = lax.broadcasted_iota(jnp.int32, state_ref.shape, 0)
    out_ref[...] = jnp.where(row == place, jnp.broadcast_to(total[0:1, :], state_ref.shape), state_ref[...])


def solve_step(chain, place, state, res, inv, cols):
    vmem = pl.BlockSpec(memory_space=pltpu.VMEM)
    return chain(
        solve_kernel,
        [place, state, res, inv, *cols],
        [pl.BlockSpec(memory_space=pltpu.SMEM)] + [vmem] * (3 + len(cols)),
        [jax.ShapeDtypeStruct(state.shape, F32)],
        [vmem],
        "solve",
        (2 * inv.size * (len(cols) + 3), 2 * inv.size * (len(cols) + 1)),
    )


def shards(matrix, upper_inv, lower_inv, solution, right_side, diagonal_block_inverses):
    slots, _, width, col_slots, _, _ = matrix.shape
    n_prow = lax.axis_size("prow")
    n_pcol = lax.axis_size("pcol")
    ny = n_prow // 2
    nz = n_pcol // ny
    prow = lax.axis_index("prow")
    pcol = lax.axis_index("pcol")
    z, y = pcol // ny, pcol % ny
    core, lane = prow % 2, y % 2
    lane_tiles = width // LANES
    groups = lane_tiles * col_slots
    rows = slots * width
    flat = matrix.reshape(rows, col_slots, lane_tiles, LANES).transpose(0, 2, 1, 3).reshape(rows * groups, LANES)
    sol = solution.reshape(col_slots, lane_tiles, LANES).transpose(1, 0, 2).reshape(groups, LANES)

    chain = Chain()

    def spread(value, axis, size):
        values = [value]
        for s in range(2, size, 2):
            pairs = [(s - 2, s), (s - 1, s + 1), (s, s - 2), (s + 1, s - 1)]
            values.append(lax.ppermute(values[-1], axis, pairs))
        return values

    def swap(value, axis, size, bit=1):
        return lax.ppermute(value, axis, [(i, i ^ bit) for i in range(size)])

    def along_z(pairs):
        return [(a * ny + k, b * ny + k) for a, b in pairs for k in range(2)]

    stages = [[[(0, nz // 2)]]]
    held, step = [nz // 2], nz // 4
    while step:
        stages.append([[(m, m - step) for m in held], [(m, m + step) for m in held]])
        held = [b for moves in stages[-1] for _, b in moves]
        step //= 2

    def picked(got, moves, value):
        mask = z == moves[0][1]
        for _, b in moves[1:]:
            mask = mask | (z == b)
        return jnp.where(mask, got, value)

    def first_stage(local):
        return lax.ppermute(local, "pcol", along_z(stages[0][0]))

    def second_stage(arrived):
        return [lax.ppermute(arrived, "pcol", along_z(moves)) for moves in stages[1]]

    source = jnp.zeros((), jnp.int32)
    for i, moves in enumerate(stages[0] + stages[1]):
        for _, b in moves:
            source = jnp.where(z == b, i + 1, source)
    source = source.astype(jnp.int32).reshape(1)

    def settle(local, arrived, outward):
        value = chain.choose(source, [local, arrived, *outward])
        for stage in stages[2:]:
            gots = [lax.ppermute(value, "pcol", along_z(moves)) for moves in stage]
            for got, moves in zip(gots, stage):
                value = picked(got, moves, value)
        for s in range(2, ny, 2):
            pairs = [(a * ny + s - 2 + k, a * ny + s + k) for a in range(nz) for k in range(2)]
            got = lax.ppermute(value, "pcol", pairs)
            value = jnp.where(y // 2 == s // 2, got, value)
        return value

    count = n_prow * diagonal_block_inverses.shape[0]
    assert diagonal_block_inverses.shape[0] == 1
    home = count - 2
    inv = diagonal_block_inverses.reshape(width, width)
    place = jnp.stack([prow, lane]).astype(jnp.int32)
    where = jnp.stack([core, lane, prow // 2]).astype(jnp.int32)
    flag = jnp.where(core != lane, 0, 1).astype(jnp.int32).reshape(1)
    bits = [1 << b for b in range(n_pcol.bit_length() - 1)]
    order = bits[1:] + bits[:1]

    sizes = [width] + [2 * width] * ((slots - 2) // 2)
    sizes += [width] * (slots - sum(sizes) // width)
    starts = [sum(sizes[:c]) for c in range(len(sizes) + 1)]
    chunks = len(sizes)
    column, first, outward, mine, other, box = {}, {}, {}, {}, {}, {"out": None}

    def extracts(a, b, with_band=False):
        part, *cols = extract(chain, flat, sol, sizes[a:b], starts[a], groups, col_slots, width, with_band)
        column.update(zip(range(a, b), cols))
        return part, cols[-1]

    parts = []
    part, band = extracts(0, 1, True)
    parts.append(part)
    first[0] = first_stage(column[0])
    bands = spread(band, "prow", n_prow)
    swaps = {0: swap(band, "prow", n_prow)}
    parts.append(extracts(1, 2)[0])

    def total_step(bit):
        def run():
            if bit == order[0]:
                box["total"] = jnp.concatenate(parts, axis=1).reshape(slots, width)
            box["total"] = chain.add(box["total"], swap(box["total"], "pcol", n_pcol, bit))
            if bit == order[-1]:
                box["residual"] = right_side.reshape(slots, width) - box["total"]

        return run

    def solve(k):
        def run():
            if k == 0:
                needed = [mine[0], other[0]]
                for j in range(2, home):
                    needed.append(lax.ppermute(column[0], "pcol", [(j, home)]))
                box["needed"] = needed + [column[0]]
                state = jnp.zeros((count, width), F32)
            else:
                state = lax.ppermute(box["state"], "prow", [(i, i + 1) for i in range(n_prow - 1)])
            state = solve_step(chain, place, state, box["residual"][0:1], inv, box["needed"])
            if k == count - 1:
                state = jnp.where((prow == n_prow - 1) & (pcol == home), state, 0.0)
            box["state"] = state

        return run

    def share(axis, size, bit):
        def run():
            box["state"] = chain.add(box["state"], swap(box["state"], axis, size, bit))

        return run

    def arrive(values):
        got = chain.gate(list(values), [])
        return got if len(values) > 1 else [got]

    def blocks_out():
        box["pick"] = spread(chain.choose(flag, [mine[0], other[0]]), "prow", n_prow)
        bands[1:] = arrive(bands[1:])
        for i, value in enumerate(bands[1:]):
            swaps[i + 1] = swap(value, "prow", n_prow)

    def bands_in():
        for i, value in zip(range(1, len(bands)), arrive([swaps[i] for i in range(1, len(bands))])):
            swaps[i] = value
        box["bands"] = [v for i, b in enumerate(bands) for v in (b, swaps[i])]

    def blocks_swap():
        blk = chain.choose(where[2:3], box["pick"])
        box["blks"] = [blk, swap(blk, "prow", n_prow)]

    def blocks_in():
        box["blks"][1:] = arrive(box["blks"][1:])

    def make_factors():
        box["v"] = factors(chain, where, box["bands"], box["blks"], upper_inv, lower_inv, groups)

    def updates(*which):
        def run():
            args = [mine[c] for c in which], [other[c] for c in which]
            box["out"] = update(chain, flat, *args, box["v"], box["out"], starts[which[0]], groups)

        return run

    def take(c):
        mine[c] = settle(column[c], first[c], outward[c])
        other[c] = swap(mine[c], "pcol", n_pcol)

    total = [total_step(b) for b in order]
    line = [solve(k) for k in range(count)]
    line += [share("prow", n_prow, 1 << b) for b in range(n_prow.bit_length() - 1)]
    line += [share("pcol", n_pcol, b) for b in bits]
    def extracted(a, b):
        if a < b:
            parts.append(extracts(a, b)[0])

    def advance(k):
        ahead = [column[k + 1]] if k + 1 < chunks else []
        extra = [swaps[0]] if k == 0 else []
        got = chain.gate([first[k], *ahead, *extra], [])
        got = got if ahead or extra else [got]
        first[k] = got[0]
        if ahead:
            column[k + 1] = got[1]
            first[k + 1] = first_stage(column[k + 1])
        if extra:
            swaps[0] = got[-1]
        outward[k] = second_stage(first[k])

    def each(tasks):
        for task in tasks:
            task()

    advance(0)
    extracted(2, min(3, chunks))
    take(0)
    extracted(3, chunks)
    if chunks == 5 and len(line) == 9:
        each(total[:2])
        advance(1)
        each([blocks_out, total[2], bands_in, line[0], blocks_swap, blocks_in, make_factors])
        advance(2)
        take(1)
        each([updates(0), *line[1:4]])
        other[1] = arrive([other[1]])[0]
        advance(3)
        take(2)
        updates(1)()
        advance(4)
        each(line[4:7])
        take(3)
        updates(2)()
        take(4)
        each([line[7], line[8], updates(3), updates(4)])
    else:
        each([*total, blocks_out, bands_in, blocks_swap, blocks_in, make_factors, *line])
        for k in range(1, chunks):
            advance(k)
            take(k)
        updates(*range(chunks))()
    residual, out, state = box["residual"], box["out"], box["state"]
    updated = out.reshape(rows, lane_tiles, col_slots, LANES).transpose(0, 2, 1, 3).reshape(matrix.shape)
    return (updated, residual.reshape(right_side.shape), state)


def solution(mesh):
    return jax.shard_map(
        shards,
        mesh=mesh,
        in_specs=(
            P(None, "prow", None, None, "pcol", None),
            P(),
            P(),
            P(None, "pcol", None),
            P(None, "prow", None),
            P(None, "prow", None, None),
        ),
        out_specs=(P(None, "prow", None, None, "pcol", None), P(None, "prow", None), P()),
        check_vma=False,
    )
```
